128 devices in a mesh: inst: 16 (over z, y_hi, core), tp: 8 (over x, y_lo).
Axes of the slice: x: 4, y: 4 (y_hi: 2, y_lo: 2; y = y_hi * 2 + y_lo), z: 4, core: 2. Of those that a mesh axis runs over, the one named last changes fastest.
Arguments:
- queries: bfloat16 [4, 64, 8192], P(None, 'inst', 'tp'), may hold values from -240 to 240
- new_kv: bfloat16 [4, 64, 8, 256], P(None, 'inst', 'tp'), may hold values from -6 to 6
- kv_pool: bfloat16 [1536, 128, 8, 256], P('inst', None, 'tp'), may hold values from -6 to 6
- out_weight: bfloat16 [8192, 8192], P('tp'), may hold values from -0.0625 to 0.0625
- send_block: int32 [256], P('inst'), may hold values from 0 to 95, as said below
- send_dest: int32 [256], P('inst'), may hold values from 0 to 15, as said below
- block_table: int32 [64, 16], P('inst'), may hold values from 0 to 127, as said below
- cache_len: int32 [64], P('inst'), may hold values from 1 to 2048, as said below
Outputs:
- projected: bfloat16 [4, 64, 8192], P(None, 'inst', 'tp')
The draws below stay inside these ranges and needn't reach their ends.
Inputs may be any that keep to these rules, and one draw needn't show every extreme that they name: `send_dest`: no entry of one instance's list names an instance more than 2 times; one instance is named exactly 2 times in every instance's list. `send_block`: the blocks of one instance's list are distinct. `block_table`: ids below 96 are own blocks that the instance did not send; an id 96 + s * 2 + r names only a block that instance s really sends to it; ids of one instance are distinct, and every arrived block is named. `cache_len`: on every instance one request holds 2048 tokens.
All inputs are finite; a program needn't handle non-finite values.
Results may differ from the reference program's by a relative error of at most 0.0049.
Values may be sent and summed in bfloat16 or wider, within the bound.
No kernel may reach another device: no remote copies, remote signals or barrier semaphores. Data moves between devices by JAX's collectives and lax.ppermute only.
A program may use at most 128 MiB of HBM per device.

```python
import jax
import jax.numpy as jnp
from jax import lax

D = 8192
H = 64
KVH = 8
HD = 128
BLOCK = 128
STEPS = 4
CAP = 2
MIGB = 16
SLOTS = 4
BLK_REQ = 16
R = 64
POOL = 96
N_INST = 16


def migration_plan(key):
    hot_target = jax.random.randint(jax.random.fold_in(key, 11), (), 0, N_INST).astype(jnp.int32)
    other_targets = (hot_target + 1 + jnp.arange((N_INST - 1) * CAP, dtype=jnp.int32) // CAP) % N_INST

    def source_lists(source_index):
        source_key = jax.random.fold_in(jax.random.fold_in(key, 13), source_index)
        first_key, second_key, third_key = jax.random.split(source_key, 3)
        chosen = jax.random.permutation(first_key, other_targets)[:MIGB - CAP]
        dest_list = jnp.concatenate([jnp.full((CAP,), hot_target, jnp.int32), chosen.astype(jnp.int32)])
        dest_list = jax.random.permutation(second_key, dest_list)
        block_list = jax.random.permutation(third_key, POOL)[:MIGB]
        return (dest_list.astype(jnp.int32), block_list.astype(jnp.int32))
    dest_lists, block_lists = jax.vmap(source_lists)(jnp.arange(N_INST, dtype=jnp.int32))
    id_count = POOL + N_INST * CAP

    def instance_table(inst_index, own_blocks):
        table_key = jax.random.fold_in(jax.random.fold_in(key, 17), inst_index)
        first_key, second_key = jax.random.split(table_key, 2)
        counts = jnp.sum((dest_lists == inst_index).astype(jnp.int32), axis=1)
        live_slots = (jnp.arange(CAP, dtype=jnp.int32)[None, :] < counts[:, None]).reshape(-1)
        sent_flags = jnp.zeros((POOL,), jnp.int32).at[own_blocks].set(1)
        identity = jnp.arange(id_count, dtype=jnp.int32)
        ranking_class = jnp.concatenate([1 + 2 * sent_flags, jnp.where(live_slots, 0, 2).astype(jnp.int32)])
        jitter_draw = jax.random.randint(first_key, (id_count,), 0, 65536).astype(jnp.int32)
        sorted_ids = jnp.argsort(ranking_class * 2 ** 26 + jitter_draw * id_count + identity, stable=True)
        picked = jax.random.permutation(second_key, sorted_ids[:SLOTS * BLK_REQ])
        return picked.reshape(SLOTS, BLK_REQ).astype(jnp.int32)
    tables = jax.vmap(instance_table)(jnp.arange(N_INST, dtype=jnp.int32), block_lists)
    return (dest_lists.reshape(-1), block_lists.reshape(-1), tables.reshape(N_INST * SLOTS, BLK_REQ))


def draw_send_dest(key, part):
    return migration_plan(key)[0]


def draw_send_block(key, part):
    return migration_plan(key)[1]


def draw_block_table(key, part):
    return migration_plan(key)[2]


def draw_cache_len(key, part):
    key = jax.random.fold_in(key, 5)
    first_key, second_key = jax.random.split(key, 2)
    lengths = jax.random.randint(first_key, (N_INST * SLOTS,), 1, BLK_REQ * BLOCK + 1).astype(jnp.int32)
    full_slot = jax.random.randint(second_key, (N_INST,), 0, SLOTS).astype(jnp.int32)
    positions = jnp.arange(N_INST * SLOTS, dtype=jnp.int32)
    is_full = positions % SLOTS == full_slot[positions // SLOTS]
    return jnp.where(is_full, BLK_REQ * BLOCK, lengths).astype(jnp.int32)


def draw_queries(key, part):
    key = jax.random.fold_in(key, 7)
    shape_all = (STEPS, N_INST * SLOTS, H * HD)
    values = jnp.clip(jax.random.normal(key, shape_all, jnp.float32), -6.0, 6.0)
    return values.astype(jnp.bfloat16)


def levels(key, extent, cuts, low, high):
    loudness, own = 1.0, jax.random.fold_in(key, 6)
    for position, blocks in cuts:
        draws = jnp.exp(jax.random.uniform(jax.random.fold_in(own, position), (blocks,), jnp.float32, low / len(cuts), high / len(cuts)))
        loudness = loudness * jnp.repeat(draws, extent[position] // blocks).reshape([-1 if axis == position else 1 for axis in range(len(extent))])
    return loudness


def gaussian(stream_key, extent, width, most, pieces=(), held_as=jnp.bfloat16):
    values = jax.random.normal(stream_key, extent, jnp.float32) * width
    if len(pieces) > 0:
        values = levels(stream_key, extent, pieces, -0.22, 0.18) * values
    return jnp.clip(values, min=-most, max=most).astype(held_as)


def setup_inputs(seed: int = 0) -> dict:
    key_of = jax.random.split(jax.random.key(seed), 9)
    return {
        "queries": draw_queries(jax.random.fold_in(key_of[8], 71), 0),
        "new_kv": gaussian(key_of[1], (STEPS, R, KVH, 2 * HD), 1.0, 6.0, ((1, 16), (2, 8))),
        "kv_pool": gaussian(key_of[2], (N_INST * POOL, BLOCK, KVH, 2 * HD), 1.0, 6.0, ((0, 16), (2, 8))),
        "out_weight": gaussian(key_of[3], (H * HD, D), (H * HD) ** -0.5, 0.0625, ((0, 8),)),
        "send_block": draw_send_block(jax.random.fold_in(key_of[8], 71), 0),
        "send_dest": draw_send_dest(jax.random.fold_in(key_of[8], 71), 0),
        "block_table": draw_block_table(jax.random.fold_in(key_of[8], 71), 0),
        "cache_len": draw_cache_len(jax.random.fold_in(key_of[8], 71), 0),
    }


def reference(queries, new_kv, kv_pool, out_weight, send_block, send_dest, block_table, cache_len):
    head_group = H // KVH
    score_scale = HD ** -0.5
    dest_lists = send_dest.reshape(N_INST, MIGB)
    sent_lists = send_block.reshape(N_INST, MIGB)
    owners = jnp.arange(N_INST, dtype=jnp.int32)
    source_rows = (owners[:, None] * POOL + sent_lists).reshape(-1)
    cache_span = BLK_REQ * BLOCK
    highest = lax.Precision.HIGHEST

    def one_instance(inst_index):
        is_target = dest_lists == inst_index
        target_rank = jnp.cumsum(is_target.astype(jnp.int32), axis=1) - 1
        arrival_slot = jnp.where(is_target, owners[:, None] * CAP + target_rank, N_INST * CAP).reshape(-1)
        arrived = jnp.zeros((N_INST * CAP + 1, BLOCK, KVH, 2 * HD), jnp.bfloat16)
        arrived = arrived.at[arrival_slot].set(kv_pool[source_rows])[: N_INST * CAP]
        own_pool = lax.dynamic_slice_in_dim(kv_pool, (inst_index * POOL).astype(jnp.int32), POOL, 0)
        extended = jnp.concatenate([own_pool, arrived], axis=0)
        first_row = (inst_index * SLOTS).astype(jnp.int32)
        inst_table = lax.dynamic_slice_in_dim(block_table, first_row, SLOTS, 0)
        inst_lens = lax.dynamic_slice_in_dim(cache_len, first_row, SLOTS, 0)
        cached = extended[inst_table].reshape(SLOTS, cache_span, KVH, 2 * HD).astype(jnp.float32)
        inst_query = lax.dynamic_slice_in_dim(queries, first_row, SLOTS, 1).astype(jnp.float32)
        inst_query = inst_query.reshape(STEPS, SLOTS, KVH, head_group, HD)
        new_tokens = lax.dynamic_slice_in_dim(new_kv, first_row, SLOTS, 1).astype(jnp.float32)
        old_scores = jnp.einsum('tskgd,slkd->tskgl', inst_query, cached[..., :HD], precision=highest) * score_scale
        is_live = jnp.arange(cache_span, dtype=jnp.int32)[None, :] < inst_lens[:, None]
        old_scores = jnp.where(is_live[None, :, None, None, :], old_scores, -jnp.inf)
        new_scores = jnp.einsum('tskgd,uskd->tskgu', inst_query, new_tokens[..., :HD], precision=highest) * score_scale
        causal = jnp.arange(STEPS, dtype=jnp.int32)[:, None] >= jnp.arange(STEPS, dtype=jnp.int32)[None, :]
        new_scores = jnp.where(causal[:, None, None, None, :], new_scores, -jnp.inf)
        scores = jnp.concatenate([old_scores, new_scores], axis=-1)
        weights = jax.nn.softmax(scores, axis=-1)
        attended_inst = jnp.einsum('tskgl,slkd->tskgd', weights[..., :cache_span], cached[..., HD:], precision=highest)
        attended_inst = attended_inst + jnp.einsum('tskgu,uskd->tskgd', weights[..., cache_span:], new_tokens[..., HD:], precision=highest)
        return attended_inst.reshape(STEPS, SLOTS, H * HD).astype(jnp.bfloat16)

    attended = lax.map(one_instance, owners)
    attended = jnp.transpose(attended, (1, 0, 2, 3)).reshape(STEPS * N_INST * SLOTS, H * HD)
    projected = jnp.dot(attended, out_weight, preferred_element_type=jnp.float32)
    return projected.reshape(STEPS, N_INST * SLOTS, D).astype(jnp.bfloat16)
```

```python
import functools

import jax
import jax.numpy as jnp
from jax import lax
from jax.experimental import pallas as pl
from jax.experimental.pallas import tpu as pltpu
from jax.sharding import PartitionSpec as P

CAP = 2
INFO = 16
MASKED = -1e30
VMEM_BYTES = 40 * 1024 * 1024

SMEM = pl.BlockSpec(memory_space=pltpu.SMEM)
VMEM = pl.BlockSpec(memory_space=pltpu.VMEM)
HBM = pl.BlockSpec(memory_space=pl.ANY)

nt_dims = (((1,), (1,)), ((), ()))


def split_dot(weights, values):
    rows = weights.shape[0]
    high = weights.astype(jnp.bfloat16)
    low = (weights - high.astype(jnp.float32)).astype(jnp.bfloat16)
    both = jnp.dot(
        jnp.concatenate([high, low], axis=0), values, preferred_element_type=jnp.float32
    )
    return both[:rows] + both[rows:]


def ask_kernel(pool_size, block_len, table_ref, len_ref, q_ref, out_ref, slot_ref, live_ref):
    slots, blocks = table_ref.shape
    rows = q_ref.shape[1]
    n_inst = out_ref.shape[0]

    def clear(a, carry):
        slot_ref[a] = -1
        live_ref[a] = 0
        return carry

    lax.fori_loop(0, n_inst * CAP, clear, 0)
    for slot in range(slots):
        query = q_ref[slot]

        def entry(b, carry):
            block_id = table_ref[slot, b]

            @pl.when(block_id >= pool_size)
            def _():
                arrival = block_id - pool_size
                source = arrival // CAP
                start = pl.multiple_of((arrival % CAP) * rows, rows)
                out_ref[source, pl.ds(start, rows), :] = query
                slot_ref[arrival] = slot
                live_ref[arrival] = jnp.clip(len_ref[slot] - b * block_len, 0, block_len)

            return carry

        lax.fori_loop(0, blocks, entry, 0)
    row = lax.broadcasted_iota(jnp.int32, (INFO, 128), 0)

    def info(source, carry):
        live = jnp.where(row < INFO // 2, live_ref[source * CAP], live_ref[source * CAP + 1])
        out_ref[source, CAP * rows :, :] = live.astype(jnp.float32).astype(jnp.bfloat16)
        return carry

    lax.fori_loop(0, n_inst, info, 0)


def own_kernel(
    scale, head_group, table_ref, len_ref, q_ref, new_ref, pool_ref,
    peak_ref, sum_ref, acc_ref, kv_ref, sems,
):
    slots, blocks = table_ref.shape
    pool_size, block_len, _ = pool_ref.shape
    rows = q_ref.shape[1]
    steps = new_ref.shape[0]
    head = q_ref.shape[2]
    span = blocks * block_len

    def copy(slot, b):
        block_id = jnp.minimum(table_ref[slot, b], pool_size - 1)
        return pltpu.make_async_copy(
            pool_ref.at[block_id],
            kv_ref.at[slot, pl.ds(b * block_len, block_len), :],
            sems.at[slot, b],
        )

    for slot in range(slots):
        for b in range(blocks):
            copy(slot, b).start()
    lane = lax.broadcasted_iota(jnp.int32, (rows, block_len), 1)
    step = lax.broadcasted_iota(jnp.int32, (rows, block_len), 0) // head_group
    for slot in range(slots):
        fresh = jnp.concatenate(
            [new_ref[u, slot : slot + 1, :].astype(jnp.float32) for u in range(steps)]
            + [jnp.zeros((block_len - steps, 2 * head), jnp.float32)],
            axis=0,
        )
        kv_ref[slot, span:, :] = fresh.astype(jnp.bfloat16)
    for slot in range(slots):
        for b in range(blocks):
            copy(slot, b).wait()
        scores = lax.dot_general(
            q_ref[slot], kv_ref[slot, :, :head], nt_dims, preferred_element_type=jnp.float32
        ) * scale
        parts = []
        for b in range(blocks):
            live = jnp.clip(len_ref[slot] - b * block_len, 0, block_len)
            live = jnp.where(table_ref[slot, b] < pool_size, live, 0)
            part = scores[:, b * block_len : (b + 1) * block_len]
            parts.append(jnp.where(lane < live, part, MASKED))
        parts.append(jnp.where((lane <= step) & (lane < steps), scores[:, span:], MASKED))
        peaks = functools.reduce(jnp.maximum, parts)
        peak = jnp.max(peaks, axis=1, keepdims=True)
        weights = [jnp.exp(part - peak) for part in parts]
        total = jnp.sum(functools.reduce(jnp.add, weights), axis=1, keepdims=True)
        acc_ref[slot] = split_dot(jnp.concatenate(weights, axis=1), kv_ref[slot, :, head:])
        peak_ref[slot] = jnp.broadcast_to(peak, (rows, head))
        sum_ref[slot] = jnp.broadcast_to(total, (rows, head))


def split_rows(row, values):
    high = values.astype(jnp.bfloat16).astype(jnp.float32)
    rest = values - high
    middle = rest.astype(jnp.bfloat16).astype(jnp.float32)
    return high, middle, rest - middle


def answer_kernel(
    scale, block_ref, dest_ref, asked_ref, pool_ref, out_ref, kv_ref, peak_ref, sum_ref, seen_ref, sems
):
    pool_size, block_len, width = pool_ref.shape
    head = width // 2
    n_inst = out_ref.shape[0]
    rows = (out_ref.shape[1] - INFO) // CAP
    entries = block_ref.shape[0]

    def copy(e):
        block_id = jnp.clip(block_ref[e], 0, pool_size - 1)
        return pltpu.make_async_copy(pool_ref.at[block_id], kv_ref.at[e], sems.at[e])

    for e in range(entries):
        copy(e).start()
    for i in range(n_inst):
        seen_ref[i] = 0
    peak_ref[...] = jnp.zeros_like(peak_ref)
    sum_ref[...] = jnp.zeros_like(sum_ref)
    lane = lax.broadcasted_iota(jnp.int32, (rows, block_len), 1)
    row = lax.broadcasted_iota(jnp.int32, (rows, block_len), 0)
    for e in range(entries):
        dest = jnp.clip(dest_ref[e], 0, n_inst - 1)
        rank = jnp.minimum(seen_ref[dest], CAP - 1)
        seen_ref[dest] = seen_ref[dest] + 1
        start = pl.multiple_of(rank * rows, rows)
        copy(e).wait()
        query = asked_ref[dest, pl.ds(start, rows), :]
        info = asked_ref[dest, CAP * rows :, :].astype(jnp.float32)
        live = jnp.where(rank == 0, info[0:1], info[INFO // 2 : INFO // 2 + 1])
        scores = lax.dot_general(
            query, kv_ref[e, :, :head], nt_dims, preferred_element_type=jnp.float32
        ) * scale
        scores = jnp.where(lane.astype(jnp.float32) < live, scores, MASKED)
        peak = jnp.max(scores, axis=1, keepdims=True)
        weights = jnp.where(lane.astype(jnp.float32) < live, jnp.exp(scores - peak), 0.0)
        total = jnp.sum(weights, axis=1, keepdims=True)
        values = split_dot(weights, kv_ref[e, :, head:])
        values = values / jnp.where(total > 0.0, total, 1.0)
        out_ref[dest, pl.ds(start, rows), :] = values.astype(jnp.bfloat16)
        here = lane == row + start
        peak_ref[pl.ds(dest, 1), :] += jnp.sum(jnp.where(here, peak, 0.0), axis=0, keepdims=True)
        sum_ref[pl.ds(dest, 1), :] += jnp.sum(jnp.where(here, total, 0.0), axis=0, keepdims=True)
    row = lax.broadcasted_iota(jnp.int32, (INFO, block_len), 0)
    peaks = split_rows(row, peak_ref[...])
    sums = split_rows(row, sum_ref[...])
    for i in range(n_inst):
        info = jnp.zeros((INFO, block_len), jnp.float32)
        for k, term in enumerate(peaks + sums):
            info = jnp.where(row == k, term[i : i + 1], info)
        out_ref[i, CAP * rows :, :] = info.astype(jnp.bfloat16)


def project_kernel(
    slot_ref, back_ref, peak_ref, sum_ref, acc_ref, weight_ref, out_ref,
    m_ref, l_ref, a_ref, att_ref, w_ref, sems,
):
    slots, rows, head = acc_ref.shape
    n_inst = back_ref.shape[0]
    parts, out_rows, part_cols = out_ref.shape
    steps = out_rows // slots
    group = rows // steps

    def copy(c):
        return pltpu.make_async_copy(
            weight_ref.at[:, pl.ds(c * part_cols, part_cols)], w_ref.at[c], sems.at[c]
        )

    for c in range(parts):
        copy(c).start()
    m_ref[...] = peak_ref[...]
    l_ref[...] = sum_ref[...]
    a_ref[...] = acc_ref[...]
    lane = lax.broadcasted_iota(jnp.int32, (rows, head), 1)
    row = lax.broadcasted_iota(jnp.int32, (rows, head), 0)

    def source(s, carry):
        info = back_ref[s, CAP * rows :, :].astype(jnp.float32)
        peaks = info[0:1] + info[1:2] + info[2:3]
        sums = info[3:4] + info[4:5] + info[5:6]
        for r in range(CAP):
            slot = slot_ref[s * CAP + r]

            @pl.when(slot >= 0)
            def _():
                here = lane == row + r * rows
                peak = jnp.sum(jnp.where(here, peaks, 0.0), axis=1, keepdims=True)
                total = jnp.sum(jnp.where(here, sums, 0.0), axis=1, keepdims=True)
                values = back_ref[s, r * rows : (r + 1) * rows, :].astype(jnp.float32)
                old = m_ref[slot]
                new = jnp.maximum(old, peak)
                keep = jnp.exp(old - new)
                gain = jnp.exp(peak - new) * total
                m_ref[slot] = new
                l_ref[slot] = l_ref[slot] * keep + gain
                a_ref[slot] = a_ref[slot] * keep + gain * values

        return carry

    lax.fori_loop(0, n_inst, source, 0)
    for slot in range(slots):
        done = a_ref[slot] / l_ref[slot]
        for step in range(steps):
            for g in range(group):
                at = step * group + g
                att_ref[step * slots + slot : step * slots + slot + 1, g * head : (g + 1) * head] = (
                    done[at : at + 1]
                )
    attended = att_ref[...].astype(jnp.bfloat16)
    for c in range(parts):
        copy(c).wait()
        out_ref[c] = jnp.dot(
            attended, w_ref[c], preferred_element_type=jnp.float32
        ).astype(jnp.bfloat16)


def params():
    return pltpu.CompilerParams(vmem_limit_bytes=VMEM_BYTES)


def shards(queries, new_kv, kv_pool, out_weight, send_block, send_dest, block_table, cache_len):
    n_inst = lax.axis_size("inst")
    n_tp = lax.axis_size("tp")
    steps, slots, head_width = queries.shape
    pool_size, block_len, _, width = kv_pool.shape
    head = width // 2
    group = head_width // head
    rows = steps * group
    blocks = block_table.shape[1]
    entries = send_block.shape[0]
    columns = out_weight.shape[1]
    scale = head ** (-0.5)
    f32, bf16 = jnp.float32, jnp.bfloat16
    pool = kv_pool.reshape(pool_size, block_len, width)
    fresh = new_kv.reshape(steps, slots, width)
    slot_query = jnp.transpose(
        queries.reshape(steps, slots, group, head), (1, 0, 2, 3)
    ).reshape(slots, rows, head)

    packet = jax.ShapeDtypeStruct((n_inst, CAP * rows + INFO, head), bf16)
    ask, slot_of = pl.pallas_call(
        functools.partial(ask_kernel, pool_size, block_len),
        out_shape=(packet, jax.ShapeDtypeStruct((n_inst * CAP,), jnp.int32)),
        in_specs=[SMEM, SMEM, VMEM],
        out_specs=(VMEM, SMEM),
        scratch_shapes=[pltpu.SMEM((n_inst * CAP,), jnp.int32)],
        compiler_params=params(),
        name="ask",
    )(block_table, cache_len, slot_query)
    asked = lax.all_to_all(ask, "inst", 0, 0, tiled=True)

    own = jax.ShapeDtypeStruct((slots, rows, head), f32)
    own_peak, own_sum, own_acc = pl.pallas_call(
        functools.partial(own_kernel, scale, group),
        out_shape=(own, own, own),
        in_specs=[SMEM, SMEM, VMEM, VMEM, HBM],
        out_specs=(VMEM, VMEM, VMEM),
        scratch_shapes=[
            pltpu.VMEM((slots, (blocks + 1) * block_len, width), bf16),
            pltpu.SemaphoreType.DMA((slots, blocks)),
        ],
        compiler_params=params(),
        cost_estimate=pl.CostEstimate(
            flops=4 * slots * rows * blocks * block_len * width,
            bytes_accessed=slots * blocks * block_len * width * 2,
            transcendentals=slots * rows * blocks * block_len,
        ),
        name="own",
    )(block_table, cache_len, slot_query, fresh, pool)

    answer = pl.pallas_call(
        functools.partial(answer_kernel, scale),
        out_shape=packet,
        in_specs=[SMEM, SMEM, VMEM, HBM],
        out_specs=VMEM,
        scratch_shapes=[
            pltpu.VMEM((entries, block_len, width), bf16),
            pltpu.VMEM((n_inst, head), f32),
            pltpu.VMEM((n_inst, head), f32),
            pltpu.SMEM((n_inst,), jnp.int32),
            pltpu.SemaphoreType.DMA((entries,)),
        ],
        compiler_params=params(),
        name="answer",
    )(send_block, send_dest, asked, pool)
    back = lax.all_to_all(answer, "inst", 0, 0, tiled=True)

    out_rows = steps * slots
    partial_out = pl.pallas_call(
        project_kernel,
        out_shape=jax.ShapeDtypeStruct((n_tp, out_rows, columns // n_tp), bf16),
        in_specs=[SMEM, VMEM, VMEM, VMEM, VMEM, HBM],
        out_specs=VMEM,
        scratch_shapes=[
            pltpu.VMEM((slots, rows, head), f32),
            pltpu.VMEM((slots, rows, head), f32),
            pltpu.VMEM((slots, rows, head), f32),
            pltpu.VMEM((out_rows, head_width), f32),
            pltpu.VMEM((n_tp, head_width, columns // n_tp), bf16),
            pltpu.SemaphoreType.DMA((n_tp,)),
        ],
        compiler_params=params(),
        name="project",
    )(slot_of, back, own_peak, own_sum, own_acc, out_weight)
    shares = lax.all_to_all(partial_out, "tp", 0, 0, tiled=True)
    total = jnp.sum(shares.astype(f32), axis=0).astype(bf16)
    return total.reshape(steps, slots, columns // n_tp)


def solution(mesh):
    return jax.shard_map(
        shards,
        mesh=mesh,
        in_specs=(
            P(None, "inst", "tp"),
            P(None, "inst", "tp", None),
            P("inst", None, "tp", None),
            P("tp", None),
            P("inst"),
            P("inst"),
            P("inst", None),
            P("inst"),
        ),
        out_specs=P(None, "inst", "tp"),
        check_vma=False,
    )
```

```python
import functools

import jax
import jax.numpy as jnp
from jax import lax
from jax.experimental import pallas as pl
from jax.experimental.pallas import tpu as pltpu
from jax.sharding import PartitionSpec as P

CAP = 2
INFO = 16
MASKED = -1e30

SMEM = pl.BlockSpec(memory_space=pltpu.SMEM)
VMEM = pl.BlockSpec(memory_space=pltpu.VMEM)
HBM = pl.BlockSpec(memory_space=pltpu.HBM)

nt_dims = (((1,), (1,)), ((), ()))


def split_dot(weights, values):
    rows = weights.shape[0]
    high = weights.astype(jnp.bfloat16)
    low = (weights - high.astype(jnp.float32)).astype(jnp.bfloat16)
    both = jnp.dot(
        jnp.concatenate([high, low], axis=0), values, preferred_element_type=jnp.float32
    )
    return both[:rows] + both[rows:]


def ask_kernel(
    pool_size, block_len, table_hbm, len_hbm, block_hbm, dest_hbm, q_hbm,
    out_ref, query_ref, plan_ref,
    table_ref, len_ref, block_ref, dest_ref, code_ref, live_ref, q_ref, rows_ref, sems,
):
    slots, blocks = table_ref.shape
    steps = q_ref.shape[0]
    rows, head = query_ref.shape[1:]
    group = rows // steps
    arrivals = out_ref.shape[0] * CAP
    copies = [
        pltpu.make_async_copy(source, target, sems.at[k])
        for k, (source, target) in enumerate(
            (
                (q_hbm, q_ref),
                (table_hbm, table_ref),
                (len_hbm, len_ref),
                (block_hbm, block_ref),
                (dest_hbm, dest_ref),
            )
        )
    ]
    for copy in copies:
        copy.start()
    for a in range(arrivals):
        code_ref[a] = 0
        live_ref[a] = 0
    for copy in copies:
        copy.wait()
    for step in range(steps):
        query = q_ref[step].astype(jnp.float32)
        for slot in range(slots):
            for g in range(group):
                at = step * group + g
                rows_ref[slot, at : at + 1, :] = query[slot : slot + 1, g * head : (g + 1) * head]
    for slot in range(slots):
        length = len_ref[slot]
        for b in range(blocks):
            block_id = table_ref[slot, b]
            arrival = jnp.where(block_id >= pool_size, block_id - pool_size, arrivals)
            code_ref[arrival] = slot
            live_ref[arrival] = jnp.clip(length - b * block_len, 0, block_len)
            plan_ref[slot * blocks + b] = block_id
    for slot in range(slots):
        query_ref[slot] = rows_ref[slot].astype(jnp.bfloat16)
    row = lax.broadcasted_iota(jnp.int32, (INFO, head), 0)
    for a in range(arrivals):
        source, rank = a // CAP, a % CAP
        out_ref[source, rank * rows : (rank + 1) * rows, :] = query_ref[code_ref[a]]
    for source in range(arrivals // CAP):
        live = jnp.where(row < INFO // 2, live_ref[source * CAP], live_ref[source * CAP + 1])
        out_ref[source, CAP * rows :, :] = live.astype(jnp.float32).astype(jnp.bfloat16)
    base = slots * blocks
    for ref in (len_ref, block_ref, dest_ref):
        for k in range(ref.shape[0]):
            plan_ref[base + k] = ref[k]
        base += ref.shape[0]


def own_kernel(
    scale, head_group, blocks,
    plan_ref, q_ref, new_ref, pool_ref,
    peak_ref, sum_ref, acc_ref, sent_ref, place_ref,
    seen_ref, kv_ref, sems, sent_sems,
):
    pool_size, block_len, _ = pool_ref.shape
    slots, rows, head = q_ref.shape
    steps = new_ref.shape[0]
    span = blocks * block_len
    entries = sent_ref.shape[0]
    n_inst = seen_ref.shape[0]
    arrivals = n_inst * CAP
    len_at = slots * blocks
    block_at = len_at + slots
    dest_at = block_at + entries

    def own_copy(slot, b):
        block_id = jnp.clip(plan_ref[slot * blocks + b], 0, pool_size - 1)
        return pltpu.make_async_copy(
            pool_ref.at[block_id],
            kv_ref.at[slot, pl.ds(b * block_len, block_len), :],
            sems.at[slot, b],
        )

    def sent_copy(e):
        block_id = jnp.clip(plan_ref[block_at + e], 0, pool_size - 1)
        return pltpu.make_async_copy(pool_ref.at[block_id], sent_ref.at[e], sent_sems.at[e])

    for slot in range(slots):
        for b in range(blocks):
            own_copy(slot, b).start()
    for e in range(entries):
        sent_copy(e).start()
    for i in range(n_inst):
        seen_ref[i] = 0
    for e in range(entries):
        dest = jnp.clip(plan_ref[dest_at + e], 0, n_inst - 1)
        rank = seen_ref[dest]
        seen_ref[dest] = rank + 1
        place_ref[e] = jnp.minimum(rank, CAP - 1) * n_inst + dest
    for a in range(arrivals):
        place_ref[entries + a] = -1
    for slot in range(slots):
        for b in range(blocks):
            block_id = plan_ref[slot * blocks + b]
            arrival = jnp.where(block_id >= pool_size, block_id - pool_size, arrivals)
            place_ref[entries + arrival] = slot
    lane = lax.broadcasted_iota(jnp.int32, (rows, block_len), 1)
    step = lax.broadcasted_iota(jnp.int32, (rows, block_len), 0) // head_group
    for slot in range(slots):
        fresh = jnp.concatenate(
            [new_ref[u, slot : slot + 1, :].astype(jnp.float32) for u in range(steps)]
            + [jnp.zeros((block_len - steps, 2 * head), jnp.float32)],
            axis=0,
        )
        kv_ref[slot, span:, :] = fresh.astype(jnp.bfloat16)
    for slot in range(slots):
        for b in range(blocks):
            own_copy(slot, b).wait()
        scores = lax.dot_general(
            q_ref[slot], kv_ref[slot, :, :head], nt_dims, preferred_element_type=jnp.float32
        ) * scale
        parts_s = []
        for b in range(blocks):
            live = jnp.clip(plan_ref[len_at + slot] - b * block_len, 0, block_len)
            live = jnp.where(plan_ref[slot * blocks + b] < pool_size, live, 0)
            part = scores[:, b * block_len : (b + 1) * block_len]
            parts_s.append(jnp.where(lane < live, part, MASKED))
        parts_s.append(jnp.where((lane <= step) & (lane < steps), scores[:, span:], MASKED))
        peak = jnp.max(functools.reduce(jnp.maximum, parts_s), axis=1, keepdims=True)
        weights = [jnp.exp(part - peak) for part in parts_s]
        total = jnp.sum(functools.reduce(jnp.add, weights), axis=1, keepdims=True)
        acc_ref[slot] = split_dot(jnp.concatenate(weights, axis=1), kv_ref[slot, :, head:])
        peak_ref[slot] = jnp.broadcast_to(peak, (rows, head))
        sum_ref[slot] = jnp.broadcast_to(total, (rows, head))
    for e in range(entries):
        sent_copy(e).wait()


def three_terms(values):
    high = values.astype(jnp.bfloat16).astype(jnp.float32)
    rest = values - high
    middle = rest.astype(jnp.bfloat16).astype(jnp.float32)
    return high, middle, rest - middle


def answer_kernel(
    scale, place_ref, asked_ref, sent_ref, out_ref, peak_ref, sum_ref
):
    entries, block_len, width = sent_ref.shape
    head = width // 2
    n_inst = out_ref.shape[0]
    rows = (out_ref.shape[1] - INFO) // CAP
    peak_ref[...] = jnp.zeros_like(peak_ref)
    sum_ref[...] = jnp.zeros_like(sum_ref)
    lane = lax.broadcasted_iota(jnp.int32, (rows, block_len), 1)
    row = lax.broadcasted_iota(jnp.int32, (rows, block_len), 0)
    key = lane.astype(jnp.float32)
    places, starts, masks, scores = [], [], [], []
    for e in range(entries):
        place = place_ref[e]
        dest = lax.rem(place, n_inst)
        rank = lax.div(place, n_inst)
        start = pl.multiple_of(rank * rows, rows)
        query = asked_ref[dest, pl.ds(start, rows), :]
        info = asked_ref[dest, CAP * rows :, :].astype(jnp.float32)
        live = jnp.where(rank == 0, info[0:1], info[INFO // 2 : INFO // 2 + 1])
        places.append((place, dest))
        starts.append(start)
        masks.append(key < live)
        scores.append(
            lax.dot_general(
                query, sent_ref[e, :, :head], nt_dims, preferred_element_type=jnp.float32
            )
        )
    peaks, totals, results = [], [], []
    for e in range(entries):
        masked = jnp.where(masks[e], scores[e] * scale, MASKED)
        peak = jnp.max(masked, axis=1, keepdims=True)
        weights = jnp.where(masks[e], jnp.exp(masked - peak), 0.0)
        total = jnp.sum(weights, axis=1, keepdims=True)
        values = split_dot(weights, sent_ref[e, :, head:])
        peaks.append(peak)
        totals.append(total)
        results.append((values / jnp.where(total > 0.0, total, 1.0)).astype(jnp.bfloat16))
    for e in range(entries):
        place, dest = places[e]
        out_ref[dest, pl.ds(starts[e], rows), :] = results[e]
        here = lane == row + starts[e]
        peak_ref[pl.ds(place, 1), :] = jnp.sum(
            jnp.where(here, peaks[e], 0.0), axis=0, keepdims=True
        )
        sum_ref[pl.ds(place, 1), :] = jnp.sum(
            jnp.where(here, totals[e], 0.0), axis=0, keepdims=True
        )
    row = lax.broadcasted_iota(jnp.int32, (INFO, block_len), 0)
    terms = three_terms(peak_ref[:n_inst] + peak_ref[n_inst:])
    terms += three_terms(sum_ref[:n_inst] + sum_ref[n_inst:])
    for i in range(n_inst):
        info = jnp.zeros((INFO, block_len), jnp.float32)
        for k, term in enumerate(terms):
            info = jnp.where(row == k, term[i : i + 1], info)
        out_ref[i, CAP * rows :, :] = info.astype(jnp.bfloat16)


def project_kernel(
    first_slot, slot_ref, back_ref, peak_ref, sum_ref, acc_ref, weight_ref, out_ref,
    m_ref, l_ref, a_ref, att_ref, w_ref, sems,
):
    slots, rows, head = acc_ref.shape
    n_inst = back_ref.shape[0]
    parts, out_rows, part_cols = out_ref.shape
    steps = out_rows // slots
    group = rows // steps
    copies = [
        pltpu.make_async_copy(
            weight_ref.at[:, pl.ds(c * part_cols, part_cols)], w_ref.at[c], sems.at[c]
        )
        for c in range(parts)
    ]
    for copy in copies:
        copy.start()
    lane = lax.broadcasted_iota(jnp.int32, (rows, head), 1)
    row = lax.broadcasted_iota(jnp.int32, (rows, head), 0)
    arrivals = []
    best = [peak_ref[slot] for slot in range(slots)]
    for s in range(n_inst):
        info = back_ref[s, CAP * rows :, :].astype(jnp.float32)
        peaks = info[0:1] + info[1:2] + info[2:3]
        sums = info[3:4] + info[4:5] + info[5:6]
        for r in range(CAP):
            slot = slot_ref[first_slot + s * CAP + r]
            here = lane == row + r * rows
            peak = jnp.sum(jnp.where(here, peaks, 0.0), axis=1, keepdims=True)
            total = jnp.sum(jnp.where(here, sums, 0.0), axis=1, keepdims=True)
            arrivals.append((slot, peak, total))
            for k in range(slots):
                best[k] = jnp.maximum(best[k], jnp.where(slot == k, peak, MASKED))
    for k in range(slots):
        keep = jnp.exp(peak_ref[k] - best[k])
        m_ref[k] = best[k]
        l_ref[k] = sum_ref[k] * keep
        a_ref[k] = acc_ref[k] * keep
    for a, (slot, peak, total) in enumerate(arrivals):
        s, r = a // CAP, a % CAP
        at = jnp.maximum(slot, 0)
        gain = jnp.where(slot >= 0, total * jnp.exp(peak - m_ref[at]), 0.0)
        values = back_ref[s, r * rows : (r + 1) * rows, :].astype(jnp.float32)
        l_ref[at] += gain
        a_ref[at] += jnp.where(slot >= 0, gain * values, 0.0)
    for slot in range(slots):
        done = a_ref[slot] / l_ref[slot]
        for step in range(steps):
            for g in range(group):
                at = step * group + g
                to = step * slots + slot
                att_ref[to : to + 1, g * head : (g + 1) * head] = done[at : at + 1]
    attended = att_ref[...].astype(jnp.bfloat16)
    for c in range(parts):
        copies[c].wait()
        out_ref[c] = jnp.dot(
            attended, w_ref[c], preferred_element_type=jnp.float32
        ).astype(jnp.bfloat16)


def params(mib):
    return pltpu.CompilerParams(vmem_limit_bytes=mib * 1024 * 1024)


def shards(queries, new_kv, kv_pool, out_weight, send_block, send_dest, block_table, cache_len):
    n_inst = lax.axis_size("inst")
    n_tp = lax.axis_size("tp")
    steps, slots, head_width = queries.shape
    pool_size, block_len, _, width = kv_pool.shape
    head = width // 2
    group = head_width // head
    rows = steps * group
    blocks = block_table.shape[1]
    entries = send_block.shape[0]
    columns = out_weight.shape[1]
    arrivals = n_inst * CAP
    scale = head ** (-0.5)
    f32, bf16, i32 = jnp.float32, jnp.bfloat16, jnp.int32
    shape = jax.ShapeDtypeStruct
    pool = kv_pool.reshape(pool_size, block_len, width)
    fresh = new_kv.reshape(steps, slots, width)

    packet = shape((n_inst, CAP * rows + INFO, head), bf16)
    ask, slot_query, plan = pl.pallas_call(
        functools.partial(ask_kernel, pool_size, block_len),
        out_shape=(
            packet,
            shape((slots, rows, head), bf16),
            shape((slots * blocks + slots + 2 * entries,), i32),
        ),
        in_specs=[HBM] * 5,
        out_specs=(VMEM, VMEM, SMEM),
        scratch_shapes=[
            pltpu.SMEM((slots, blocks), i32),
            pltpu.SMEM((slots,), i32),
            pltpu.SMEM((entries,), i32),
            pltpu.SMEM((entries,), i32),
            pltpu.SMEM((arrivals + 1,), i32),
            pltpu.SMEM((arrivals + 1,), i32),
            pltpu.VMEM(queries.shape, bf16),
            pltpu.VMEM((slots, rows, head), f32),
            pltpu.SemaphoreType.DMA((5,)),
        ],
        compiler_params=params(64),
        name="ask",
    )(block_table, cache_len, send_block, send_dest, queries)
    asked = lax.all_to_all(ask, "inst", 0, 0, tiled=True)

    own = shape((slots, rows, head), f32)
    own_peak, own_sum, own_acc, sent, place = pl.pallas_call(
        functools.partial(own_kernel, scale, group, blocks),
        out_shape=(
            own, own, own,
            shape((entries, block_len, width), bf16),
            shape((entries + arrivals + 1,), i32),
        ),
        in_specs=[SMEM, VMEM, VMEM, HBM],
        out_specs=(VMEM, VMEM, VMEM, VMEM, SMEM),
        scratch_shapes=[
            pltpu.SMEM((n_inst,), i32),
            pltpu.VMEM((slots, (blocks + 1) * block_len, width), bf16),
            pltpu.SemaphoreType.DMA((slots, blocks)),
            pltpu.SemaphoreType.DMA((entries,)),
        ],
        compiler_params=params(50),
        cost_estimate=pl.CostEstimate(
            flops=4 * slots * rows * blocks * block_len * width,
            bytes_accessed=8 * slots * blocks * block_len * width,
            transcendentals=slots * rows * blocks * block_len,
        ),
        name="own",
    )(plan, slot_query, fresh, pool)

    part_cols = columns // n_tp
    answer = pl.pallas_call(
        functools.partial(answer_kernel, scale),
        out_shape=packet,
        in_specs=[SMEM, VMEM, VMEM],
        out_specs=VMEM,
        scratch_shapes=[
            pltpu.VMEM((arrivals, head), f32),
            pltpu.VMEM((arrivals, head), f32),
        ],
        compiler_params=params(16),
        name="answer",
    )(place, asked, sent)
    back = lax.all_to_all(answer, "inst", 0, 0, tiled=True)

    out_rows = steps * slots
    partial_out = pl.pallas_call(
        functools.partial(project_kernel, entries),
        out_shape=shape((n_tp, out_rows, part_cols), bf16),
        in_specs=[SMEM, VMEM, VMEM, VMEM, VMEM, HBM],
        out_specs=VMEM,
        scratch_shapes=[
            pltpu.VMEM((slots, rows, head), f32),
            pltpu.VMEM((slots, rows, head), f32),
            pltpu.VMEM((slots, rows, head), f32),
            pltpu.VMEM((out_rows, head_width), f32),
            pltpu.VMEM((n_tp, head_width, part_cols), bf16),
            pltpu.SemaphoreType.DMA((n_tp,)),
        ],
        compiler_params=params(44),
        name="project",
    )(place, back, own_peak, own_sum, own_acc, out_weight)
    shares = lax.all_to_all(partial_out, "tp", 0, 0, tiled=True)
    total = jnp.sum(shares.astype(f32), axis=0).astype(bf16)
    return total.reshape(steps, slots, columns // n_tp)


def solution(mesh):
    return jax.shard_map(
        shards,
        mesh=mesh,
        in_specs=(
            P(None, "inst", "tp"),
            P(None, "inst", "tp", None),
            P("inst", None, "tp", None),
            P("tp", None),
            P("inst"),
            P("inst"),
            P("inst", None),
            P("inst"),
        ),
        out_specs=P(None, "inst", "tp"),
        check_vma=False,
    )
```

```python
import functools

import jax
import jax.numpy as jnp
from jax import lax
from jax.experimental import pallas as pl
from jax.experimental.pallas import tpu as pltpu
from jax.sharding import PartitionSpec as P

CAP = 2
INFO = 8
MASKED = -1e30
TILE = 256

SMEM = pl.BlockSpec(memory_space=pltpu.SMEM)
VMEM = pl.BlockSpec(memory_space=pltpu.VMEM)
HBM = pl.BlockSpec(memory_space=pltpu.HBM)

nt_dims = (((1,), (1,)), ((), ()))


def split_dot(weights, values):
    rows = weights.shape[0]
    high = weights.astype(jnp.bfloat16)
    low = (weights - high.astype(jnp.float32)).astype(jnp.bfloat16)
    both = jnp.dot(
        jnp.concatenate([high, low], axis=0), values, preferred_element_type=jnp.float32
    )
    return both[:rows] + both[rows:]


def ask_kernel(
    pool_size, block_len, table_hbm, len_hbm, block_hbm, dest_hbm, q_hbm,
    out_ref, query_ref, plan_ref,
    table_ref, len_ref, block_ref, dest_ref, code_ref, live_ref, q_ref, rows_ref, sems,
):
    slots, blocks = table_ref.shape
    steps = q_ref.shape[0]
    rows, head = query_ref.shape[1:]
    group = rows // steps
    arrivals = out_ref.shape[0] * CAP
    copies = [
        pltpu.make_async_copy(source, target, sems.at[k])
        for k, (source, target) in enumerate(
            (
                (q_hbm, q_ref),
                (table_hbm, table_ref),
                (len_hbm, len_ref),
                (block_hbm, block_ref),
                (dest_hbm, dest_ref),
            )
        )
    ]
    for copy in copies:
        copy.start()
    for a in range(arrivals):
        code_ref[a] = 0
        live_ref[a] = 0
    for copy in copies:
        copy.wait()
    for step in range(steps):
        query = q_ref[step].astype(jnp.float32)
        for slot in range(slots):
            for g in range(group):
                at = step * group + g
                rows_ref[slot, at : at + 1, :] = query[slot : slot + 1, g * head : (g + 1) * head]
    for slot in range(slots):
        length = len_ref[slot]
        for b in range(blocks):
            block_id = table_ref[slot, b]
            arrival = jnp.where(block_id >= pool_size, block_id - pool_size, arrivals)
            code_ref[arrival] = slot
            live_ref[arrival] = jnp.clip(length - b * block_len, 0, block_len)
            plan_ref[slot * blocks + b] = block_id
    for slot in range(slots):
        query_ref[slot] = rows_ref[slot].astype(jnp.bfloat16)
    row = lax.broadcasted_iota(jnp.int32, (INFO, head), 0)
    for a in range(arrivals):
        source, rank = a // CAP, a % CAP
        out_ref[source, rank * rows : (rank + 1) * rows, :] = query_ref[code_ref[a]]
    for source in range(arrivals // CAP):
        live = jnp.where(row < INFO // 2, live_ref[source * CAP], live_ref[source * CAP + 1])
        out_ref[source, CAP * rows :, :] = live.astype(jnp.float32).astype(jnp.bfloat16)
    base = slots * blocks
    for ref in (len_ref, block_ref, dest_ref):
        for k in range(ref.shape[0]):
            plan_ref[base + k] = ref[k]
        base += ref.shape[0]


def own_kernel(
    scale, head_group, blocks, first,
    plan_ref, q_ref, new_ref, pool_ref,
    peak_ref, sum_ref, acc_ref, kv_ref, sems, bring,
):
    pool_size, block_len, _ = pool_ref.shape
    slots, rows, head = q_ref.shape
    steps = new_ref.shape[0]
    span = blocks * block_len
    len_at = slots * blocks
    mine = range(first, first + peak_ref.shape[0])

    def own_copy(slot, b):
        block_id = jnp.clip(plan_ref[slot * blocks + b], 0, pool_size - 1)
        return pltpu.make_async_copy(
            pool_ref.at[block_id],
            kv_ref.at[slot - first, pl.ds(b * block_len, block_len), :],
            sems.at[slot - first, b],
        )

    for slot in mine:
        for b in range(blocks):
            own_copy(slot, b).start()
    brought = bring()
    lane = lax.broadcasted_iota(jnp.int32, (rows, block_len), 1)
    step = lax.broadcasted_iota(jnp.int32, (rows, block_len), 0) // head_group
    for slot in mine:
        fresh = jnp.concatenate(
            [new_ref[u, slot : slot + 1, :].astype(jnp.float32) for u in range(steps)]
            + [jnp.zeros((block_len - steps, 2 * head), jnp.float32)],
            axis=0,
        )
        kv_ref[slot - first, span:, :] = fresh.astype(jnp.bfloat16)
    for slot in mine:
        for b in range(blocks):
            own_copy(slot, b).wait()
        scores = lax.dot_general(
            q_ref[slot], kv_ref[slot - first, :, :head], nt_dims, preferred_element_type=jnp.float32
        ) * scale
        parts_s = []
        for b in range(blocks):
            live = jnp.clip(plan_ref[len_at + slot] - b * block_len, 0, block_len)
            live = jnp.where(plan_ref[slot * blocks + b] < pool_size, live, 0)
            part = scores[:, b * block_len : (b + 1) * block_len]
            parts_s.append(jnp.where(lane < live, part, MASKED))
        parts_s.append(jnp.where((lane <= step) & (lane < steps), scores[:, span:], MASKED))
        peak = jnp.max(functools.reduce(jnp.maximum, parts_s), axis=1, keepdims=True)
        weights = [jnp.exp(part - peak) for part in parts_s]
        total = jnp.sum(functools.reduce(jnp.add, weights), axis=1, keepdims=True)
        acc_ref[slot - first] = split_dot(jnp.concatenate(weights, axis=1), kv_ref[slot - first, :, head:])
        peak_ref[slot - first] = jnp.broadcast_to(peak, (rows, head))
        sum_ref[slot - first] = jnp.broadcast_to(total, (rows, head))
    for copy in brought:
        copy.wait()


def first_kernel(
    scale, head_group, blocks,
    plan_ref, q_ref, new_ref, pool_ref,
    peak_ref, sum_ref, acc_ref, sent_ref, place_ref,
    seen_ref, kv_ref, sems, sent_sems,
):
    pool_size = pool_ref.shape[0]
    slots = q_ref.shape[0]
    entries = sent_ref.shape[0]
    n_inst = seen_ref.shape[0]
    arrivals = n_inst * CAP
    block_at = slots * blocks + slots
    dest_at = block_at + entries

    def bring():
        copies = []
        for e in range(entries):
            block_id = jnp.clip(plan_ref[block_at + e], 0, pool_size - 1)
            copies.append(
                pltpu.make_async_copy(pool_ref.at[block_id], sent_ref.at[e], sent_sems.at[e])
            )
            copies[e].start()
        for i in range(n_inst):
            seen_ref[i] = 0
        for e in range(entries):
            dest = jnp.clip(plan_ref[dest_at + e], 0, n_inst - 1)
            rank = seen_ref[dest]
            seen_ref[dest] = rank + 1
            place_ref[e] = jnp.minimum(rank, CAP - 1) * n_inst + dest
        for a in range(arrivals):
            place_ref[entries + a] = -1
        for slot in range(slots):
            for b in range(blocks):
                block_id = plan_ref[slot * blocks + b]
                arrival = jnp.where(block_id >= pool_size, block_id - pool_size, arrivals)
                place_ref[entries + arrival] = slot
        return copies

    own_kernel(
        scale, head_group, blocks, 0, plan_ref, q_ref, new_ref, pool_ref,
        peak_ref, sum_ref, acc_ref, kv_ref, sems, bring,
    )


def second_kernel(
    scale, head_group, blocks, first,
    plan_ref, q_ref, new_ref, pool_ref, weight_ref, after_ref,
    peak_ref, sum_ref, acc_ref, held_ref,
    kv_ref, sems, weight_sem,
):
    del after_ref

    def bring():
        copy = pltpu.make_async_copy(
            weight_ref.at[:, pl.ds(0, held_ref.shape[1])], held_ref, weight_sem
        )
        copy.start()
        return [copy]

    own_kernel(
        scale, head_group, blocks, first, plan_ref, q_ref, new_ref, pool_ref,
        peak_ref, sum_ref, acc_ref, kv_ref, sems, bring,
    )


def three_terms(values):
    high = values.astype(jnp.bfloat16).astype(jnp.float32)
    rest = values - high
    middle = rest.astype(jnp.bfloat16).astype(jnp.float32)
    return high, middle, rest - middle


def answer_kernel(
    scale, place_ref, asked_ref, sent_ref, out_ref, peak_ref, sum_ref
):
    entries, block_len, width = sent_ref.shape
    head = width // 2
    n_inst = out_ref.shape[0]
    rows = (out_ref.shape[1] - INFO) // CAP
    peak_ref[...] = jnp.zeros_like(peak_ref)
    sum_ref[...] = jnp.zeros_like(sum_ref)
    lane = lax.broadcasted_iota(jnp.int32, (rows, block_len), 1)
    row = lax.broadcasted_iota(jnp.int32, (rows, block_len), 0)
    key = lane.astype(jnp.float32)
    places, starts, masks, scores = [], [], [], []
    for e in range(entries):
        place = place_ref[e]
        dest = lax.rem(place, n_inst)
        rank = lax.div(place, n_inst)
        start = pl.multiple_of(rank * rows, rows)
        query = asked_ref[dest, pl.ds(start, rows), :]
        info = asked_ref[dest, CAP * rows :, :].astype(jnp.float32)
        live = jnp.where(rank == 0, info[0:1], info[INFO // 2 : INFO // 2 + 1])
        places.append((place, dest))
        starts.append(start)
        masks.append(key < live)
        scores.append(
            lax.dot_general(
                query, sent_ref[e, :, :head], nt_dims, preferred_element_type=jnp.float32
            )
        )
    peaks, totals, results = [], [], []
    for e in range(entries):
        masked = jnp.where(masks[e], scores[e] * scale, MASKED)
        peak = jnp.max(masked, axis=1, keepdims=True)
        weights = jnp.where(masks[e], jnp.exp(masked - peak), 0.0)
        total = jnp.sum(weights, axis=1, keepdims=True)
        values = split_dot(weights, sent_ref[e, :, head:])
        peaks.append(peak)
        totals.append(total)
        results.append((values / jnp.where(total > 0.0, total, 1.0)).astype(jnp.bfloat16))
    for e in range(entries):
        place, dest = places[e]
        out_ref[dest, pl.ds(starts[e], rows), :] = results[e]
        here = lane == row + starts[e]
        peak_ref[pl.ds(place, 1), :] = jnp.sum(
            jnp.where(here, peaks[e], 0.0), axis=0, keepdims=True
        )
        sum_ref[pl.ds(place, 1), :] = jnp.sum(
            jnp.where(here, totals[e], 0.0), axis=0, keepdims=True
        )
    row = lax.broadcasted_iota(jnp.int32, (INFO, block_len), 0)
    terms = three_terms(peak_ref[:n_inst] + peak_ref[n_inst:])
    terms += three_terms(sum_ref[:n_inst] + sum_ref[n_inst:])
    for i in range(n_inst):
        info = jnp.zeros((INFO, block_len), jnp.float32)
        for k, term in enumerate(terms):
            info = jnp.where(row == k, term[i : i + 1], info)
        out_ref[i, CAP * rows :, :] = info.astype(jnp.bfloat16)


def project_kernel(
    first_slot, slot_ref, back_ref, peak_a, sum_a, acc_a, peak_b, sum_b, acc_b,
    held_ref, weight_ref, out_ref,
    m_ref, l_ref, a_ref, att_ref, w_ref, sems,
):
    slots, rows, head = a_ref.shape
    n_inst = back_ref.shape[0]
    parts, out_rows, part_cols = out_ref.shape
    held = held_ref.shape[1]
    half = acc_a.shape[0]
    steps = out_rows // slots
    group = rows // steps
    copies = {}
    for c in range(parts):
        low, high = max(held, c * part_cols), (c + 1) * part_cols
        if low < high:
            copies[c] = pltpu.make_async_copy(
                weight_ref.at[:, pl.ds(low, high - low)],
                w_ref.at[:, pl.ds(low - held, high - low)],
                sems.at[c],
            )
            copies[c].start()
    lane = lax.broadcasted_iota(jnp.int32, (rows, head), 1)
    row = lax.broadcasted_iota(jnp.int32, (rows, head), 0)
    arrivals = []
    peak_own = [peak_a[k] for k in range(half)] + [peak_b[k] for k in range(slots - half)]
    sum_own = [sum_a[k] for k in range(half)] + [sum_b[k] for k in range(slots - half)]
    acc_own = [acc_a[k] for k in range(half)] + [acc_b[k] for k in range(slots - half)]
    best = list(peak_own)
    for s in range(n_inst):
        info = back_ref[s, CAP * rows :, :].astype(jnp.float32)
        peaks = info[0:1] + info[1:2] + info[2:3]
        sums = info[3:4] + info[4:5] + info[5:6]
        for r in range(CAP):
            slot = slot_ref[first_slot + s * CAP + r]
            here = lane == row + r * rows
            peak = jnp.sum(jnp.where(here, peaks, 0.0), axis=1, keepdims=True)
            total = jnp.sum(jnp.where(here, sums, 0.0), axis=1, keepdims=True)
            arrivals.append((slot, peak, total))
            for k in range(slots):
                best[k] = jnp.maximum(best[k], jnp.where(slot == k, peak, MASKED))
    for k in range(slots):
        keep = jnp.exp(peak_own[k] - best[k])
        m_ref[k] = best[k]
        l_ref[k] = sum_own[k] * keep
        a_ref[k] = acc_own[k] * keep
    for a, (slot, peak, total) in enumerate(arrivals):
        s, r = a // CAP, a % CAP
        at = jnp.maximum(slot, 0)
        gain = jnp.where(slot >= 0, total * jnp.exp(peak - m_ref[at]), 0.0)
        values = back_ref[s, r * rows : (r + 1) * rows, :].astype(jnp.float32)
        l_ref[at] += gain
        a_ref[at] += jnp.where(slot >= 0, gain * values, 0.0)
    for slot in range(slots):
        done = a_ref[slot] / l_ref[slot]
        for step in range(steps):
            for g in range(group):
                at = step * group + g
                to = step * slots + slot
                att_ref[to : to + 1, g * head : (g + 1) * head] = done[at : at + 1]
    attended = att_ref[...].astype(jnp.bfloat16)
    for c in range(parts):
        if c in copies:
            copies[c].wait()
        for low in range(c * part_cols, (c + 1) * part_cols, TILE):
            if low < held:
                weight = held_ref[:, low : low + TILE]
            else:
                weight = w_ref[:, low - held : low - held + TILE]
            at = low - c * part_cols
            out_ref[c, :, at : at + TILE] = jnp.dot(
                attended, weight, preferred_element_type=jnp.float32
            ).astype(jnp.bfloat16)


def params(mib):
    return pltpu.CompilerParams(vmem_limit_bytes=mib * 1024 * 1024)


def shards(queries, new_kv, kv_pool, out_weight, send_block, send_dest, block_table, cache_len):
    n_inst = lax.axis_size("inst")
    n_tp = lax.axis_size("tp")
    steps, slots, head_width = queries.shape
    pool_size, block_len, _, width = kv_pool.shape
    head = width // 2
    group = head_width // head
    rows = steps * group
    blocks = block_table.shape[1]
    entries = send_block.shape[0]
    columns = out_weight.shape[1]
    arrivals = n_inst * CAP
    scale = head ** (-0.5)
    f32, bf16, i32 = jnp.float32, jnp.bfloat16, jnp.int32
    shape = jax.ShapeDtypeStruct
    pool = kv_pool.reshape(pool_size, block_len, width)
    fresh = new_kv.reshape(steps, slots, width)

    packet = shape((n_inst, CAP * rows + INFO, head), bf16)
    ask, slot_query, plan = pl.pallas_call(
        functools.partial(ask_kernel, pool_size, block_len),
        out_shape=(
            packet,
            shape((slots, rows, head), bf16),
            shape((slots * blocks + slots + 2 * entries,), i32),
        ),
        in_specs=[HBM] * 5,
        out_specs=(VMEM, VMEM, SMEM),
        scratch_shapes=[
            pltpu.SMEM((slots, blocks), i32),
            pltpu.SMEM((slots,), i32),
            pltpu.SMEM((entries,), i32),
            pltpu.SMEM((entries,), i32),
            pltpu.SMEM((arrivals + 1,), i32),
            pltpu.SMEM((arrivals + 1,), i32),
            pltpu.VMEM(queries.shape, bf16),
            pltpu.VMEM((slots, rows, head), f32),
            pltpu.SemaphoreType.DMA((5,)),
        ],
        compiler_params=params(64),
        name="ask",
    )(block_table, cache_len, send_block, send_dest, queries)
    asked = lax.all_to_all(ask, "inst", 0, 0, tiled=True)

    half = slots // 2
    own = shape((half, rows, head), f32)
    kv_scratch = pltpu.VMEM((half, (blocks + 1) * block_len, width), bf16)
    own_cost = pl.CostEstimate(
        flops=2 * slots * rows * blocks * block_len * width,
        bytes_accessed=4 * slots * blocks * block_len * width,
        transcendentals=half * rows * blocks * block_len,
    )
    peak_a, sum_a, acc_a, sent, place = pl.pallas_call(
        functools.partial(first_kernel, scale, group, blocks),
        out_shape=(
            own, own, own,
            shape((entries, block_len, width), bf16),
            shape((entries + arrivals + 1,), i32),
        ),
        in_specs=[SMEM, VMEM, VMEM, HBM],
        out_specs=(VMEM, VMEM, VMEM, VMEM, SMEM),
        scratch_shapes=[
            pltpu.SMEM((n_inst,), i32),
            kv_scratch,
            pltpu.SemaphoreType.DMA((half, blocks)),
            pltpu.SemaphoreType.DMA((entries,)),
        ],
        compiler_params=params(50),
        cost_estimate=own_cost,
        name="own_first",
    )(plan, slot_query, fresh, pool)

    part_cols = columns // n_tp
    answer = pl.pallas_call(
        functools.partial(answer_kernel, scale),
        out_shape=packet,
        in_specs=[SMEM, VMEM, VMEM],
        out_specs=VMEM,
        scratch_shapes=[
            pltpu.VMEM((arrivals, head), f32),
            pltpu.VMEM((arrivals, head), f32),
        ],
        compiler_params=params(16),
        name="answer",
    )(place, asked, sent)
    back = lax.all_to_all(answer, "inst", 0, 0, tiled=True)

    ahead = 5 * TILE
    peak_b, sum_b, acc_b, held = pl.pallas_call(
        functools.partial(second_kernel, scale, group, blocks, half),
        out_shape=(own, own, own, shape((head_width, ahead), bf16)),
        in_specs=[SMEM, VMEM, VMEM, HBM, HBM, pl.BlockSpec(memory_space=pl.ANY)],
        out_specs=(VMEM, VMEM, VMEM, VMEM),
        scratch_shapes=[
            kv_scratch,
            pltpu.SemaphoreType.DMA((half, blocks)),
            pltpu.SemaphoreType.DMA,
        ],
        compiler_params=params(50),
        cost_estimate=own_cost,
        name="own_second",
    )(plan, slot_query, fresh, pool, out_weight, answer)

    out_rows = steps * slots
    partial_out = pl.pallas_call(
        functools.partial(project_kernel, entries),
        out_shape=shape((n_tp, out_rows, part_cols), bf16),
        in_specs=[SMEM] + [VMEM] * 8 + [HBM],
        out_specs=VMEM,
        scratch_shapes=[
            pltpu.VMEM((slots, rows, head), f32),
            pltpu.VMEM((slots, rows, head), f32),
            pltpu.VMEM((slots, rows, head), f32),
            pltpu.VMEM((out_rows, head_width), f32),
            pltpu.VMEM((head_width, columns - ahead), bf16),
            pltpu.SemaphoreType.DMA((n_tp,)),
        ],
        compiler_params=params(44),
        name="project",
    )(place, back, peak_a, sum_a, acc_a, peak_b, sum_b, acc_b, held, out_weight)
    shares = lax.all_to_all(partial_out, "tp", 0, 0, tiled=True)
    total = jnp.sum(shares.astype(f32), axis=0).astype(bf16)
    return total.reshape(steps, slots, columns // n_tp)


def solution(mesh):
    return jax.shard_map(
        shards,
        mesh=mesh,
        in_specs=(
            P(None, "inst", "tp"),
            P(None, "inst", "tp", None),
            P("inst", None, "tp", None),
            P("tp", None),
            P("inst"),
            P("inst"),
            P("inst", None),
            P("inst"),
        ),
        out_specs=P(None, "inst", "tp"),
        check_vma=False,
    )
```

```python
import functools

import jax
import jax.numpy as jnp
from jax import lax
from jax.experimental import pallas as pl
from jax.experimental.pallas import tpu as pltpu
from jax.sharding import PartitionSpec as P

CAP = 2
INFO = 8
MASKED = -1e30
TILE = 256
FRESH = 8

SMEM = pl.BlockSpec(memory_space=pltpu.SMEM)
VMEM = pl.BlockSpec(memory_space=pltpu.VMEM)
HBM = pl.BlockSpec(memory_space=pltpu.HBM)

nt_dims = (((1,), (1,)), ((), ()))


def split_dot(weights, values):
    rows = weights.shape[0]
    high = weights.astype(jnp.bfloat16)
    low = (weights - high.astype(jnp.float32)).astype(jnp.bfloat16)
    both = jnp.dot(
        jnp.concatenate([high, low], axis=0), values, preferred_element_type=jnp.float32
    )
    return both[:rows] + both[rows:]


def ask_kernel(
    pool_size, block_len, table_hbm, len_hbm, block_hbm, dest_hbm, q_hbm, new_hbm,
    out_ref, query_ref, plan_ref,
    table_ref, len_ref, block_ref, dest_ref, code_ref, live_ref, q_ref, new_ref, rows_ref, sems,
):
    slots, blocks = table_ref.shape
    steps = q_ref.shape[0]
    rows, head = query_ref.shape[1] - 2 * FRESH, query_ref.shape[2]
    group = rows // steps
    arrivals = out_ref.shape[0] * CAP
    copies = [
        pltpu.make_async_copy(source, target, sems.at[k])
        for k, (source, target) in enumerate(
            (
                (q_hbm, q_ref),
                (new_hbm, new_ref),
                (table_hbm, table_ref),
                (len_hbm, len_ref),
                (block_hbm, block_ref),
                (dest_hbm, dest_ref),
            )
        )
    ]
    for copy in copies:
        copy.start()
    rows_ref[:, rows:, :] = jnp.zeros((slots, 2 * FRESH, head), jnp.float32)
    for a in range(arrivals):
        code_ref[a] = 0
        live_ref[a] = 0
    for copy in copies:
        copy.wait()
    for step in range(steps):
        query = q_ref[step].astype(jnp.float32)
        for slot in range(slots):
            for g in range(group):
                at = step * group + g
                rows_ref[slot, at : at + 1, :] = query[slot : slot + 1, g * head : (g + 1) * head]
        fresh = new_ref[step].astype(jnp.float32)
        for slot in range(slots):
            for k in range(2):
                at = rows + k * FRESH + step
                rows_ref[slot, at : at + 1, :] = fresh[slot : slot + 1, k * head : (k + 1) * head]
    for slot in range(slots):
        length = len_ref[slot]
        for b in range(blocks):
            block_id = table_ref[slot, b]
            arrival = jnp.where(block_id >= pool_size, block_id - pool_size, arrivals)
            code_ref[arrival] = slot
            live_ref[arrival] = jnp.clip(length - b * block_len, 0, block_len)
            plan_ref[slot * blocks + b] = block_id
    for slot in range(slots):
        query_ref[slot] = rows_ref[slot].astype(jnp.bfloat16)
    row = lax.broadcasted_iota(jnp.int32, (INFO, head), 0)
    for a in range(arrivals):
        source, rank = a // CAP, a % CAP
        out_ref[source, rank * rows : (rank + 1) * rows, :] = query_ref[code_ref[a], :rows, :]
    for source in range(arrivals // CAP):
        live = jnp.where(row < INFO // 2, live_ref[source * CAP], live_ref[source * CAP + 1])
        out_ref[source, CAP * rows :, :] = live.astype(jnp.float32).astype(jnp.bfloat16)
    base = slots * blocks
    for ref in (len_ref, block_ref, dest_ref):
        for k in range(ref.shape[0]):
            plan_ref[base + k] = ref[k]
        base += ref.shape[0]


def own_kernel(
    scale, head_group, blocks, first,
    steps, plan_ref, q_ref, pool_ref,
    peak_ref, sum_ref, acc_ref, kv_ref, sems, bring,
):
    pool_size, block_len, _ = pool_ref.shape
    slots, rows, head = q_ref.shape[0], q_ref.shape[1] - 2 * FRESH, q_ref.shape[2]
    span = blocks * block_len
    len_at = slots * blocks
    mine = range(first, first + peak_ref.shape[0])

    def own_copy(slot, b):
        block_id = jnp.clip(plan_ref[slot * blocks + b], 0, pool_size - 1)
        return pltpu.make_async_copy(
            pool_ref.at[block_id],
            kv_ref.at[slot - first, pl.ds(b * block_len, block_len), :],
            sems.at[slot - first, b],
        )

    for slot in mine:
        for b in range(blocks):
            own_copy(slot, b).start()
    brought = bring()
    lane = lax.broadcasted_iota(jnp.int32, (rows, block_len), 1)
    step = lax.broadcasted_iota(jnp.int32, (rows, block_len), 0) // head_group
    for slot in mine:
        fresh = q_ref[slot, rows:, :].astype(jnp.float32)
        rest = jnp.zeros((block_len - FRESH, head), jnp.float32)
        for k in range(2):
            part = jnp.concatenate([fresh[k * FRESH : (k + 1) * FRESH], rest], axis=0)
            kv_ref[slot - first, span:, k * head : (k + 1) * head] = part.astype(jnp.bfloat16)
    for slot in mine:
        for b in range(blocks):
            own_copy(slot, b).wait()
        scores = lax.dot_general(
            q_ref[slot, :rows, :], kv_ref[slot - first, :, :head], nt_dims, preferred_element_type=jnp.float32
        ) * scale
        parts_s = []
        for b in range(blocks):
            live = jnp.clip(plan_ref[len_at + slot] - b * block_len, 0, block_len)
            live = jnp.where(plan_ref[slot * blocks + b] < pool_size, live, 0)
            part = scores[:, b * block_len : (b + 1) * block_len]
            parts_s.append(jnp.where(lane < live, part, MASKED))
        parts_s.append(jnp.where((lane <= step) & (lane < steps), scores[:, span:], MASKED))
        peak = jnp.max(functools.reduce(jnp.maximum, parts_s), axis=1, keepdims=True)
        weights = [jnp.exp(part - peak) for part in parts_s]
        total = jnp.sum(functools.reduce(jnp.add, weights), axis=1, keepdims=True)
        acc_ref[slot - first] = split_dot(jnp.concatenate(weights, axis=1), kv_ref[slot - first, :, head:])
        same = lane % rows == lax.broadcasted_iota(jnp.int32, (rows, block_len), 0)
        for ref, column in ((peak_ref, peak), (sum_ref, total)):
            across = jnp.sum(jnp.where(same, column, 0.0), axis=0, keepdims=True)
            ref[slot - first] = jnp.broadcast_to(across, ref.shape[1:])
    for copy in brought:
        copy.wait()


def first_kernel(
    scale, head_group, blocks, steps,
    plan_ref, q_ref, pool_ref,
    peak_ref, sum_ref, acc_ref, sent_ref, place_ref,
    seen_ref, kv_ref, sems, sent_sems,
):
    pool_size = pool_ref.shape[0]
    slots = q_ref.shape[0]
    entries = sent_ref.shape[0]
    n_inst = seen_ref.shape[0]
    arrivals = n_inst * CAP
    block_at = slots * blocks + slots
    dest_at = block_at + entries

    def bring():
        copies = []
        for e in range(entries):
            block_id = jnp.clip(plan_ref[block_at + e], 0, pool_size - 1)
            copies.append(
                pltpu.make_async_copy(pool_ref.at[block_id], sent_ref.at[e], sent_sems.at[e])
            )
            copies[e].start()
        for i in range(n_inst):
            seen_ref[i] = 0
        for e in range(entries):
            dest = jnp.clip(plan_ref[dest_at + e], 0, n_inst - 1)
            rank = seen_ref[dest]
            seen_ref[dest] = rank + 1
            place_ref[e] = jnp.minimum(rank, CAP - 1) * n_inst + dest
        for a in range(arrivals):
            place_ref[entries + a] = -1
        for slot in range(slots):
            for b in range(blocks):
                block_id = plan_ref[slot * blocks + b]
                arrival = jnp.where(block_id >= pool_size, block_id - pool_size, arrivals)
                place_ref[entries + arrival] = slot
        return copies

    own_kernel(
        scale, head_group, blocks, 0, steps, plan_ref, q_ref, pool_ref,
        peak_ref, sum_ref, acc_ref, kv_ref, sems, bring,
    )


def second_kernel(
    scale, head_group, blocks, steps, first,
    plan_ref, q_ref, pool_ref, weight_ref, after_ref,
    peak_ref, sum_ref, acc_ref, held_ref,
    kv_ref, sems, weight_sem,
):
    del after_ref

    def bring():
        copy = pltpu.make_async_copy(
            weight_ref.at[:, pl.ds(0, held_ref.shape[1])], held_ref, weight_sem
        )
        copy.start()
        return [copy]

    own_kernel(
        scale, head_group, blocks, first, steps, plan_ref, q_ref, pool_ref,
        peak_ref, sum_ref, acc_ref, kv_ref, sems, bring,
    )


def three_terms(values):
    high = values.astype(jnp.bfloat16).astype(jnp.float32)
    rest = values - high
    middle = rest.astype(jnp.bfloat16).astype(jnp.float32)
    return high, middle, rest - middle


def answer_kernel(
    scale, place_ref, asked_ref, sent_ref, out_ref, peak_ref, sum_ref
):
    entries, block_len, width = sent_ref.shape
    head = width // 2
    n_inst = out_ref.shape[0]
    rows = (out_ref.shape[1] - INFO) // CAP
    out_ref[...] = jnp.zeros_like(out_ref)
    peak_ref[...] = jnp.zeros_like(peak_ref)
    sum_ref[...] = jnp.zeros_like(sum_ref)
    lane = lax.broadcasted_iota(jnp.int32, (rows, block_len), 1)
    row = lax.broadcasted_iota(jnp.int32, (rows, block_len), 0)
    key = lane.astype(jnp.float32)
    places, starts, masks, scores = [], [], [], []
    for e in range(entries):
        place = place_ref[e]
        dest = lax.rem(place, n_inst)
        rank = lax.div(place, n_inst)
        start = pl.multiple_of(rank * rows, rows)
        query = asked_ref[dest, pl.ds(start, rows), :]
        info = asked_ref[dest, CAP * rows :, :].astype(jnp.float32)
        live = jnp.where(rank == 0, info[0:1], info[INFO // 2 : INFO // 2 + 1])
        places.append((place, dest))
        starts.append(start)
        masks.append(key < live)
        scores.append(
            lax.dot_general(
                query, sent_ref[e, :, :head], nt_dims, preferred_element_type=jnp.float32
            )
        )
    peaks, totals, results = [], [], []
    for e in range(entries):
        masked = jnp.where(masks[e], scores[e] * scale, MASKED)
        peak = jnp.max(masked, axis=1, keepdims=True)
        weights = jnp.where(masks[e], jnp.exp(masked - peak), 0.0)
        total = jnp.sum(weights, axis=1, keepdims=True)
        values = split_dot(weights, sent_ref[e, :, head:])
        peaks.append(peak)
        totals.append(total)
        results.append((values / jnp.where(total > 0.0, total, 1.0)).astype(jnp.bfloat16))
    for e in range(entries):
        place, dest = places[e]
        out_ref[dest, pl.ds(starts[e], rows), :] = results[e]
        here = lane == row + starts[e]
        peak_ref[pl.ds(place, 1), :] = jnp.sum(
            jnp.where(here, peaks[e], 0.0), axis=0, keepdims=True
        )
        sum_ref[pl.ds(place, 1), :] = jnp.sum(
            jnp.where(here, totals[e], 0.0), axis=0, keepdims=True
        )
    row = lax.broadcasted_iota(jnp.int32, (INFO, block_len), 0)
    terms = three_terms(peak_ref[:n_inst] + peak_ref[n_inst:])
    terms += three_terms(sum_ref[:n_inst] + sum_ref[n_inst:])
    for i in range(n_inst):
        info = jnp.zeros((INFO, block_len), jnp.float32)
        for k, term in enumerate(terms):
            info = jnp.where(row == k, term[i : i + 1], info)
        out_ref[i, CAP * rows :, :] = info.astype(jnp.bfloat16)


def over_groups(combine, row, size):
    shift = row.shape[1] // 2
    while shift >= size:
        row = combine(row, pltpu.roll(row, shift, axis=1))
        shift //= 2
    return row


def project_kernel(
    first_slot, slot_ref, back_ref, peak_a, sum_a, acc_a, peak_b, sum_b, acc_b,
    held_ref, weight_ref, out_ref, att_ref, w_ref, sems,
):
    half, rows, head = acc_a.shape
    slots = half + acc_b.shape[0]
    n_inst = back_ref.shape[0]
    parts, out_rows, part_cols = out_ref.shape
    held = held_ref.shape[1]
    steps = out_rows // slots
    group = rows // steps
    copies = {}
    for c in range(parts):
        low, high = max(held, c * part_cols), (c + 1) * part_cols
        if low < high:
            copies[c] = pltpu.make_async_copy(
                weight_ref.at[:, pl.ds(low, high - low)],
                w_ref.at[:, pl.ds(low - held, high - low)],
                sems.at[c],
            )
            copies[c].start()
    across = head // rows
    lines = n_inst * CAP // across
    line = lax.broadcasted_iota(jnp.int32, (lines, head), 0)
    lane_group = lax.broadcasted_iota(jnp.int32, (lines, head), 1) // rows
    slot_of = jnp.full((lines, head), -1, jnp.int32)
    for j in range(lines):
        for i in range(across):
            here = (line == j) & (lane_group == i)
            slot_of = jnp.where(here, slot_ref[first_slot + j * across + i], slot_of)
    apart = across // CAP
    peak_rows, sum_rows = [], []
    for s in range(n_inst):
        info = back_ref[s, CAP * rows :, :].astype(jnp.float32)
        peak_rows.append(info[0:1] + info[1:2] + info[2:3])
        sum_rows.append(info[3:4] + info[4:5] + info[5:6])

    def together(per_source):
        total = None
        for k in range(apart):
            part = jnp.concatenate(per_source[k::apart], axis=0)
            if k:
                part = pltpu.roll(part, k * CAP * rows, axis=1)
            total = part if total is None else total + part
        return total

    peaks, sums = together(peak_rows), together(sum_rows)
    peak_own = [peak_a[k] for k in range(half)] + [peak_b[k] for k in range(slots - half)]
    sum_own = [sum_a[k] for k in range(half)] + [sum_b[k] for k in range(slots - half)]
    acc_own = [acc_a[k] for k in range(half)] + [acc_b[k] for k in range(slots - half)]
    best, best_of = [], jnp.zeros((lines, head), jnp.float32)
    for k in range(slots):
        top = jnp.max(jnp.where(slot_of == k, peaks, MASKED), axis=0, keepdims=True)
        best.append(jnp.maximum(over_groups(jnp.maximum, top, rows), peak_own[k]))
        best_of = jnp.where(slot_of == k, best[k], best_of)
    gains = jnp.where(slot_of >= 0, sums * jnp.exp(peaks - best_of), 0.0)
    keeps, matrix = [], []
    same = lax.broadcasted_iota(jnp.int32, (rows, head), 1) % rows == lax.broadcasted_iota(
        jnp.int32, (rows, head), 0
    )
    first_group = lax.broadcasted_iota(jnp.int32, (rows, head), 1) < rows
    for k in range(slots):
        mine = jnp.where(slot_of == k, gains, 0.0)
        keep = jnp.exp(peak_own[k] - best[k])
        total = over_groups(jnp.add, jnp.sum(mine, axis=0, keepdims=True), rows)
        inverse = 1.0 / (total + sum_own[k] * keep)
        keep = (keep * inverse)[0:1]
        keeps.append(
            jnp.sum(jnp.where(same & first_group, keep, 0.0), axis=1, keepdims=True)
        )
        mine = mine * inverse
        matrix.append(
            jnp.concatenate(
                [jnp.where(same, mine[j : j + 1], 0.0) for j in range(lines)], axis=1
            )
        )
    values = back_ref[:, : CAP * rows, :].reshape(n_inst * CAP * rows, head)
    arrived = split_dot(jnp.concatenate(matrix, axis=0), values)
    for slot in range(slots):
        done = keeps[slot] * acc_own[slot] + arrived[slot * rows : (slot + 1) * rows]
        for step in range(steps):
            for g in range(group):
                at = step * group + g
                to = step * slots + slot
                att_ref[to : to + 1, g * head : (g + 1) * head] = done[at : at + 1]
    attended = att_ref[...].astype(jnp.bfloat16)
    for c in range(parts):
        if c in copies:
            copies[c].wait()
        for low in range(c * part_cols, (c + 1) * part_cols, TILE):
            if low < held:
                weight = held_ref[:, low : low + TILE]
            else:
                weight = w_ref[:, low - held : low - held + TILE]
            at = low - c * part_cols
            out_ref[c, :, at : at + TILE] = jnp.dot(
                attended, weight, preferred_element_type=jnp.float32
            ).astype(jnp.bfloat16)


def params(mib):
    return pltpu.CompilerParams(vmem_limit_bytes=mib * 1024 * 1024)


def shards(queries, new_kv, kv_pool, out_weight, send_block, send_dest, block_table, cache_len):
    n_inst = lax.axis_size("inst")
    n_tp = lax.axis_size("tp")
    steps, slots, head_width = queries.shape
    pool_size, block_len, _, width = kv_pool.shape
    head = width // 2
    group = head_width // head
    rows = steps * group
    blocks = block_table.shape[1]
    entries = send_block.shape[0]
    columns = out_weight.shape[1]
    arrivals = n_inst * CAP
    scale = head ** (-0.5)
    f32, bf16, i32 = jnp.float32, jnp.bfloat16, jnp.int32
    shape = jax.ShapeDtypeStruct
    pool = kv_pool.reshape(pool_size, block_len, width)
    fresh = new_kv.reshape(steps, slots, width)

    packet = shape((n_inst, CAP * rows + INFO, head), bf16)
    ask, slot_query, plan = pl.pallas_call(
        functools.partial(ask_kernel, pool_size, block_len),
        out_shape=(
            packet,
            shape((slots, rows + 2 * FRESH, head), bf16),
            shape((slots * blocks + slots + 2 * entries,), i32),
        ),
        in_specs=[HBM] * 6,
        out_specs=(VMEM, VMEM, SMEM),
        scratch_shapes=[
            pltpu.SMEM((slots, blocks), i32),
            pltpu.SMEM((slots,), i32),
            pltpu.SMEM((entries,), i32),
            pltpu.SMEM((entries,), i32),
            pltpu.SMEM((arrivals + 1,), i32),
            pltpu.SMEM((arrivals + 1,), i32),
            pltpu.VMEM(queries.shape, bf16),
            pltpu.VMEM(fresh.shape, bf16),
            pltpu.VMEM((slots, rows + 2 * FRESH, head), f32),
            pltpu.SemaphoreType.DMA((6,)),
        ],
        compiler_params=params(64),
        name="ask",
    )(block_table, cache_len, send_block, send_dest, queries, fresh)
    asked = lax.all_to_all(ask, "inst", 0, 0, tiled=True)

    half = slots // 2
    own = shape((half, rows, head), f32)
    stat = shape((half, 8, head), f32)
    kv_scratch = pltpu.VMEM((half, (blocks + 1) * block_len, width), bf16)
    own_cost = pl.CostEstimate(
        flops=2 * slots * rows * blocks * block_len * width,
        bytes_accessed=4 * slots * blocks * block_len * width,
        transcendentals=half * rows * blocks * block_len,
    )
    peak_a, sum_a, acc_a, sent, place = pl.pallas_call(
        functools.partial(first_kernel, scale, group, blocks, steps),
        out_shape=(
            stat, stat, own,
            shape((entries, block_len, width), bf16),
            shape((entries + arrivals + 1,), i32),
        ),
        in_specs=[SMEM, VMEM, HBM],
        out_specs=(VMEM, VMEM, VMEM, VMEM, SMEM),
        scratch_shapes=[
            pltpu.SMEM((n_inst,), i32),
            kv_scratch,
            pltpu.SemaphoreType.DMA((half, blocks)),
            pltpu.SemaphoreType.DMA((entries,)),
        ],
        compiler_params=params(50),
        cost_estimate=own_cost,
        name="own_first",
    )(plan, slot_query, pool)

    part_cols = columns // n_tp
    answer = pl.pallas_call(
        functools.partial(answer_kernel, scale),
        out_shape=packet,
        in_specs=[SMEM, VMEM, VMEM],
        out_specs=VMEM,
        scratch_shapes=[
            pltpu.VMEM((arrivals, head), f32),
            pltpu.VMEM((arrivals, head), f32),
        ],
        compiler_params=params(16),
        name="answer",
    )(place, asked, sent)
    back = lax.all_to_all(answer, "inst", 0, 0, tiled=True)

    ahead = 5 * TILE
    peak_b, sum_b, acc_b, held = pl.pallas_call(
        functools.partial(second_kernel, scale, group, blocks, steps, half),
        out_shape=(stat, stat, own, shape((head_width, ahead), bf16)),
        in_specs=[SMEM, VMEM, HBM, HBM, pl.BlockSpec(memory_space=pl.ANY)],
        out_specs=(VMEM, VMEM, VMEM, VMEM),
        scratch_shapes=[
            kv_scratch,
            pltpu.SemaphoreType.DMA((half, blocks)),
            pltpu.SemaphoreType.DMA,
        ],
        compiler_params=params(50),
        cost_estimate=own_cost,
        name="own_second",
    )(plan, slot_query, pool, out_weight, answer)

    out_rows = steps * slots
    partial_out = pl.pallas_call(
        functools.partial(project_kernel, entries),
        out_shape=shape((n_tp, out_rows, part_cols), bf16),
        in_specs=[SMEM] + [VMEM] * 8 + [HBM],
        out_specs=VMEM,
        scratch_shapes=[
            pltpu.VMEM((out_rows, head_width), f32),
            pltpu.VMEM((head_width, columns - ahead), bf16),
            pltpu.SemaphoreType.DMA((n_tp,)),
        ],
        compiler_params=params(44),
        name="project",
    )(place, back, peak_a, sum_a, acc_a, peak_b, sum_b, acc_b, held, out_weight)
    shares = lax.all_to_all(partial_out, "tp", 0, 0, tiled=True)
    total = jnp.sum(shares.astype(f32), axis=0).astype(bf16)
    return total.reshape(steps, slots, columns // n_tp)


def solution(mesh):
    return jax.shard_map(
        shards,
        mesh=mesh,
        in_specs=(
            P(None, "inst", "tp"),
            P(None, "inst", "tp", None),
            P("inst", None, "tp", None),
            P("tp", None),
            P("inst"),
            P("inst"),
            P("inst", None),
            P("inst"),
        ),
        out_specs=P(None, "inst", "tp"),
        check_vma=False,
    )
```

```python
import functools

import jax
import jax.numpy as jnp
from jax import lax
from jax.experimental import pallas as pl
from jax.experimental.pallas import tpu as pltpu
from jax.sharding import PartitionSpec as P

CAP = 2
INFO = 8
MASKED = -1e30
TILE = 256
FRESH = 8
PLAN_ROW = 4
LENGTH_BASE = 64

VMEM = pl.BlockSpec(memory_space=pltpu.VMEM)
HBM = pl.BlockSpec(memory_space=pltpu.HBM)
ANY = pl.BlockSpec(memory_space=pl.ANY)

nt_dims = (((1,), (1,)), ((), ()))


def split_dot(weights, values):
    rows = weights.shape[0]
    high = weights.astype(jnp.bfloat16)
    low = (weights - high.astype(jnp.float32)).astype(jnp.bfloat16)
    both = jnp.dot(
        jnp.concatenate([high, low], axis=0), values, preferred_element_type=jnp.float32
    )
    return both[:rows] + both[rows:]


def ask_kernel(
    pool_size, block_len, table_hbm, len_hbm, block_hbm, dest_hbm, q_hbm, new_hbm,
    out_ref, query_ref,
    table_ref, len_ref, block_ref, dest_ref, code_ref, live_ref, q_ref, new_ref, rows_ref, sems,
):
    slots, blocks = table_ref.shape
    steps = q_ref.shape[0]
    rows, head = query_ref.shape[1] - 2 * FRESH, query_ref.shape[2]
    group = rows // steps
    arrivals = out_ref.shape[0] * CAP
    copies = [
        pltpu.make_async_copy(source, target, sems.at[k])
        for k, (source, target) in enumerate(
            (
                (q_hbm, q_ref),
                (new_hbm, new_ref),
                (table_hbm, table_ref),
                (len_hbm, len_ref),
                (block_hbm, block_ref),
                (dest_hbm, dest_ref),
            )
        )
    ]
    for copy in copies:
        copy.start()
    rows_ref[:, rows:, :] = jnp.zeros((slots, 2 * FRESH, head), jnp.float32)
    for a in range(arrivals):
        code_ref[a] = 0
        live_ref[a] = 0
    for copy in copies:
        copy.wait()
    for step in range(steps):
        query = q_ref[step].astype(jnp.float32)
        for slot in range(slots):
            for g in range(group):
                at = step * group + g
                rows_ref[slot, at : at + 1, :] = query[slot : slot + 1, g * head : (g + 1) * head]
        fresh = new_ref[step].astype(jnp.float32)
        for slot in range(slots):
            for k in range(2):
                at = rows + k * FRESH + step
                rows_ref[slot, at : at + 1, :] = fresh[slot : slot + 1, k * head : (k + 1) * head]
    plan = []
    for slot in range(slots):
        length = len_ref[slot]
        for b in range(blocks):
            block_id = table_ref[slot, b]
            arrival = jnp.where(block_id >= pool_size, block_id - pool_size, arrivals)
            code_ref[arrival] = slot
            live_ref[arrival] = jnp.clip(length - b * block_len, 0, block_len)
            plan.append(block_id)
    plan += [len_ref[slot] // LENGTH_BASE for slot in range(slots)]
    plan += [len_ref[slot] % LENGTH_BASE for slot in range(slots)]
    plan += [block_ref[e] for e in range(block_ref.shape[0])]
    plan += [dest_ref[e] for e in range(dest_ref.shape[0])]
    lane = lax.broadcasted_iota(jnp.int32, (1, head), 1)
    line = jnp.zeros((1, head), jnp.int32)
    for k, number in enumerate(plan):
        line = jnp.where(lane == k, number, line)
    rows_ref[0, rows + PLAN_ROW : rows + PLAN_ROW + 1, :] = line.astype(jnp.float32)
    for slot in range(slots):
        query_ref[slot] = rows_ref[slot].astype(jnp.bfloat16)
    row = lax.broadcasted_iota(jnp.int32, (INFO, head), 0)
    for a in range(arrivals):
        source, rank = a // CAP, a % CAP
        out_ref[source, rank * rows : (rank + 1) * rows, :] = query_ref[code_ref[a], :rows, :]
    for source in range(arrivals // CAP):
        live = jnp.where(row < INFO // 2, live_ref[source * CAP], live_ref[source * CAP + 1])
        out_ref[source, CAP * rows :, :] = live.astype(jnp.float32).astype(jnp.bfloat16)


class Plan:
    def __init__(self, q_ref, blocks, entries):
        slots, rows = q_ref.shape[0], q_ref.shape[1] - 2 * FRESH
        row = q_ref[0, rows:, :].astype(jnp.float32)[PLAN_ROW : PLAN_ROW + 1].astype(jnp.int32)
        numbers = [row[0, k] for k in range(slots * (blocks + 2) + 2 * entries)]
        at = slots * blocks
        self.table = [numbers[slot * blocks : (slot + 1) * blocks] for slot in range(slots)]
        self.length = [
            numbers[at + slot] * LENGTH_BASE + numbers[at + slots + slot] for slot in range(slots)
        ]
        at += 2 * slots
        self.block, self.dest = numbers[at : at + entries], numbers[at + entries :]


def own_kernel(
    scale, head_group, blocks, first,
    steps, plan, q_ref, pool_ref,
    peak_ref, sum_ref, acc_ref, kv_ref, sems, bring,
):
    pool_size, block_len, _ = pool_ref.shape
    slots, rows, head = q_ref.shape[0], q_ref.shape[1] - 2 * FRESH, q_ref.shape[2]
    span = blocks * block_len
    mine = range(first, first + peak_ref.shape[0])

    def own_copy(slot, b):
        block_id = jnp.clip(plan.table[slot][b], 0, pool_size - 1)
        return pltpu.make_async_copy(
            pool_ref.at[block_id],
            kv_ref.at[slot - first, pl.ds(b * block_len, block_len), :],
            sems.at[slot - first, b],
        )

    for slot in mine:
        for b in range(blocks):
            own_copy(slot, b).start()
    brought = bring()
    lane = lax.broadcasted_iota(jnp.int32, (rows, block_len), 1)
    step = lax.broadcasted_iota(jnp.int32, (rows, block_len), 0) // head_group
    for slot in mine:
        fresh = q_ref[slot, rows:, :].astype(jnp.float32)
        rest = jnp.zeros((block_len - FRESH, head), jnp.float32)
        for k in range(2):
            part = jnp.concatenate([fresh[k * FRESH : (k + 1) * FRESH], rest], axis=0)
            kv_ref[slot - first, span:, k * head : (k + 1) * head] = part.astype(jnp.bfloat16)
    for slot in mine:
        for b in range(blocks):
            own_copy(slot, b).wait()
        scores = lax.dot_general(
            q_ref[slot, :rows, :], kv_ref[slot - first, :, :head], nt_dims, preferred_element_type=jnp.float32
        ) * scale
        parts_s = []
        for b in range(blocks):
            live = jnp.clip(plan.length[slot] - b * block_len, 0, block_len)
            live = jnp.where(plan.table[slot][b] < pool_size, live, 0)
            part = scores[:, b * block_len : (b + 1) * block_len]
            parts_s.append(jnp.where(lane < live, part, MASKED))
        parts_s.append(jnp.where((lane <= step) & (lane < steps), scores[:, span:], MASKED))
        peak = jnp.max(functools.reduce(jnp.maximum, parts_s), axis=1, keepdims=True)
        weights = [jnp.exp(part - peak) for part in parts_s]
        total = jnp.sum(functools.reduce(jnp.add, weights), axis=1, keepdims=True)
        acc_ref[slot - first] = split_dot(jnp.concatenate(weights, axis=1), kv_ref[slot - first, :, head:])
        same = lane % rows == lax.broadcasted_iota(jnp.int32, (rows, block_len), 0)
        for ref, column in ((peak_ref, peak), (sum_ref, total)):
            across = jnp.sum(jnp.where(same, column, 0.0), axis=0, keepdims=True)
            ref[slot - first] = jnp.broadcast_to(across, ref.shape[1:])
    for copy in brought:
        copy.wait()


def first_kernel(
    scale, head_group, blocks, steps, n_inst,
    q_ref, pool_ref,
    peak_ref, sum_ref, acc_ref, sent_ref, place_ref, slot_ref,
    kv_ref, sems, sent_sems,
):
    pool_size = pool_ref.shape[0]
    slots, rows, head = q_ref.shape[0], q_ref.shape[1] - 2 * FRESH, q_ref.shape[2]
    entries = sent_ref.shape[0]
    plan = Plan(q_ref, blocks, entries)

    def bring():
        copies = []
        for e in range(entries):
            block_id = jnp.clip(plan.block[e], 0, pool_size - 1)
            copies.append(
                pltpu.make_async_copy(pool_ref.at[block_id], sent_ref.at[e], sent_sems.at[e])
            )
            copies[e].start()
        lane = lax.broadcasted_iota(jnp.int32, place_ref.shape, 1)
        places = jnp.zeros(place_ref.shape, jnp.int32)
        for e in range(entries):
            dest = jnp.clip(plan.dest[e], 0, n_inst - 1)
            rank = sum((plan.dest[f] == plan.dest[e]).astype(jnp.int32) for f in range(e))
            place = jnp.minimum(rank, CAP - 1) * n_inst + dest
            places = jnp.where(lane == e, place, places)
        place_ref[...] = places
        line = lax.broadcasted_iota(jnp.int32, slot_ref.shape, 0)
        arrival = line * (head // rows) + lax.broadcasted_iota(jnp.int32, slot_ref.shape, 1) // rows
        slot_of = jnp.full(slot_ref.shape, -1, jnp.int32)
        for slot in range(slots):
            for b in range(blocks):
                slot_of = jnp.where(arrival == plan.table[slot][b] - pool_size, slot, slot_of)
        slot_ref[...] = slot_of
        return copies

    own_kernel(
        scale, head_group, blocks, 0, steps, plan, q_ref, pool_ref,
        peak_ref, sum_ref, acc_ref, kv_ref, sems, bring,
    )


def second_kernel(
    scale, head_group, blocks, steps, entries, first,
    q_ref, pool_ref, weight_ref, after_ref,
    peak_ref, sum_ref, acc_ref, held_ref,
    kv_ref, sems, weight_sem,
):
    del after_ref

    def bring():
        copy = pltpu.make_async_copy(
            weight_ref.at[:, pl.ds(0, held_ref.shape[1])], held_ref, weight_sem
        )
        copy.start()
        return [copy]

    own_kernel(
        scale, head_group, blocks, first, steps, Plan(q_ref, blocks, entries), q_ref, pool_ref,
        peak_ref, sum_ref, acc_ref, kv_ref, sems, bring,
    )


def three_terms(values):
    high = values.astype(jnp.bfloat16).astype(jnp.float32)
    rest = values - high
    middle = rest.astype(jnp.bfloat16).astype(jnp.float32)
    return high, middle, rest - middle


def answer_kernel(
    scale, place_ref, asked_ref, sent_ref, out_ref, peak_ref, sum_ref
):
    entries, block_len, width = sent_ref.shape
    head = width // 2
    n_inst = out_ref.shape[0]
    rows = (out_ref.shape[1] - INFO) // CAP
    out_ref[...] = jnp.zeros_like(out_ref)
    peak_ref[...] = jnp.zeros_like(peak_ref)
    sum_ref[...] = jnp.zeros_like(sum_ref)
    lane = lax.broadcasted_iota(jnp.int32, (rows, block_len), 1)
    row = lax.broadcasted_iota(jnp.int32, (rows, block_len), 0)
    key = lane.astype(jnp.float32)
    places, starts, masks, scores = [], [], [], []
    across = place_ref[...]
    for e in range(entries):
        place = across[0, e]
        dest = lax.rem(place, n_inst)
        rank = lax.div(place, n_inst)
        start = pl.multiple_of(rank * rows, rows)
        query = asked_ref[dest, pl.ds(start, rows), :]
        info = asked_ref[dest, CAP * rows :, :].astype(jnp.float32)
        live = jnp.where(rank == 0, info[0:1], info[INFO // 2 : INFO // 2 + 1])
        places.append((place, dest))
        starts.append(start)
        masks.append(key < live)
        scores.append(
            lax.dot_general(
                query, sent_ref[e, :, :head], nt_dims, preferred_element_type=jnp.float32
            )
        )
    peaks, totals, results = [], [], []
    for e in range(entries):
        masked = jnp.where(masks[e], scores[e] * scale, MASKED)
        peak = jnp.max(masked, axis=1, keepdims=True)
        weights = jnp.where(masks[e], jnp.exp(masked - peak), 0.0)
        total = jnp.sum(weights, axis=1, keepdims=True)
        values = split_dot(weights, sent_ref[e, :, head:])
        peaks.append(peak)
        totals.append(total)
        results.append((values / jnp.where(total > 0.0, total, 1.0)).astype(jnp.bfloat16))
    for e in range(entries):
        place, dest = places[e]
        out_ref[dest, pl.ds(starts[e], rows), :] = results[e]
        here = lane == row + starts[e]
        peak_ref[pl.ds(place, 1), :] = jnp.sum(
            jnp.where(here, peaks[e], 0.0), axis=0, keepdims=True
        )
        sum_ref[pl.ds(place, 1), :] = jnp.sum(
            jnp.where(here, totals[e], 0.0), axis=0, keepdims=True
        )
    row = lax.broadcasted_iota(jnp.int32, (INFO, block_len), 0)
    terms = three_terms(peak_ref[:n_inst] + peak_ref[n_inst:])
    terms += three_terms(sum_ref[:n_inst] + sum_ref[n_inst:])
    for i in range(n_inst):
        info = jnp.zeros((INFO, block_len), jnp.float32)
        for k, term in enumerate(terms):
            info = jnp.where(row == k, term[i : i + 1], info)
        out_ref[i, CAP * rows :, :] = info.astype(jnp.bfloat16)


def over_groups(combine, row, size):
    shift = row.shape[1] // 2
    while shift >= size:
        row = combine(row, pltpu.roll(row, shift, axis=1))
        shift //= 2
    return row


def project_kernel(
    slot_ref, back_ref, peak_a, sum_a, acc_a, peak_b, sum_b, acc_b,
    held_ref, weight_ref, out_ref, att_ref, w_ref, sems,
):
    half, rows, head = acc_a.shape
    slots = half + acc_b.shape[0]
    n_inst = back_ref.shape[0]
    parts, out_rows, part_cols = out_ref.shape
    held = held_ref.shape[1]
    steps = out_rows // slots
    group = rows // steps
    copies = {}
    for c in range(parts):
        low, high = max(held, c * part_cols), (c + 1) * part_cols
        if low < high:
            copies[c] = pltpu.make_async_copy(
                weight_ref.at[:, pl.ds(low, high - low)],
                w_ref.at[:, pl.ds(low - held, high - low)],
                sems.at[c],
            )
            copies[c].start()
    across = head // rows
    slot_of = slot_ref[...]
    lines = slot_of.shape[0]
    apart = across // CAP
    peak_rows, sum_rows = [], []
    for s in range(n_inst):
        info = back_ref[s, CAP * rows :, :].astype(jnp.float32)
        peak_rows.append(info[0:1] + info[1:2] + info[2:3])
        sum_rows.append(info[3:4] + info[4:5] + info[5:6])

    def together(per_source):
        total = None
        for k in range(apart):
            part = jnp.concatenate(per_source[k::apart], axis=0)
            if k:
                part = pltpu.roll(part, k * CAP * rows, axis=1)
            total = part if total is None else total + part
        return total

    peaks, sums = together(peak_rows), together(sum_rows)
    peak_own = [peak_a[k] for k in range(half)] + [peak_b[k] for k in range(slots - half)]
    sum_own = [sum_a[k] for k in range(half)] + [sum_b[k] for k in range(slots - half)]
    acc_own = [acc_a[k] for k in range(half)] + [acc_b[k] for k in range(slots - half)]
    best, best_of = [], jnp.zeros((lines, head), jnp.float32)
    for k in range(slots):
        top = jnp.max(jnp.where(slot_of == k, peaks, MASKED), axis=0, keepdims=True)
        best.append(jnp.maximum(over_groups(jnp.maximum, top, rows), peak_own[k]))
        best_of = jnp.where(slot_of == k, best[k], best_of)
    gains = jnp.where(slot_of >= 0, sums * jnp.exp(peaks - best_of), 0.0)
    keeps, matrix = [], []
    same = lax.broadcasted_iota(jnp.int32, (rows, head), 1) % rows == lax.broadcasted_iota(
        jnp.int32, (rows, head), 0
    )
    first_group = lax.broadcasted_iota(jnp.int32, (rows, head), 1) < rows
    for k in range(slots):
        mine = jnp.where(slot_of == k, gains, 0.0)
        keep = jnp.exp(peak_own[k] - best[k])
        total = over_groups(jnp.add, jnp.sum(mine, axis=0, keepdims=True), rows)
        inverse = 1.0 / (total + sum_own[k] * keep)
        keep = (keep * inverse)[0:1]
        keeps.append(
            jnp.sum(jnp.where(same & first_group, keep, 0.0), axis=1, keepdims=True)
        )
        mine = mine * inverse
        matrix.append(
            jnp.concatenate(
                [jnp.where(same, mine[j : j + 1], 0.0) for j in range(lines)], axis=1
            )
        )
    values = back_ref[:, : CAP * rows, :].reshape(n_inst * CAP * rows, head)
    arrived = split_dot(jnp.concatenate(matrix, axis=0), values)
    for slot in range(slots):
        done = keeps[slot] * acc_own[slot] + arrived[slot * rows : (slot + 1) * rows]
        for step in range(steps):
            for g in range(group):
                at = step * group + g
                to = step * slots + slot
                att_ref[to : to + 1, g * head : (g + 1) * head] = done[at : at + 1]
    attended = att_ref[...].astype(jnp.bfloat16)
    for c in range(parts):
        if c in copies:
            copies[c].wait()
        for low in range(c * part_cols, (c + 1) * part_cols, TILE):
            if low < held:
                weight = held_ref[:, low : low + TILE]
            else:
                weight = w_ref[:, low - held : low - held + TILE]
            at = low - c * part_cols
            out_ref[c, :, at : at + TILE] = jnp.dot(
                attended, weight, preferred_element_type=jnp.float32
            ).astype(jnp.bfloat16)


def params(mib):
    return pltpu.CompilerParams(vmem_limit_bytes=mib * 1024 * 1024)


def shards(queries, new_kv, kv_pool, out_weight, send_block, send_dest, block_table, cache_len):
    n_inst = lax.axis_size("inst")
    n_tp = lax.axis_size("tp")
    steps, slots, head_width = queries.shape
    pool_size, block_len, _, width = kv_pool.shape
    head = width // 2
    group = head_width // head
    rows = steps * group
    blocks = block_table.shape[1]
    entries = send_block.shape[0]
    columns = out_weight.shape[1]
    arrivals = n_inst * CAP
    scale = head ** (-0.5)
    f32, bf16, i32 = jnp.float32, jnp.bfloat16, jnp.int32
    shape = jax.ShapeDtypeStruct
    pool = kv_pool.reshape(pool_size, block_len, width)
    fresh = new_kv.reshape(steps, slots, width)

    packet = shape((n_inst, CAP * rows + INFO, head), bf16)
    ask, slot_query = pl.pallas_call(
        functools.partial(ask_kernel, pool_size, block_len),
        out_shape=(
            packet,
            shape((slots, rows + 2 * FRESH, head), bf16),
        ),
        in_specs=[HBM] * 6,
        out_specs=(VMEM, VMEM),
        scratch_shapes=[
            pltpu.SMEM((slots, blocks), i32),
            pltpu.SMEM((slots,), i32),
            pltpu.SMEM((entries,), i32),
            pltpu.SMEM((entries,), i32),
            pltpu.SMEM((arrivals + 1,), i32),
            pltpu.SMEM((arrivals + 1,), i32),
            pltpu.VMEM(queries.shape, bf16),
            pltpu.VMEM(fresh.shape, bf16),
            pltpu.VMEM((slots, rows + 2 * FRESH, head), f32),
            pltpu.SemaphoreType.DMA((6,)),
        ],
        compiler_params=params(64),
        name="ask",
    )(block_table, cache_len, send_block, send_dest, queries, fresh)
    asked = lax.all_to_all(ask, "inst", 0, 0, tiled=True)

    half = slots // 2
    own = shape((half, rows, head), f32)
    stat = shape((half, 8, head), f32)
    kv_scratch = pltpu.VMEM((half, (blocks + 1) * block_len, width), bf16)
    own_cost = pl.CostEstimate(
        flops=2 * slots * rows * blocks * block_len * width,
        bytes_accessed=4 * slots * blocks * block_len * width,
        transcendentals=half * rows * blocks * block_len,
    )
    peak_a, sum_a, acc_a, sent, place, slot_of = pl.pallas_call(
        functools.partial(first_kernel, scale, group, blocks, steps, n_inst),
        out_shape=(
            stat, stat, own,
            shape((entries, block_len, width), bf16),
            shape((8, head), i32),
            shape((arrivals * rows // head, head), i32),
        ),
        in_specs=[VMEM, HBM],
        out_specs=(VMEM,) * 6,
        scratch_shapes=[
            kv_scratch,
            pltpu.SemaphoreType.DMA((half, blocks)),
            pltpu.SemaphoreType.DMA((entries,)),
        ],
        compiler_params=params(50),
        cost_estimate=own_cost,
        name="own_first",
    )(slot_query, pool)

    part_cols = columns // n_tp
    answer = pl.pallas_call(
        functools.partial(answer_kernel, scale),
        out_shape=packet,
        in_specs=[VMEM, VMEM, VMEM],
        out_specs=VMEM,
        scratch_shapes=[
            pltpu.VMEM((arrivals, head), f32),
            pltpu.VMEM((arrivals, head), f32),
        ],
        compiler_params=params(16),
        name="answer",
    )(place, asked, sent)
    back = lax.all_to_all(answer, "inst", 0, 0, tiled=True)

    ahead = 5 * TILE
    peak_b, sum_b, acc_b, held = pl.pallas_call(
        functools.partial(second_kernel, scale, group, blocks, steps, entries, half),
        out_shape=(stat, stat, own, shape((head_width, ahead), bf16)),
        in_specs=[VMEM, HBM, HBM, ANY],
        out_specs=(VMEM, VMEM, VMEM, VMEM),
        scratch_shapes=[
            kv_scratch,
            pltpu.SemaphoreType.DMA((half, blocks)),
            pltpu.SemaphoreType.DMA,
        ],
        compiler_params=params(50),
        cost_estimate=own_cost,
        name="own_second",
    )(slot_query, pool, out_weight, answer)

    out_rows = steps * slots
    partial_out = pl.pallas_call(
        project_kernel,
        out_shape=shape((n_tp, out_rows, part_cols), bf16),
        in_specs=[VMEM] * 9 + [HBM],
        out_specs=VMEM,
        scratch_shapes=[
            pltpu.VMEM((out_rows, head_width), f32),
            pltpu.VMEM((head_width, columns - ahead), bf16),
            pltpu.SemaphoreType.DMA((n_tp,)),
        ],
        compiler_params=params(44),
        name="project",
    )(slot_of, back, peak_a, sum_a, acc_a, peak_b, sum_b, acc_b, held, out_weight)
    shares = lax.all_to_all(partial_out, "tp", 0, 0, tiled=True)
    total = jnp.sum(shares.astype(f32), axis=0).astype(bf16)
    return total.reshape(steps, slots, columns // n_tp)


def solution(mesh):
    return jax.shard_map(
        shards,
        mesh=mesh,
        in_specs=(
            P(None, "inst", "tp"),
            P(None, "inst", "tp", None),
            P("inst", None, "tp", None),
            P("tp", None),
            P("inst"),
            P("inst"),
            P("inst", None),
            P("inst"),
        ),
        out_specs=P(None, "inst", "tp"),
        check_vma=False,
    )
```

```python
import functools

import jax
import jax.numpy as jnp
from jax import lax
from jax.experimental import pallas as pl
from jax.experimental.pallas import tpu as pltpu
from jax.sharding import PartitionSpec as P

CAP = 2
INFO = 8
MASKED = -1e30
TILE = 256
AHEAD = 4
FRESH = 8
PLAN_ROW = 4
LENGTH_BASE = 64

VMEM = pl.BlockSpec(memory_space=pltpu.VMEM)
HBM = pl.BlockSpec(memory_space=pltpu.HBM)

nt_dims = (((1,), (1,)), ((), ()))


def split_dot(weights, values):
    rows = weights.shape[0]
    high = weights.astype(jnp.bfloat16)
    low = (weights - high.astype(jnp.float32)).astype(jnp.bfloat16)
    both = jnp.dot(
        jnp.concatenate([high, low], axis=0), values, preferred_element_type=jnp.float32
    )
    return both[:rows] + both[rows:]


def ask_kernel(
    pool_size, block_len, table_hbm, len_hbm, block_hbm, dest_hbm, q_hbm, new_hbm,
    out_ref, query_ref,
    table_ref, len_ref, block_ref, dest_ref, code_ref, live_ref, q_ref, new_ref, rows_ref, sems,
):
    slots, blocks = table_ref.shape
    steps = q_ref.shape[0]
    rows, head = query_ref.shape[1] - 2 * FRESH, query_ref.shape[2]
    group = rows // steps
    arrivals = out_ref.shape[0] * CAP
    copies = [
        pltpu.make_async_copy(source, target, sems.at[k])
        for k, (source, target) in enumerate(
            (
                (q_hbm, q_ref),
                (new_hbm, new_ref),
                (table_hbm, table_ref),
                (len_hbm, len_ref),
                (block_hbm, block_ref),
                (dest_hbm, dest_ref),
            )
        )
    ]
    for copy in copies:
        copy.start()
    rows_ref[:, rows:, :] = jnp.zeros((slots, 2 * FRESH, head), jnp.float32)
    for a in range(arrivals):
        code_ref[a] = 0
        live_ref[a] = 0
    for copy in copies:
        copy.wait()
    for step in range(steps):
        query = q_ref[step].astype(jnp.float32)
        for slot in range(slots):
            for g in range(group):
                at = step * group + g
                rows_ref[slot, at : at + 1, :] = query[slot : slot + 1, g * head : (g + 1) * head]
        fresh = new_ref[step].astype(jnp.float32)
        for slot in range(slots):
            for k in range(2):
                at = rows + k * FRESH + step
                rows_ref[slot, at : at + 1, :] = fresh[slot : slot + 1, k * head : (k + 1) * head]
    plan = []
    for slot in range(slots):
        length = len_ref[slot]
        for b in range(blocks):
            block_id = table_ref[slot, b]
            arrival = jnp.where(block_id >= pool_size, block_id - pool_size, arrivals)
            code_ref[arrival] = slot
            live_ref[arrival] = jnp.clip(length - b * block_len, 0, block_len)
            plan.append(block_id)
    plan += [len_ref[slot] // LENGTH_BASE for slot in range(slots)]
    plan += [len_ref[slot] % LENGTH_BASE for slot in range(slots)]
    plan += [block_ref[e] for e in range(block_ref.shape[0])]
    plan += [dest_ref[e] for e in range(dest_ref.shape[0])]
    lane = lax.broadcasted_iota(jnp.int32, (1, head), 1)
    line = jnp.zeros((1, head), jnp.int32)
    for k, number in enumerate(plan):
        line = jnp.where(lane == k, number, line)
    rows_ref[0, rows + PLAN_ROW : rows + PLAN_ROW + 1, :] = line.astype(jnp.float32)
    for slot in range(slots):
        query_ref[slot] = rows_ref[slot].astype(jnp.bfloat16)
    row = lax.broadcasted_iota(jnp.int32, (INFO, head), 0)
    for a in range(arrivals):
        source, rank = a // CAP, a % CAP
        out_ref[source, rank * rows : (rank + 1) * rows, :] = query_ref[code_ref[a], :rows, :]
    for source in range(arrivals // CAP):
        live = jnp.where(row < INFO // 2, live_ref[source * CAP], live_ref[source * CAP + 1])
        out_ref[source, CAP * rows :, :] = live.astype(jnp.float32).astype(jnp.bfloat16)


class Plan:
    def __init__(self, q_ref, blocks, entries):
        slots, rows = q_ref.shape[0], q_ref.shape[1] - 2 * FRESH
        row = q_ref[0, rows:, :].astype(jnp.float32)[PLAN_ROW : PLAN_ROW + 1].astype(jnp.int32)
        numbers = [row[0, k] for k in range(slots * (blocks + 2) + 2 * entries)]
        at = slots * blocks
        self.table = [numbers[slot * blocks : (slot + 1) * blocks] for slot in range(slots)]
        self.length = [
            numbers[at + slot] * LENGTH_BASE + numbers[at + slots + slot] for slot in range(slots)
        ]
        at += 2 * slots
        self.block, self.dest = numbers[at : at + entries], numbers[at + entries :]


def own_kernel(
    scale, head_group, blocks, first,
    steps, plan, q_ref, pool_ref,
    peak_ref, sum_ref, acc_ref, kv_ref, sems, bring,
):
    pool_size, block_len, _ = pool_ref.shape
    slots, rows, head = q_ref.shape[0], q_ref.shape[1] - 2 * FRESH, q_ref.shape[2]
    span = blocks * block_len
    mine = range(first, first + peak_ref.shape[0])

    def own_copy(slot, b):
        block_id = jnp.clip(plan.table[slot][b], 0, pool_size - 1)
        return pltpu.make_async_copy(
            pool_ref.at[block_id],
            kv_ref.at[slot - first, pl.ds(b * block_len, block_len), :],
            sems.at[slot - first, b],
        )

    for slot in mine:
        for b in range(blocks):
            own_copy(slot, b).start()
    brought = bring()
    lane = lax.broadcasted_iota(jnp.int32, (rows, block_len), 1)
    step = lax.broadcasted_iota(jnp.int32, (rows, block_len), 0) // head_group
    for slot in mine:
        fresh = q_ref[slot, rows:, :].astype(jnp.float32)
        rest = jnp.zeros((block_len - FRESH, head), jnp.float32)
        for k in range(2):
            part = jnp.concatenate([fresh[k * FRESH : (k + 1) * FRESH], rest], axis=0)
            kv_ref[slot - first, span:, k * head : (k + 1) * head] = part.astype(jnp.bfloat16)
    for slot in mine:
        for b in range(blocks):
            own_copy(slot, b).wait()
        scores = lax.dot_general(
            q_ref[slot, :rows, :], kv_ref[slot - first, :, :head], nt_dims, preferred_element_type=jnp.float32
        ) * scale
        parts_s = []
        for b in range(blocks):
            live = jnp.clip(plan.length[slot] - b * block_len, 0, block_len)
            live = jnp.where(plan.table[slot][b] < pool_size, live, 0)
            part = scores[:, b * block_len : (b + 1) * block_len]
            parts_s.append(jnp.where(lane < live, part, MASKED))
        parts_s.append(jnp.where((lane <= step) & (lane < steps), scores[:, span:], MASKED))
        peak = jnp.max(functools.reduce(jnp.maximum, parts_s), axis=1, keepdims=True)
        weights = [jnp.exp(part - peak) for part in parts_s]
        total = jnp.sum(functools.reduce(jnp.add, weights), axis=1, keepdims=True)
        acc_ref[slot - first] = split_dot(jnp.concatenate(weights, axis=1), kv_ref[slot - first, :, head:])
        same = lane % rows == lax.broadcasted_iota(jnp.int32, (rows, block_len), 0)
        for ref, column in ((peak_ref, peak), (sum_ref, total)):
            across = jnp.sum(jnp.where(same, column, 0.0), axis=0, keepdims=True)
            ref[slot - first] = jnp.broadcast_to(across, ref.shape[1:])
    for copy in brought:
        copy.wait()


def bring_kernel(
    scale, head_group, blocks, steps, n_inst,
    q_ref, pool_ref, weight_ref,
    peak_ref, sum_ref, acc_ref, sent_ref, held_ref, place_ref, slot_ref,
    kv_ref, sems, sent_sems, held_sem,
):
    pool_size = pool_ref.shape[0]
    slots, rows, head = q_ref.shape[0], q_ref.shape[1] - 2 * FRESH, q_ref.shape[2]
    entries = sent_ref.shape[0]
    plan = Plan(q_ref, blocks, entries)

    def bring():
        copies = []
        for e in range(entries):
            block_id = jnp.clip(plan.block[e], 0, pool_size - 1)
            copies.append(
                pltpu.make_async_copy(pool_ref.at[block_id], sent_ref.at[e], sent_sems.at[e])
            )
            copies[e].start()
        held_copy = pltpu.make_async_copy(
            weight_ref.at[:, pl.ds(0, held_ref.shape[1])], held_ref, held_sem
        )
        held_copy.start()
        copies.append(held_copy)
        lane = lax.broadcasted_iota(jnp.int32, place_ref.shape, 1)
        places = jnp.zeros(place_ref.shape, jnp.int32)
        for e in range(entries):
            dest = jnp.clip(plan.dest[e], 0, n_inst - 1)
            rank = sum((plan.dest[f] == plan.dest[e]).astype(jnp.int32) for f in range(e))
            place = jnp.minimum(rank, CAP - 1) * n_inst + dest
            places = jnp.where(lane == e, place, places)
        place_ref[...] = places
        line = lax.broadcasted_iota(jnp.int32, slot_ref.shape, 0)
        arrival = line * (head // rows) + lax.broadcasted_iota(jnp.int32, slot_ref.shape, 1) // rows
        slot_of = jnp.full(slot_ref.shape, -1, jnp.int32)
        for slot in range(slots):
            for b in range(blocks):
                slot_of = jnp.where(arrival == plan.table[slot][b] - pool_size, slot, slot_of)
        slot_ref[...] = slot_of
        return copies

    own_kernel(
        scale, head_group, blocks, 0, steps, plan, q_ref, pool_ref,
        peak_ref, sum_ref, acc_ref, kv_ref, sems, bring,
    )


def three_terms(values):
    high = values.astype(jnp.bfloat16).astype(jnp.float32)
    rest = values - high
    middle = rest.astype(jnp.bfloat16).astype(jnp.float32)
    return high, middle, rest - middle


def answer_kernel(
    scale, place_ref, asked_ref, sent_ref, out_ref, peak_ref, sum_ref
):
    entries, block_len, width = sent_ref.shape
    head = width // 2
    n_inst = out_ref.shape[0]
    rows = (out_ref.shape[1] - INFO) // CAP
    out_ref[...] = jnp.zeros_like(out_ref)
    peak_ref[...] = jnp.zeros_like(peak_ref)
    sum_ref[...] = jnp.zeros_like(sum_ref)
    lane = lax.broadcasted_iota(jnp.int32, (rows, block_len), 1)
    row = lax.broadcasted_iota(jnp.int32, (rows, block_len), 0)
    key = lane.astype(jnp.float32)
    places, starts, masks, scores = [], [], [], []
    across = place_ref[...]
    for e in range(entries):
        place = across[0, e]
        dest = lax.rem(place, n_inst)
        rank = lax.div(place, n_inst)
        start = pl.multiple_of(rank * rows, rows)
        query = asked_ref[dest, pl.ds(start, rows), :]
        info = asked_ref[dest, CAP * rows :, :].astype(jnp.float32)
        live = jnp.where(rank == 0, info[0:1], info[INFO // 2 : INFO // 2 + 1])
        places.append((place, dest))
        starts.append(start)
        masks.append(key < live)
        scores.append(
            lax.dot_general(
                query, sent_ref[e, :, :head], nt_dims, preferred_element_type=jnp.float32
            )
        )
    peaks, totals, results = [], [], []
    for e in range(entries):
        masked = jnp.where(masks[e], scores[e] * scale, MASKED)
        peak = jnp.max(masked, axis=1, keepdims=True)
        weights = jnp.where(masks[e], jnp.exp(masked - peak), 0.0)
        total = jnp.sum(weights, axis=1, keepdims=True)
        values = split_dot(weights, sent_ref[e, :, head:])
        peaks.append(peak)
        totals.append(total)
        results.append((values / jnp.where(total > 0.0, total, 1.0)).astype(jnp.bfloat16))
    for e in range(entries):
        place, dest = places[e]
        out_ref[dest, pl.ds(starts[e], rows), :] = results[e]
        here = lane == row + starts[e]
        peak_ref[pl.ds(place, 1), :] = jnp.sum(
            jnp.where(here, peaks[e], 0.0), axis=0, keepdims=True
        )
        sum_ref[pl.ds(place, 1), :] = jnp.sum(
            jnp.where(here, totals[e], 0.0), axis=0, keepdims=True
        )
    row = lax.broadcasted_iota(jnp.int32, (INFO, block_len), 0)
    terms = three_terms(peak_ref[:n_inst] + peak_ref[n_inst:])
    terms += three_terms(sum_ref[:n_inst] + sum_ref[n_inst:])
    for i in range(n_inst):
        info = jnp.zeros((INFO, block_len), jnp.float32)
        for k, term in enumerate(terms):
            info = jnp.where(row == k, term[i : i + 1], info)
        out_ref[i, CAP * rows :, :] = info.astype(jnp.bfloat16)


def over_groups(combine, row, size):
    shift = row.shape[1] // 2
    while shift >= size:
        row = combine(row, pltpu.roll(row, shift, axis=1))
        shift //= 2
    return row


def project_kernel(
    slot_ref, back_ref, peak_ref, sum_ref, acc_ref,
    held_ref, weight_ref, out_ref, att_ref, w_ref, sems,
):
    slots, rows, head = acc_ref.shape
    n_inst = back_ref.shape[0]
    parts, out_rows, part_cols = out_ref.shape
    held = held_ref.shape[1]
    steps = out_rows // slots
    group = rows // steps
    columns = parts * part_cols
    edges = list(range(held, columns - part_cols + 1, part_cols)) + [columns]
    while edges[-1] - edges[-2] > TILE:
        edges.insert(-1, columns - (columns - edges[-2]) // (2 * TILE) * TILE)
    copies = {}
    for k, (low, high) in enumerate(zip(edges, edges[1:])):
        copies[low] = pltpu.make_async_copy(
            weight_ref.at[:, pl.ds(low, high - low)],
            w_ref.at[:, pl.ds(low - held, high - low)],
            sems.at[k],
        )
        copies[low].start()
    across = head // rows
    slot_of = slot_ref[...]
    lines = slot_of.shape[0]
    apart = across // CAP
    peak_rows, sum_rows = [], []
    for s in range(n_inst):
        info = back_ref[s, CAP * rows :, :].astype(jnp.float32)
        peak_rows.append(info[0:1] + info[1:2] + info[2:3])
        sum_rows.append(info[3:4] + info[4:5] + info[5:6])

    def together(per_source):
        total = None
        for k in range(apart):
            part = jnp.concatenate(per_source[k::apart], axis=0)
            if k:
                part = pltpu.roll(part, k * CAP * rows, axis=1)
            total = part if total is None else total + part
        return total

    peaks, sums = together(peak_rows), together(sum_rows)
    best, best_of = [], jnp.zeros((lines, head), jnp.float32)
    for k in range(slots):
        top = jnp.max(jnp.where(slot_of == k, peaks, MASKED), axis=0, keepdims=True)
        best.append(jnp.maximum(over_groups(jnp.maximum, top, rows), peak_ref[k]))
        best_of = jnp.where(slot_of == k, best[k], best_of)
    gains = jnp.where(slot_of >= 0, sums * jnp.exp(peaks - best_of), 0.0)
    keeps, matrix = [], []
    same = lax.broadcasted_iota(jnp.int32, (rows, head), 1) % rows == lax.broadcasted_iota(
        jnp.int32, (rows, head), 0
    )
    first_group = lax.broadcasted_iota(jnp.int32, (rows, head), 1) < rows
    for k in range(slots):
        mine = jnp.where(slot_of == k, gains, 0.0)
        keep = jnp.exp(peak_ref[k] - best[k])
        total = over_groups(jnp.add, jnp.sum(mine, axis=0, keepdims=True), rows)
        inverse = 1.0 / (total + sum_ref[k] * keep)
        keep = (keep * inverse)[0:1]
        keeps.append(
            jnp.sum(jnp.where(same & first_group, keep, 0.0), axis=1, keepdims=True)
        )
        mine = mine * inverse
        matrix.append(
            jnp.concatenate(
                [jnp.where(same, mine[j : j + 1], 0.0) for j in range(lines)], axis=1
            )
        )
    values = back_ref[:, : CAP * rows, :].reshape(n_inst * CAP * rows, head)
    arrived = split_dot(jnp.concatenate(matrix, axis=0), values)
    for slot in range(slots):
        done = keeps[slot] * acc_ref[slot] + arrived[slot * rows : (slot + 1) * rows]
        for step in range(steps):
            for g in range(group):
                at = step * group + g
                to = step * slots + slot
                att_ref[to : to + 1, g * head : (g + 1) * head] = done[at : at + 1]
    attended = att_ref[...].astype(jnp.bfloat16)
    for low in range(0, columns, TILE):
        if low in copies:
            copies[low].wait()
        if low < held:
            weight = held_ref[:, low : low + TILE]
        else:
            weight = w_ref[:, low - held : low - held + TILE]
        c, at = low // part_cols, low % part_cols
        out_ref[c, :, at : at + TILE] = jnp.dot(
            attended, weight, preferred_element_type=jnp.float32
        ).astype(jnp.bfloat16)


def params(mib):
    return pltpu.CompilerParams(vmem_limit_bytes=mib * 1024 * 1024)


def shards(queries, new_kv, kv_pool, out_weight, send_block, send_dest, block_table, cache_len):
    n_inst = lax.axis_size("inst")
    n_tp = lax.axis_size("tp")
    steps, slots, head_width = queries.shape
    pool_size, block_len, _, width = kv_pool.shape
    head = width // 2
    group = head_width // head
    rows = steps * group
    blocks = block_table.shape[1]
    entries = send_block.shape[0]
    columns = out_weight.shape[1]
    arrivals = n_inst * CAP
    scale = head ** (-0.5)
    f32, bf16, i32 = jnp.float32, jnp.bfloat16, jnp.int32
    shape = jax.ShapeDtypeStruct
    pool = kv_pool.reshape(pool_size, block_len, width)
    fresh = new_kv.reshape(steps, slots, width)

    packet = shape((n_inst, CAP * rows + INFO, head), bf16)
    ask, slot_query = pl.pallas_call(
        functools.partial(ask_kernel, pool_size, block_len),
        out_shape=(
            packet,
            shape((slots, rows + 2 * FRESH, head), bf16),
        ),
        in_specs=[HBM] * 6,
        out_specs=(VMEM, VMEM),
        scratch_shapes=[
            pltpu.SMEM((slots, blocks), i32),
            pltpu.SMEM((slots,), i32),
            pltpu.SMEM((entries,), i32),
            pltpu.SMEM((entries,), i32),
            pltpu.SMEM((arrivals + 1,), i32),
            pltpu.SMEM((arrivals + 1,), i32),
            pltpu.VMEM(queries.shape, bf16),
            pltpu.VMEM(fresh.shape, bf16),
            pltpu.VMEM((slots, rows + 2 * FRESH, head), f32),
            pltpu.SemaphoreType.DMA((6,)),
        ],
        compiler_params=params(64),
        name="ask",
    )(block_table, cache_len, send_block, send_dest, queries, fresh)
    asked = lax.all_to_all(ask, "inst", 0, 0, tiled=True)

    ahead = AHEAD * TILE
    own = shape((slots, rows, head), f32)
    stat = shape((slots, 8, head), f32)
    own_peak, own_sum, own_acc, sent, held, place, slot_of = pl.pallas_call(
        functools.partial(bring_kernel, scale, group, blocks, steps, n_inst),
        out_shape=(
            stat, stat, own,
            shape((entries, block_len, width), bf16),
            shape((head_width, ahead), bf16),
            shape((8, head), i32),
            shape((arrivals * rows // head, head), i32),
        ),
        in_specs=[VMEM, HBM, HBM],
        out_specs=(VMEM,) * 7,
        scratch_shapes=[
            pltpu.VMEM((slots, (blocks + 1) * block_len, width), bf16),
            pltpu.SemaphoreType.DMA((slots, blocks)),
            pltpu.SemaphoreType.DMA((entries,)),
            pltpu.SemaphoreType.DMA,
        ],
        compiler_params=params(50),
        cost_estimate=pl.CostEstimate(
            flops=4 * slots * rows * blocks * block_len * width,
            bytes_accessed=8 * slots * blocks * block_len * width,
            transcendentals=slots * rows * blocks * block_len,
        ),
        name="own",
    )(slot_query, pool, out_weight)

    part_cols = columns // n_tp
    answer = pl.pallas_call(
        functools.partial(answer_kernel, scale),
        out_shape=packet,
        in_specs=[VMEM, VMEM, VMEM],
        out_specs=VMEM,
        scratch_shapes=[
            pltpu.VMEM((arrivals, head), f32),
            pltpu.VMEM((arrivals, head), f32),
        ],
        compiler_params=params(16),
        name="answer",
    )(place, asked, sent)
    back = lax.all_to_all(answer, "inst", 0, 0, tiled=True)

    out_rows = steps * slots
    partial_out = pl.pallas_call(
        project_kernel,
        out_shape=shape((n_tp, out_rows, part_cols), bf16),
        in_specs=[VMEM] * 6 + [HBM],
        out_specs=VMEM,
        scratch_shapes=[
            pltpu.VMEM((out_rows, head_width), f32),
            pltpu.VMEM((head_width, columns - ahead), bf16),
            pltpu.SemaphoreType.DMA((2 * n_tp,)),
        ],
        compiler_params=params(44),
        name="project",
    )(slot_of, back, own_peak, own_sum, own_acc, held, out_weight)
    shares = lax.all_to_all(partial_out, "tp", 0, 0, tiled=True)
    total = jnp.sum(shares.astype(f32), axis=0).astype(bf16)
    return total.reshape(steps, slots, columns // n_tp)


def solution(mesh):
    return jax.shard_map(
        shards,
        mesh=mesh,
        in_specs=(
            P(None, "inst", "tp"),
            P(None, "inst", "tp", None),
            P("inst", None, "tp", None),
            P("tp", None),
            P("inst"),
            P("inst"),
            P("inst", None),
            P("inst"),
        ),
        out_specs=P(None, "inst", "tp"),
        check_vma=False,
    )
```

```python
import functools

import jax
import jax.numpy as jnp
from jax import lax
from jax.experimental import pallas as pl
from jax.experimental.pallas import tpu as pltpu
from jax.sharding import PartitionSpec as P

CAP = 2
INFO = 8
MASKED = -1e30
TILE = 256
LATE = 1
FRESH = 8
PLAN_ROW = 4
LENGTH_BASE = 64

VMEM = pl.BlockSpec(memory_space=pltpu.VMEM)
HBM = pl.BlockSpec(memory_space=pltpu.HBM)

nt_dims = (((1,), (1,)), ((), ()))


def split_dot(weights, values):
    rows = weights.shape[0]
    high = weights.astype(jnp.bfloat16)
    low = (weights - high.astype(jnp.float32)).astype(jnp.bfloat16)
    both = jnp.dot(
        jnp.concatenate([high, low], axis=0), values, preferred_element_type=jnp.float32
    )
    return both[:rows] + both[rows:]


def ask_kernel(
    pool_size, block_len, table_hbm, len_hbm, block_hbm, dest_hbm, q_hbm, new_hbm,
    out_ref, query_ref,
    table_ref, len_ref, block_ref, dest_ref, code_ref, live_ref, q_ref, new_ref, rows_ref, sems,
):
    slots, blocks = table_ref.shape
    steps = q_ref.shape[0]
    rows, head = query_ref.shape[1] - 2 * FRESH, query_ref.shape[2]
    group = rows // steps
    arrivals = out_ref.shape[0] * CAP
    copies = [
        pltpu.make_async_copy(source, target, sems.at[k])
        for k, (source, target) in enumerate(
            (
                (q_hbm, q_ref),
                (new_hbm, new_ref),
                (table_hbm, table_ref),
                (len_hbm, len_ref),
                (block_hbm, block_ref),
                (dest_hbm, dest_ref),
            )
        )
    ]
    for copy in copies:
        copy.start()
    rows_ref[:, rows:, :] = jnp.zeros((slots, 2 * FRESH, head), jnp.float32)
    for a in range(arrivals):
        code_ref[a] = 0
        live_ref[a] = 0
    for copy in copies:
        copy.wait()
    for step in range(steps):
        query = q_ref[step].astype(jnp.float32)
        for slot in range(slots):
            for g in range(group):
                at = step * group + g
                rows_ref[slot, at : at + 1, :] = query[slot : slot + 1, g * head : (g + 1) * head]
        fresh = new_ref[step].astype(jnp.float32)
        for slot in range(slots):
            for k in range(2):
                at = rows + k * FRESH + step
                rows_ref[slot, at : at + 1, :] = fresh[slot : slot + 1, k * head : (k + 1) * head]
    plan = []
    for slot in range(slots):
        length = len_ref[slot]
        for b in range(blocks):
            block_id = table_ref[slot, b]
            arrival = jnp.where(block_id >= pool_size, block_id - pool_size, arrivals)
            code_ref[arrival] = slot
            live_ref[arrival] = jnp.clip(length - b * block_len, 0, block_len)
            plan.append(block_id)
    plan += [len_ref[slot] // LENGTH_BASE for slot in range(slots)]
    plan += [len_ref[slot] % LENGTH_BASE for slot in range(slots)]
    plan += [block_ref[e] for e in range(block_ref.shape[0])]
    plan += [dest_ref[e] for e in range(dest_ref.shape[0])]
    lane = lax.broadcasted_iota(jnp.int32, (1, head), 1)
    line = jnp.zeros((1, head), jnp.int32)
    for k, number in enumerate(plan):
        line = jnp.where(lane == k, number, line)
    rows_ref[0, rows + PLAN_ROW : rows + PLAN_ROW + 1, :] = line.astype(jnp.float32)
    for slot in range(slots):
        query_ref[slot] = rows_ref[slot].astype(jnp.bfloat16)
    row = lax.broadcasted_iota(jnp.int32, (INFO, head), 0)
    for a in range(arrivals):
        source, rank = a // CAP, a % CAP
        out_ref[source, rank * rows : (rank + 1) * rows, :] = query_ref[code_ref[a], :rows, :]
    for source in range(arrivals // CAP):
        live = jnp.where(row < INFO // 2, live_ref[source * CAP], live_ref[source * CAP + 1])
        out_ref[source, CAP * rows :, :] = live.astype(jnp.float32).astype(jnp.bfloat16)


class Plan:
    def __init__(self, q_ref, blocks, entries):
        slots, rows = q_ref.shape[0], q_ref.shape[1] - 2 * FRESH
        row = q_ref[0, rows:, :].astype(jnp.float32)[PLAN_ROW : PLAN_ROW + 1].astype(jnp.int32)
        numbers = [row[0, k] for k in range(slots * (blocks + 2) + 2 * entries)]
        at = slots * blocks
        self.table = [numbers[slot * blocks : (slot + 1) * blocks] for slot in range(slots)]
        self.length = [
            numbers[at + slot] * LENGTH_BASE + numbers[at + slots + slot] for slot in range(slots)
        ]
        at += 2 * slots
        self.block, self.dest = numbers[at : at + entries], numbers[at + entries :]


def own_kernel(
    scale, head_group, blocks, first,
    steps, plan, q_ref, pool_ref,
    stat_ref, acc_ref, kv_ref, sems, bring,
):
    pool_size, block_len, _ = pool_ref.shape
    slots, rows, head = q_ref.shape[0], q_ref.shape[1] - 2 * FRESH, q_ref.shape[2]
    span = blocks * block_len
    mine = range(first, first + acc_ref.shape[0])

    def own_copy(slot, b):
        block_id = jnp.clip(plan.table[slot][b], 0, pool_size - 1)
        return pltpu.make_async_copy(
            pool_ref.at[block_id],
            kv_ref.at[slot - first, pl.ds(b * block_len, block_len), :],
            sems.at[slot - first, b],
        )

    for slot in mine:
        for b in range(blocks):
            own_copy(slot, b).start()
    brought = bring()
    lane = lax.broadcasted_iota(jnp.int32, (rows, block_len), 1)
    step = lax.broadcasted_iota(jnp.int32, (rows, block_len), 0) // head_group
    for slot in mine:
        fresh = q_ref[slot, rows:, :].astype(jnp.float32)
        rest = jnp.zeros((block_len - FRESH, head), jnp.float32)
        for k in range(2):
            part = jnp.concatenate([fresh[k * FRESH : (k + 1) * FRESH], rest], axis=0)
            kv_ref[slot - first, span:, k * head : (k + 1) * head] = part.astype(jnp.bfloat16)
    for slot in mine:
        for b in range(blocks):
            own_copy(slot, b).wait()
        scores = lax.dot_general(
            q_ref[slot, :rows, :], kv_ref[slot - first, :, :head], nt_dims, preferred_element_type=jnp.float32
        ) * scale
        parts_s = []
        for b in range(blocks):
            live = jnp.clip(plan.length[slot] - b * block_len, 0, block_len)
            live = jnp.where(plan.table[slot][b] < pool_size, live, 0)
            part = scores[:, b * block_len : (b + 1) * block_len]
            parts_s.append(jnp.where(lane < live, part, MASKED))
        parts_s.append(jnp.where((lane <= step) & (lane < steps), scores[:, span:], MASKED))
        peak = jnp.max(functools.reduce(jnp.maximum, parts_s), axis=1, keepdims=True)
        weights = [jnp.exp(part - peak) for part in parts_s]
        total = jnp.sum(functools.reduce(jnp.add, weights), axis=1, keepdims=True)
        acc_ref[slot - first] = split_dot(jnp.concatenate(weights, axis=1), kv_ref[slot - first, :, head:])
        same = lane % rows == lax.broadcasted_iota(jnp.int32, (rows, block_len), 0)
        for row, column in ((0, peak), (stat_ref.shape[0] // 2, total)):
            row += slot - first
            stat_ref[row : row + 1, :] = jnp.sum(
                jnp.where(same, column, 0.0), axis=0, keepdims=True
            )
    for copy in brought:
        copy.wait()


def bring_kernel(
    scale, head_group, blocks, steps, n_inst,
    q_ref, pool_ref, weight_ref,
    stat_ref, acc_ref, sent_ref, held_ref, place_ref, slot_ref,
    kv_ref, sems, sent_sems, held_sem,
):
    pool_size = pool_ref.shape[0]
    slots, rows, head = q_ref.shape[0], q_ref.shape[1] - 2 * FRESH, q_ref.shape[2]
    entries = sent_ref.shape[0]
    plan = Plan(q_ref, blocks, entries)

    def bring():
        copies = []
        for e in range(entries):
            block_id = jnp.clip(plan.block[e], 0, pool_size - 1)
            copies.append(
                pltpu.make_async_copy(pool_ref.at[block_id], sent_ref.at[e], sent_sems.at[e])
            )
            copies[e].start()
        held_copy = pltpu.make_async_copy(
            weight_ref.at[:, pl.ds(0, held_ref.shape[1])], held_ref, held_sem
        )
        held_copy.start()
        copies.append(held_copy)
        lane = lax.broadcasted_iota(jnp.int32, place_ref.shape, 1)
        places = jnp.zeros(place_ref.shape, jnp.int32)
        for e in range(entries):
            dest = jnp.clip(plan.dest[e], 0, n_inst - 1)
            rank = sum((plan.dest[f] == plan.dest[e]).astype(jnp.int32) for f in range(e))
            place = jnp.minimum(rank, CAP - 1) * n_inst + dest
            places = jnp.where(lane == e, place, places)
        place_ref[...] = places
        line = lax.broadcasted_iota(jnp.int32, slot_ref.shape, 0)
        arrival = line * (head // rows) + lax.broadcasted_iota(jnp.int32, slot_ref.shape, 1) // rows
        slot_of = jnp.full(slot_ref.shape, -1, jnp.int32)
        for slot in range(slots):
            for b in range(blocks):
                slot_of = jnp.where(arrival == plan.table[slot][b] - pool_size, slot, slot_of)
        slot_ref[...] = slot_of
        return copies

    own_kernel(
        scale, head_group, blocks, 0, steps, plan, q_ref, pool_ref,
        stat_ref, acc_ref, kv_ref, sems, bring,
    )


def three_terms(values):
    high = values.astype(jnp.bfloat16).astype(jnp.float32)
    rest = values - high
    middle = rest.astype(jnp.bfloat16).astype(jnp.float32)
    return high, middle, rest - middle


def answer_kernel(
    scale, place_ref, asked_ref, sent_ref, out_ref, peak_ref, sum_ref
):
    entries, block_len, width = sent_ref.shape
    head = width // 2
    n_inst = out_ref.shape[0]
    rows = (out_ref.shape[1] - INFO) // CAP
    out_ref[...] = jnp.zeros_like(out_ref)
    peak_ref[...] = jnp.zeros_like(peak_ref)
    sum_ref[...] = jnp.zeros_like(sum_ref)
    lane = lax.broadcasted_iota(jnp.int32, (rows, block_len), 1)
    row = lax.broadcasted_iota(jnp.int32, (rows, block_len), 0)
    key = lane.astype(jnp.float32)
    places, starts, masks, scores = [], [], [], []
    across = place_ref[...]
    for e in range(entries):
        place = across[0, e]
        dest = lax.rem(place, n_inst)
        rank = lax.div(place, n_inst)
        start = pl.multiple_of(rank * rows, rows)
        query = asked_ref[dest, pl.ds(start, rows), :]
        info = asked_ref[dest, CAP * rows :, :].astype(jnp.float32)
        live = jnp.where(rank == 0, info[0:1], info[INFO // 2 : INFO // 2 + 1])
        places.append((place, dest))
        starts.append(start)
        masks.append(key < live)
        scores.append(
            lax.dot_general(
                query, sent_ref[e, :, :head], nt_dims, preferred_element_type=jnp.float32
            )
        )
    peaks, totals, results = [], [], []
    for e in range(entries):
        masked = jnp.where(masks[e], scores[e] * scale, MASKED)
        peak = jnp.max(masked, axis=1, keepdims=True)
        weights = jnp.where(masks[e], jnp.exp(masked - peak), 0.0)
        total = jnp.sum(weights, axis=1, keepdims=True)
        values = split_dot(weights, sent_ref[e, :, head:])
        peaks.append(peak)
        totals.append(total)
        results.append((values / jnp.where(total > 0.0, total, 1.0)).astype(jnp.bfloat16))
    for e in range(entries):
        place, dest = places[e]
        out_ref[dest, pl.ds(starts[e], rows), :] = results[e]
        here = lane == row + starts[e]
        peak_ref[pl.ds(place, 1), :] = jnp.sum(
            jnp.where(here, peaks[e], 0.0), axis=0, keepdims=True
        )
        sum_ref[pl.ds(place, 1), :] = jnp.sum(
            jnp.where(here, totals[e], 0.0), axis=0, keepdims=True
        )
    row = lax.broadcasted_iota(jnp.int32, (INFO, block_len), 0)
    terms = three_terms(peak_ref[:n_inst] + peak_ref[n_inst:])
    terms += three_terms(sum_ref[:n_inst] + sum_ref[n_inst:])
    for i in range(n_inst):
        info = jnp.zeros((INFO, block_len), jnp.float32)
        for k, term in enumerate(terms):
            info = jnp.where(row == k, term[i : i + 1], info)
        out_ref[i, CAP * rows :, :] = info.astype(jnp.bfloat16)


def over_groups(combine, row, size):
    shift = row.shape[1] // 2
    while shift >= size:
        row = combine(row, pltpu.roll(row, shift, axis=1))
        shift //= 2
    return row


def project_kernel(
    scale, head_group, blocks, steps, entries,
    slot_ref, back_ref, q_ref, stat_ref, acc_ref,
    held_ref, weight_ref, pool_ref, out_ref,
    late_stat, late_acc, kv_ref, att_ref, w_ref, own_sems, sems,
):
    early, rows, head = acc_ref.shape
    slots = early + late_acc.shape[0]
    n_inst = back_ref.shape[0]
    parts, out_rows, part_cols = out_ref.shape
    held = held_ref.shape[1]
    group = rows // steps
    ahead = held // part_cols

    def copy(c):
        return pltpu.make_async_copy(
            weight_ref.at[:, pl.ds(pl.multiple_of(c * part_cols, part_cols), part_cols)],
            w_ref.at[:, pl.ds(pl.multiple_of((c - ahead) * part_cols, part_cols), part_cols)],
            sems.at[c],
        )

    for c in range(ahead, ahead + 2):
        copy(c).start()

    def bring():
        for c in range(ahead + 2, parts):
            copy(c).start()
        return []

    own_kernel(
        scale, head_group, blocks, early, steps, Plan(q_ref, blocks, entries), q_ref, pool_ref,
        late_stat, late_acc, kv_ref, own_sems, bring,
    )
    owns = [(stat_ref, acc_ref, k) for k in range(early)]
    owns += [(late_stat, late_acc, k) for k in range(slots - early)]
    sums_at = stat_ref.shape[0] // 2
    peak_own = [stat[k : k + 1, :] for stat, _, k in owns]
    sum_own = [stat[sums_at + k : sums_at + k + 1, :] for stat, _, k in owns]
    acc_own = [acc[k] for _, acc, k in owns]
    across = head // rows
    slot_of = slot_ref[...]
    lines = slot_of.shape[0]
    apart = across // CAP
    peak_rows, sum_rows = [], []
    for s in range(n_inst):
        info = back_ref[s, CAP * rows :, :].astype(jnp.float32)
        peak_rows.append(info[0:1] + info[1:2] + info[2:3])
        sum_rows.append(info[3:4] + info[4:5] + info[5:6])

    def together(per_source):
        total = None
        for k in range(apart):
            part = jnp.concatenate(per_source[k::apart], axis=0)
            if k:
                part = pltpu.roll(part, k * CAP * rows, axis=1)
            total = part if total is None else total + part
        return total

    peaks, sums = together(peak_rows), together(sum_rows)
    best, best_of = [], jnp.zeros((lines, head), jnp.float32)
    for k in range(slots):
        top = jnp.max(jnp.where(slot_of == k, peaks, MASKED), axis=0, keepdims=True)
        best.append(jnp.maximum(over_groups(jnp.maximum, top, rows), peak_own[k]))
        best_of = jnp.where(slot_of == k, best[k], best_of)
    gains = jnp.where(slot_of >= 0, sums * jnp.exp(peaks - best_of), 0.0)
    keeps, matrix = [], []
    same = lax.broadcasted_iota(jnp.int32, (rows, head), 1) % rows == lax.broadcasted_iota(
        jnp.int32, (rows, head), 0
    )
    first_group = lax.broadcasted_iota(jnp.int32, (rows, head), 1) < rows
    for k in range(slots):
        mine = jnp.where(slot_of == k, gains, 0.0)
        keep = jnp.exp(peak_own[k] - best[k])
        total = over_groups(jnp.add, jnp.sum(mine, axis=0, keepdims=True), rows)
        inverse = 1.0 / (total + sum_own[k] * keep)
        keep = keep * inverse
        keeps.append(
            jnp.sum(jnp.where(same & first_group, keep, 0.0), axis=1, keepdims=True)
        )
        mine = mine * inverse
        matrix.append(
            jnp.concatenate(
                [jnp.where(same, mine[j : j + 1], 0.0) for j in range(lines)], axis=1
            )
        )
    values = back_ref[:, : CAP * rows, :].reshape(n_inst * CAP * rows, head)
    arrived = split_dot(jnp.concatenate(matrix, axis=0), values)
    for slot in range(slots):
        done = keeps[slot] * acc_own[slot] + arrived[slot * rows : (slot + 1) * rows]
        for step in range(steps):
            for g in range(group):
                at = step * group + g
                to = step * slots + slot
                att_ref[to : to + 1, g * head : (g + 1) * head] = done[at : at + 1]
    attended = att_ref[...].astype(jnp.bfloat16)

    def multiply(c, source, start):
        def tile(k, carry):
            at = pl.multiple_of(k * TILE, TILE)
            weight = source[:, pl.ds(pl.multiple_of(start + at, TILE), TILE)]
            out_ref[c, :, pl.ds(at, TILE)] = jnp.dot(
                attended, weight, preferred_element_type=jnp.float32
            ).astype(jnp.bfloat16)
            return carry

        lax.fori_loop(0, part_cols // TILE, tile, 0, unroll=True)

    for c in range(ahead):
        multiply(c, held_ref, c * part_cols)

    def part(c, carry):
        copy(c).wait()
        multiply(c, w_ref, (c - ahead) * part_cols)
        return carry

    lax.fori_loop(ahead, parts, part, 0)


def params(mib):
    return pltpu.CompilerParams(vmem_limit_bytes=mib * 1024 * 1024)


def shards(queries, new_kv, kv_pool, out_weight, send_block, send_dest, block_table, cache_len):
    n_inst = lax.axis_size("inst")
    n_tp = lax.axis_size("tp")
    steps, slots, head_width = queries.shape
    pool_size, block_len, _, width = kv_pool.shape
    head = width // 2
    group = head_width // head
    rows = steps * group
    blocks = block_table.shape[1]
    entries = send_block.shape[0]
    columns = out_weight.shape[1]
    arrivals = n_inst * CAP
    scale = head ** (-0.5)
    f32, bf16, i32 = jnp.float32, jnp.bfloat16, jnp.int32
    shape = jax.ShapeDtypeStruct
    pool = kv_pool.reshape(pool_size, block_len, width)
    fresh = new_kv.reshape(steps, slots, width)

    packet = shape((n_inst, CAP * rows + INFO, head), bf16)
    ask, slot_query = pl.pallas_call(
        functools.partial(ask_kernel, pool_size, block_len),
        out_shape=(
            packet,
            shape((slots, rows + 2 * FRESH, head), bf16),
        ),
        in_specs=[HBM] * 6,
        out_specs=(VMEM, VMEM),
        scratch_shapes=[
            pltpu.SMEM((slots, blocks), i32),
            pltpu.SMEM((slots,), i32),
            pltpu.SMEM((entries,), i32),
            pltpu.SMEM((entries,), i32),
            pltpu.SMEM((arrivals + 1,), i32),
            pltpu.SMEM((arrivals + 1,), i32),
            pltpu.VMEM(queries.shape, bf16),
            pltpu.VMEM(fresh.shape, bf16),
            pltpu.VMEM((slots, rows + 2 * FRESH, head), f32),
            pltpu.SemaphoreType.DMA((6,)),
        ],
        compiler_params=params(64),
        name="ask",
    )(block_table, cache_len, send_block, send_dest, queries, fresh)
    asked = lax.all_to_all(ask, "inst", 0, 0, tiled=True)

    ahead = columns // n_tp
    early = slots - LATE
    own = shape((early, rows, head), f32)
    stat = shape((8, head), f32)
    own_stat, own_acc, sent, held, place, slot_of = pl.pallas_call(
        functools.partial(bring_kernel, scale, group, blocks, steps, n_inst),
        out_shape=(
            stat, own,
            shape((entries, block_len, width), bf16),
            shape((head_width, ahead), bf16),
            shape((8, head), i32),
            shape((arrivals * rows // head, head), i32),
        ),
        in_specs=[VMEM, HBM, HBM],
        out_specs=(VMEM,) * 6,
        scratch_shapes=[
            pltpu.VMEM((early, (blocks + 1) * block_len, width), bf16),
            pltpu.SemaphoreType.DMA((early, blocks)),
            pltpu.SemaphoreType.DMA((entries,)),
            pltpu.SemaphoreType.DMA,
        ],
        compiler_params=params(50),
        cost_estimate=pl.CostEstimate(
            flops=4 * slots * rows * blocks * block_len * width,
            bytes_accessed=8 * slots * blocks * block_len * width,
            transcendentals=slots * rows * blocks * block_len,
        ),
        name="own",
    )(slot_query, pool, out_weight)

    part_cols = columns // n_tp
    answer = pl.pallas_call(
        functools.partial(answer_kernel, scale),
        out_shape=packet,
        in_specs=[VMEM, VMEM, VMEM],
        out_specs=VMEM,
        scratch_shapes=[
            pltpu.VMEM((arrivals, head), f32),
            pltpu.VMEM((arrivals, head), f32),
        ],
        compiler_params=params(16),
        name="answer",
    )(place, asked, sent)
    back = lax.all_to_all(answer, "inst", 0, 0, tiled=True)

    out_rows = steps * slots
    partial_out = pl.pallas_call(
        functools.partial(project_kernel, scale, group, blocks, steps, entries),
        out_shape=shape((n_tp, out_rows, part_cols), bf16),
        in_specs=[VMEM] * 6 + [HBM, HBM],
        out_specs=VMEM,
        scratch_shapes=[
            pltpu.VMEM(stat.shape, f32),
            pltpu.VMEM((LATE, rows, head), f32),
            pltpu.VMEM((LATE, (blocks + 1) * block_len, width), bf16),
            pltpu.VMEM((out_rows, head_width), f32),
            pltpu.VMEM((head_width, columns - ahead), bf16),
            pltpu.SemaphoreType.DMA((LATE, blocks)),
            pltpu.SemaphoreType.DMA((n_tp,)),
        ],
        compiler_params=params(49),
        name="project",
    )(slot_of, back, slot_query, own_stat, own_acc, held, out_weight, pool)
    shares = lax.all_to_all(partial_out, "tp", 0, 0, tiled=True)
    total = jnp.sum(shares.astype(f32), axis=0).astype(bf16)
    return total.reshape(steps, slots, columns // n_tp)


def solution(mesh):
    return jax.shard_map(
        shards,
        mesh=mesh,
        in_specs=(
            P(None, "inst", "tp"),
            P(None, "inst", "tp", None),
            P("inst", None, "tp", None),
            P("tp", None),
            P("inst"),
            P("inst"),
            P("inst", None),
            P("inst"),
        ),
        out_specs=P(None, "inst", "tp"),
        check_vma=False,
    )
```

```python
import functools

import jax
import jax.numpy as jnp
from jax import lax
from jax.experimental import pallas as pl
from jax.experimental.pallas import tpu as pltpu
from jax.sharding import PartitionSpec as P

CAP = 2
INFO = 8
MASKED = -1e30
TILE = 256
FRESH = 8
PLAN_ROW = 4
LENGTH_BASE = 64

VMEM = pl.BlockSpec(memory_space=pltpu.VMEM)
HBM = pl.BlockSpec(memory_space=pltpu.HBM)

nt_dims = (((1,), (1,)), ((), ()))


def split_dot(weights, values):
    rows = weights.shape[0]
    high = weights.astype(jnp.bfloat16)
    low = (weights - high.astype(jnp.float32)).astype(jnp.bfloat16)
    both = jnp.dot(
        jnp.concatenate([high, low], axis=0), values, preferred_element_type=jnp.float32
    )
    return both[:rows] + both[rows:]


def ask_kernel(
    pool_size, block_len, table_hbm, len_hbm, block_hbm, dest_hbm, q_hbm, new_hbm,
    out_ref, query_ref,
    table_ref, len_ref, block_ref, dest_ref, code_ref, live_ref, q_ref, new_ref, rows_ref, sems,
):
    slots, blocks = table_ref.shape
    steps = q_ref.shape[0]
    rows, head = query_ref.shape[1] - 2 * FRESH, query_ref.shape[2]
    group = rows // steps
    arrivals = out_ref.shape[0] * CAP
    copies = [
        pltpu.make_async_copy(source, target, sems.at[k])
        for k, (source, target) in enumerate(
            (
                (q_hbm, q_ref),
                (new_hbm, new_ref),
                (table_hbm, table_ref),
                (len_hbm, len_ref),
                (block_hbm, block_ref),
                (dest_hbm, dest_ref),
            )
        )
    ]
    for copy in copies:
        copy.start()
    rows_ref[:, rows:, :] = jnp.zeros((slots, 2 * FRESH, head), jnp.float32)
    for a in range(arrivals):
        code_ref[a] = 0
        live_ref[a] = 0
    for copy in copies:
        copy.wait()
    for step in range(steps):
        query = q_ref[step].astype(jnp.float32)
        for slot in range(slots):
            for g in range(group):
                at = step * group + g
                rows_ref[slot, at : at + 1, :] = query[slot : slot + 1, g * head : (g + 1) * head]
        fresh = new_ref[step].astype(jnp.float32)
        for slot in range(slots):
            for k in range(2):
                at = rows + k * FRESH + step
                rows_ref[slot, at : at + 1, :] = fresh[slot : slot + 1, k * head : (k + 1) * head]
    plan = []
    for slot in range(slots):
        length = len_ref[slot]
        for b in range(blocks):
            block_id = table_ref[slot, b]
            arrival = jnp.where(block_id >= pool_size, block_id - pool_size, arrivals)
            code_ref[arrival] = slot
            live_ref[arrival] = jnp.clip(length - b * block_len, 0, block_len)
            plan.append(block_id)
    plan += [len_ref[slot] // LENGTH_BASE for slot in range(slots)]
    plan += [len_ref[slot] % LENGTH_BASE for slot in range(slots)]
    plan += [block_ref[e] for e in range(block_ref.shape[0])]
    plan += [dest_ref[e] for e in range(dest_ref.shape[0])]
    lane = lax.broadcasted_iota(jnp.int32, (1, head), 1)
    line = jnp.zeros((1, head), jnp.int32)
    for k, number in enumerate(plan):
        line = jnp.where(lane == k, number, line)
    rows_ref[0, rows + PLAN_ROW : rows + PLAN_ROW + 1, :] = line.astype(jnp.float32)
    for slot in range(slots):
        query_ref[slot] = rows_ref[slot].astype(jnp.bfloat16)
    row = lax.broadcasted_iota(jnp.int32, (INFO, head), 0)
    for a in range(arrivals):
        source, rank = a // CAP, a % CAP
        out_ref[source, rank * rows : (rank + 1) * rows, :] = query_ref[code_ref[a], :rows, :]
    for source in range(arrivals // CAP):
        live = jnp.where(row < INFO // 2, live_ref[source * CAP], live_ref[source * CAP + 1])
        out_ref[source, CAP * rows :, :] = live.astype(jnp.float32).astype(jnp.bfloat16)


class Plan:
    def __init__(self, q_ref, blocks, entries):
        slots, rows = q_ref.shape[0], q_ref.shape[1] - 2 * FRESH
        row = q_ref[0, rows:, :].astype(jnp.float32)[PLAN_ROW : PLAN_ROW + 1].astype(jnp.int32)
        numbers = [row[0, k] for k in range(slots * (blocks + 2) + 2 * entries)]
        at = slots * blocks
        self.table = [numbers[slot * blocks : (slot + 1) * blocks] for slot in range(slots)]
        self.length = [
            numbers[at + slot] * LENGTH_BASE + numbers[at + slots + slot] for slot in range(slots)
        ]
        at += 2 * slots
        self.block, self.dest = numbers[at : at + entries], numbers[at + entries :]


def own_kernel(
    scale, head_group, blocks, first,
    steps, plan, q_ref, pool_ref,
    peak_ref, sum_ref, acc_ref, kv_ref, sems, bring,
):
    pool_size, block_len, _ = pool_ref.shape
    slots, rows, head = q_ref.shape[0], q_ref.shape[1] - 2 * FRESH, q_ref.shape[2]
    span = blocks * block_len
    mine = range(first, first + peak_ref.shape[0])

    def own_copy(slot, b):
        block_id = jnp.clip(plan.table[slot][b], 0, pool_size - 1)
        return pltpu.make_async_copy(
            pool_ref.at[block_id],
            kv_ref.at[slot - first, pl.ds(b * block_len, block_len), :],
            sems.at[slot - first, b],
        )

    for slot in mine:
        for b in range(blocks):
            own_copy(slot, b).start()
    brought = bring()
    lane = lax.broadcasted_iota(jnp.int32, (rows, block_len), 1)
    step = lax.broadcasted_iota(jnp.int32, (rows, block_len), 0) // head_group
    for slot in mine:
        fresh = q_ref[slot, rows:, :].astype(jnp.float32)
        rest = jnp.zeros((block_len - FRESH, head), jnp.float32)
        for k in range(2):
            part = jnp.concatenate([fresh[k * FRESH : (k + 1) * FRESH], rest], axis=0)
            kv_ref[slot - first, span:, k * head : (k + 1) * head] = part.astype(jnp.bfloat16)
    def score(slot):
        for b in range(blocks):
            own_copy(slot, b).wait()
        return lax.dot_general(
            q_ref[slot, :rows, :], kv_ref[slot - first, :, :head], nt_dims, preferred_element_type=jnp.float32
        ) * scale

    def attend(slot, scores):
        parts_s = []
        for b in range(blocks):
            live = jnp.clip(plan.length[slot] - b * block_len, 0, block_len)
            live = jnp.where(plan.table[slot][b] < pool_size, live, 0)
            part = scores[:, b * block_len : (b + 1) * block_len]
            parts_s.append(jnp.where(lane < live, part, MASKED))
        parts_s.append(jnp.where((lane <= step) & (lane < steps), scores[:, span:], MASKED))
        peak = jnp.max(functools.reduce(jnp.maximum, parts_s), axis=1, keepdims=True)
        weights = [jnp.exp(part - peak) for part in parts_s]
        total = jnp.sum(functools.reduce(jnp.add, weights), axis=1, keepdims=True)
        acc_ref[slot - first] = split_dot(jnp.concatenate(weights, axis=1), kv_ref[slot - first, :, head:])
        same = lane % rows == lax.broadcasted_iota(jnp.int32, (rows, block_len), 0)
        for ref, column in ((peak_ref, peak), (sum_ref, total)):
            across = jnp.sum(jnp.where(same, column, 0.0), axis=0, keepdims=True)
            ref[slot - first] = jnp.broadcast_to(across, ref.shape[1:])

    scores = score(first)
    for slot in mine:
        later = score(slot + 1) if slot + 1 in mine else None
        attend(slot, scores)
        scores = later
    for copy in brought:
        copy.wait()


def bring_kernel(
    scale, head_group, blocks, steps, n_inst,
    q_ref, pool_ref, weight_ref,
    peak_ref, sum_ref, acc_ref, sent_ref, held_ref, place_ref, slot_ref,
    kv_ref, sems, sent_sems, held_sem,
):
    pool_size = pool_ref.shape[0]
    slots, rows, head = q_ref.shape[0], q_ref.shape[1] - 2 * FRESH, q_ref.shape[2]
    entries = sent_ref.shape[0]
    plan = Plan(q_ref, blocks, entries)

    def bring():
        copies = []
        for e in range(entries):
            block_id = jnp.clip(plan.block[e], 0, pool_size - 1)
            copies.append(
                pltpu.make_async_copy(pool_ref.at[block_id], sent_ref.at[e], sent_sems.at[e])
            )
            copies[e].start()
        held_copy = pltpu.make_async_copy(
            weight_ref.at[:, pl.ds(0, held_ref.shape[1])], held_ref, held_sem
        )
        held_copy.start()
        copies.append(held_copy)
        lane = lax.broadcasted_iota(jnp.int32, place_ref.shape, 1)
        places = jnp.zeros(place_ref.shape, jnp.int32)
        for e in range(entries):
            dest = jnp.clip(plan.dest[e], 0, n_inst - 1)
            rank = sum((plan.dest[f] == plan.dest[e]).astype(jnp.int32) for f in range(e))
            place = jnp.minimum(rank, CAP - 1) * n_inst + dest
            places = jnp.where(lane == e, place, places)
        place_ref[...] = places
        line = lax.broadcasted_iota(jnp.int32, slot_ref.shape, 0)
        arrival = line * (head // rows) + lax.broadcasted_iota(jnp.int32, slot_ref.shape, 1) // rows
        slot_of = jnp.full(slot_ref.shape, -1, jnp.int32)
        for slot in range(slots):
            for b in range(blocks):
                slot_of = jnp.where(arrival == plan.table[slot][b] - pool_size, slot, slot_of)
        slot_ref[...] = slot_of
        return copies

    own_kernel(
        scale, head_group, blocks, 0, steps, plan, q_ref, pool_ref,
        peak_ref, sum_ref, acc_ref, kv_ref, sems, bring,
    )


def three_terms(values):
    high = values.astype(jnp.bfloat16).astype(jnp.float32)
    rest = values - high
    middle = rest.astype(jnp.bfloat16).astype(jnp.float32)
    return high, middle, rest - middle


def answer_kernel(
    scale, place_ref, asked_ref, sent_ref, out_ref, peak_ref, sum_ref
):
    entries, block_len, width = sent_ref.shape
    head = width // 2
    n_inst = out_ref.shape[0]
    rows = (out_ref.shape[1] - INFO) // CAP
    out_ref[...] = jnp.zeros_like(out_ref)
    peak_ref[...] = jnp.zeros_like(peak_ref)
    sum_ref[...] = jnp.zeros_like(sum_ref)
    lane = lax.broadcasted_iota(jnp.int32, (rows, block_len), 1)
    row = lax.broadcasted_iota(jnp.int32, (rows, block_len), 0)
    key = lane.astype(jnp.float32)
    places, starts, masks, scores = [], [], [], []
    across = place_ref[...]
    for e in range(entries):
        place = across[0, e]
        dest = lax.rem(place, n_inst)
        rank = lax.div(place, n_inst)
        start = pl.multiple_of(rank * rows, rows)
        query = asked_ref[dest, pl.ds(start, rows), :]
        info = asked_ref[dest, CAP * rows :, :].astype(jnp.float32)
        live = jnp.where(rank == 0, info[0:1], info[INFO // 2 : INFO // 2 + 1])
        places.append((place, dest))
        starts.append(start)
        masks.append(key < live)
        scores.append(
            lax.dot_general(
                query, sent_ref[e, :, :head], nt_dims, preferred_element_type=jnp.float32
            )
        )
    peaks, totals, results = [], [], []
    for e in range(entries):
        masked = jnp.where(masks[e], scores[e] * scale, MASKED)
        peak = jnp.max(masked, axis=1, keepdims=True)
        weights = jnp.where(masks[e], jnp.exp(masked - peak), 0.0)
        total = jnp.sum(weights, axis=1, keepdims=True)
        values = split_dot(weights, sent_ref[e, :, head:])
        peaks.append(peak)
        totals.append(total)
        results.append((values / jnp.where(total > 0.0, total, 1.0)).astype(jnp.bfloat16))
    for e in range(entries):
        place, dest = places[e]
        out_ref[dest, pl.ds(starts[e], rows), :] = results[e]
        here = lane == row + starts[e]
        peak_ref[pl.ds(place, 1), :] = jnp.sum(
            jnp.where(here, peaks[e], 0.0), axis=0, keepdims=True
        )
        sum_ref[pl.ds(place, 1), :] = jnp.sum(
            jnp.where(here, totals[e], 0.0), axis=0, keepdims=True
        )
    row = lax.broadcasted_iota(jnp.int32, (INFO, block_len), 0)
    terms = three_terms(peak_ref[:n_inst] + peak_ref[n_inst:])
    terms += three_terms(sum_ref[:n_inst] + sum_ref[n_inst:])
    for i in range(n_inst):
        info = jnp.zeros((INFO, block_len), jnp.float32)
        for k, term in enumerate(terms):
            info = jnp.where(row == k, term[i : i + 1], info)
        out_ref[i, CAP * rows :, :] = info.astype(jnp.bfloat16)


def over_groups(combine, row, size):
    shift = row.shape[1] // 2
    while shift >= size:
        row = combine(row, pltpu.roll(row, shift, axis=1))
        shift //= 2
    return row


def project_kernel(
    slot_ref, back_ref, peak_ref, sum_ref, acc_ref,
    held_ref, weight_ref, out_ref, att_ref, w_ref, sems,
):
    slots, rows, head = acc_ref.shape
    n_inst = back_ref.shape[0]
    parts, out_rows, part_cols = out_ref.shape
    held = held_ref.shape[1]
    steps = out_rows // slots
    group = rows // steps
    ahead = held // part_cols

    def copy(c):
        return pltpu.make_async_copy(
            weight_ref.at[:, pl.ds(pl.multiple_of(c * part_cols, part_cols), part_cols)],
            w_ref.at[:, pl.ds(pl.multiple_of((c - ahead) * part_cols, part_cols), part_cols)],
            sems.at[c],
        )

    for c in range(ahead, parts):
        copy(c).start()
    across = head // rows
    slot_of = slot_ref[...]
    lines = slot_of.shape[0]
    apart = across // CAP
    peak_rows, sum_rows = [], []
    for s in range(n_inst):
        info = back_ref[s, CAP * rows :, :].astype(jnp.float32)
        peak_rows.append(info[0:1] + info[1:2] + info[2:3])
        sum_rows.append(info[3:4] + info[4:5] + info[5:6])

    def together(per_source):
        total = None
        for k in range(apart):
            part = jnp.concatenate(per_source[k::apart], axis=0)
            if k:
                part = pltpu.roll(part, k * CAP * rows, axis=1)
            total = part if total is None else total + part
        return total

    peaks, sums = together(peak_rows), together(sum_rows)
    best, best_of = [], jnp.zeros((lines, head), jnp.float32)
    for k in range(slots):
        top = jnp.max(jnp.where(slot_of == k, peaks, MASKED), axis=0, keepdims=True)
        best.append(jnp.maximum(over_groups(jnp.maximum, top, rows), peak_ref[k]))
        best_of = jnp.where(slot_of == k, best[k], best_of)
    gains = jnp.where(slot_of >= 0, sums * jnp.exp(peaks - best_of), 0.0)
    keeps, matrix = [], []
    same = lax.broadcasted_iota(jnp.int32, (rows, head), 1) % rows == lax.broadcasted_iota(
        jnp.int32, (rows, head), 0
    )
    first_group = lax.broadcasted_iota(jnp.int32, (rows, head), 1) < rows
    for k in range(slots):
        mine = jnp.where(slot_of == k, gains, 0.0)
        keep = jnp.exp(peak_ref[k] - best[k])
        total = over_groups(jnp.add, jnp.sum(mine, axis=0, keepdims=True), rows)
        inverse = 1.0 / (total + sum_ref[k] * keep)
        keep = (keep * inverse)[0:1]
        keeps.append(
            jnp.sum(jnp.where(same & first_group, keep, 0.0), axis=1, keepdims=True)
        )
        mine = mine * inverse
        matrix.append(
            jnp.concatenate(
                [jnp.where(same, mine[j : j + 1], 0.0) for j in range(lines)], axis=1
            )
        )
    values = back_ref[:, : CAP * rows, :].reshape(n_inst * CAP * rows, head)
    arrived = split_dot(jnp.concatenate(matrix, axis=0), values)
    for slot in range(slots):
        done = keeps[slot] * acc_ref[slot] + arrived[slot * rows : (slot + 1) * rows]
        for step in range(steps):
            for g in range(group):
                at = step * group + g
                to = step * slots + slot
                att_ref[to : to + 1, g * head : (g + 1) * head] = done[at : at + 1]
    attended = att_ref[...].astype(jnp.bfloat16)

    def multiply(c, source, start):
        def tile(k, carry):
            at = pl.multiple_of(k * TILE, TILE)
            weight = source[:, pl.ds(pl.multiple_of(start + at, TILE), TILE)]
            out_ref[c, :, pl.ds(at, TILE)] = jnp.dot(
                attended, weight, preferred_element_type=jnp.float32
            ).astype(jnp.bfloat16)
            return carry

        lax.fori_loop(0, part_cols // TILE, tile, 0, unroll=True)

    for c in range(ahead):
        multiply(c, held_ref, c * part_cols)

    def part(c, carry):
        copy(c).wait()
        multiply(c, w_ref, (c - ahead) * part_cols)
        return carry

    lax.fori_loop(ahead, parts, part, 0)


def params(mib):
    return pltpu.CompilerParams(vmem_limit_bytes=mib * 1024 * 1024)


def shards(queries, new_kv, kv_pool, out_weight, send_block, send_dest, block_table, cache_len):
    n_inst = lax.axis_size("inst")
    n_tp = lax.axis_size("tp")
    steps, slots, head_width = queries.shape
    pool_size, block_len, _, width = kv_pool.shape
    head = width // 2
    group = head_width // head
    rows = steps * group
    blocks = block_table.shape[1]
    entries = send_block.shape[0]
    columns = out_weight.shape[1]
    arrivals = n_inst * CAP
    scale = head ** (-0.5)
    f32, bf16, i32 = jnp.float32, jnp.bfloat16, jnp.int32
    shape = jax.ShapeDtypeStruct
    pool = kv_pool.reshape(pool_size, block_len, width)
    fresh = new_kv.reshape(steps, slots, width)

    packet = shape((n_inst, CAP * rows + INFO, head), bf16)
    ask, slot_query = pl.pallas_call(
        functools.partial(ask_kernel, pool_size, block_len),
        out_shape=(
            packet,
            shape((slots, rows + 2 * FRESH, head), bf16),
        ),
        in_specs=[HBM] * 6,
        out_specs=(VMEM, VMEM),
        scratch_shapes=[
            pltpu.SMEM((slots, blocks), i32),
            pltpu.SMEM((slots,), i32),
            pltpu.SMEM((entries,), i32),
            pltpu.SMEM((entries,), i32),
            pltpu.SMEM((arrivals + 1,), i32),
            pltpu.SMEM((arrivals + 1,), i32),
            pltpu.VMEM(queries.shape, bf16),
            pltpu.VMEM(fresh.shape, bf16),
            pltpu.VMEM((slots, rows + 2 * FRESH, head), f32),
            pltpu.SemaphoreType.DMA((6,)),
        ],
        compiler_params=params(64),
        name="ask",
    )(block_table, cache_len, send_block, send_dest, queries, fresh)
    asked = lax.all_to_all(ask, "inst", 0, 0, tiled=True)

    ahead = columns // n_tp
    own = shape((slots, rows, head), f32)
    stat = shape((slots, 8, head), f32)
    own_peak, own_sum, own_acc, sent, held, place, slot_of = pl.pallas_call(
        functools.partial(bring_kernel, scale, group, blocks, steps, n_inst),
        out_shape=(
            stat, stat, own,
            shape((entries, block_len, width), bf16),
            shape((head_width, ahead), bf16),
            shape((8, head), i32),
            shape((arrivals * rows // head, head), i32),
        ),
        in_specs=[VMEM, HBM, HBM],
        out_specs=(VMEM,) * 7,
        scratch_shapes=[
            pltpu.VMEM((slots, (blocks + 1) * block_len, width), bf16),
            pltpu.SemaphoreType.DMA((slots, blocks)),
            pltpu.SemaphoreType.DMA((entries,)),
            pltpu.SemaphoreType.DMA,
        ],
        compiler_params=params(50),
        cost_estimate=pl.CostEstimate(
            flops=4 * slots * rows * blocks * block_len * width,
            bytes_accessed=8 * slots * blocks * block_len * width,
            transcendentals=slots * rows * blocks * block_len,
        ),
        name="own",
    )(slot_query, pool, out_weight)

    part_cols = columns // n_tp
    answer = pl.pallas_call(
        functools.partial(answer_kernel, scale),
        out_shape=packet,
        in_specs=[VMEM, VMEM, VMEM],
        out_specs=VMEM,
        scratch_shapes=[
            pltpu.VMEM((arrivals, head), f32),
            pltpu.VMEM((arrivals, head), f32),
        ],
        compiler_params=params(16),
        name="answer",
    )(place, asked, sent)
    back = lax.all_to_all(answer, "inst", 0, 0, tiled=True)

    out_rows = steps * slots
    partial_out = pl.pallas_call(
        project_kernel,
        out_shape=shape((n_tp, out_rows, part_cols), bf16),
        in_specs=[VMEM] * 6 + [HBM],
        out_specs=VMEM,
        scratch_shapes=[
            pltpu.VMEM((out_rows, head_width), f32),
            pltpu.VMEM((head_width, columns - ahead), bf16),
            pltpu.SemaphoreType.DMA((n_tp,)),
        ],
        compiler_params=params(44),
        name="project",
    )(slot_of, back, own_peak, own_sum, own_acc, held, out_weight)
    shares = lax.all_to_all(partial_out, "tp", 0, 0, tiled=True)
    total = jnp.sum(shares.astype(f32), axis=0).astype(bf16)
    return total.reshape(steps, slots, columns // n_tp)


def solution(mesh):
    return jax.shard_map(
        shards,
        mesh=mesh,
        in_specs=(
            P(None, "inst", "tp"),
            P(None, "inst", "tp", None),
            P("inst", None, "tp", None),
            P("tp", None),
            P("inst"),
            P("inst"),
            P("inst", None),
            P("inst"),
        ),
        out_specs=P(None, "inst", "tp"),
        check_vma=False,
    )
```

```python
import functools

import jax
import jax.numpy as jnp
from jax import lax
from jax.experimental import pallas as pl
from jax.experimental.pallas import tpu as pltpu
from jax.sharding import PartitionSpec as P

CAP = 2
INFO = 8
MASKED = -1e30
TILE = 256
FRESH = 8
PLAN_ROW = 4
LENGTH_BASE = 64

VMEM = pl.BlockSpec(memory_space=pltpu.VMEM)
HBM = pl.BlockSpec(memory_space=pltpu.HBM)

nt_dims = (((1,), (1,)), ((), ()))


def split_dot(weights, values):
    rows = weights.shape[0]
    high = weights.astype(jnp.bfloat16)
    low = (weights - high.astype(jnp.float32)).astype(jnp.bfloat16)
    both = jnp.dot(
        jnp.concatenate([high, low], axis=0), values, preferred_element_type=jnp.float32
    )
    return both[:rows] + both[rows:]


def ask_kernel(
    pool_size, block_len, table_hbm, len_hbm, block_hbm, dest_hbm, q_hbm, new_hbm,
    out_ref, query_ref,
    table_ref, len_ref, block_ref, dest_ref, code_ref, live_ref, q_ref, new_ref, rows_ref, sems,
):
    slots, blocks = table_ref.shape
    steps = q_ref.shape[0]
    rows, head = query_ref.shape[1] - 2 * FRESH, query_ref.shape[2]
    group = rows // steps
    arrivals = out_ref.shape[0] * CAP
    copies = [
        pltpu.make_async_copy(source, target, sems.at[k])
        for k, (source, target) in enumerate(
            (
                (q_hbm, q_ref),
                (new_hbm, new_ref),
                (table_hbm, table_ref),
                (len_hbm, len_ref),
                (block_hbm, block_ref),
                (dest_hbm, dest_ref),
            )
        )
    ]
    for copy in copies:
        copy.start()
    rows_ref[:, rows:, :] = jnp.zeros((slots, 2 * FRESH, head), jnp.float32)
    for a in range(arrivals):
        code_ref[a] = 0
        live_ref[a] = 0
    for copy in copies:
        copy.wait()
    for step in range(steps):
        query = q_ref[step].astype(jnp.float32)
        for slot in range(slots):
            for g in range(group):
                at = step * group + g
                rows_ref[slot, at : at + 1, :] = query[slot : slot + 1, g * head : (g + 1) * head]
        fresh = new_ref[step].astype(jnp.float32)
        for slot in range(slots):
            for k in range(2):
                at = rows + k * FRESH + step
                rows_ref[slot, at : at + 1, :] = fresh[slot : slot + 1, k * head : (k + 1) * head]
    plan = []
    for slot in range(slots):
        length = len_ref[slot]
        for b in range(blocks):
            block_id = table_ref[slot, b]
            arrival = jnp.where(block_id >= pool_size, block_id - pool_size, arrivals)
            code_ref[arrival] = slot
            live_ref[arrival] = jnp.clip(length - b * block_len, 0, block_len)
            plan.append(block_id)
    plan += [len_ref[slot] // LENGTH_BASE for slot in range(slots)]
    plan += [len_ref[slot] % LENGTH_BASE for slot in range(slots)]
    plan += [block_ref[e] for e in range(block_ref.shape[0])]
    plan += [dest_ref[e] for e in range(dest_ref.shape[0])]
    lane = lax.broadcasted_iota(jnp.int32, (1, head), 1)
    line = jnp.zeros((1, head), jnp.int32)
    for k, number in enumerate(plan):
        line = jnp.where(lane == k, number, line)
    rows_ref[0, rows + PLAN_ROW : rows + PLAN_ROW + 1, :] = line.astype(jnp.float32)
    for slot in range(slots):
        query_ref[slot] = rows_ref[slot].astype(jnp.bfloat16)
    row = lax.broadcasted_iota(jnp.int32, (INFO, head), 0)
    for a in range(arrivals):
        source, rank = a // CAP, a % CAP
        out_ref[source, rank * rows : (rank + 1) * rows, :] = query_ref[code_ref[a], :rows, :]
    for source in range(arrivals // CAP):
        live = jnp.where(row < INFO // 2, live_ref[source * CAP], live_ref[source * CAP + 1])
        out_ref[source, CAP * rows :, :] = live.astype(jnp.float32).astype(jnp.bfloat16)


class Plan:
    def __init__(self, q_ref, blocks, entries):
        slots, rows = q_ref.shape[0], q_ref.shape[1] - 2 * FRESH
        row = q_ref[0, rows:, :].astype(jnp.float32)[PLAN_ROW : PLAN_ROW + 1].astype(jnp.int32)
        numbers = [row[0, k] for k in range(slots * (blocks + 2) + 2 * entries)]
        at = slots * blocks
        self.table = [numbers[slot * blocks : (slot + 1) * blocks] for slot in range(slots)]
        self.length = [
            numbers[at + slot] * LENGTH_BASE + numbers[at + slots + slot] for slot in range(slots)
        ]
        at += 2 * slots
        self.block, self.dest = numbers[at : at + entries], numbers[at + entries :]


def own_kernel(
    scale, head_group, blocks, first,
    steps, plan, q_ref, pool_ref,
    peak_ref, sum_ref, acc_ref, kv_ref, sems, bring,
):
    pool_size, block_len, _ = pool_ref.shape
    slots, rows, head = q_ref.shape[0], q_ref.shape[1] - 2 * FRESH, q_ref.shape[2]
    span = blocks * block_len
    mine = range(first, first + peak_ref.shape[0])

    def own_copy(slot, b):
        block_id = jnp.clip(plan.table[slot][b], 0, pool_size - 1)
        return pltpu.make_async_copy(
            pool_ref.at[block_id],
            kv_ref.at[slot - first, pl.ds(b * block_len, block_len), :],
            sems.at[slot - first, b],
        )

    def live_tokens(slot, b):
        live = jnp.clip(plan.length[slot] - b * block_len, 0, block_len)
        return jnp.where(plan.table[slot][b] < pool_size, live, 0)

    lives = {(slot, b): live_tokens(slot, b) for slot in mine for b in range(blocks)}
    kv_ref[:, :, head:] = jnp.zeros((kv_ref.shape[0], kv_ref.shape[1], head), kv_ref.dtype)
    for slot in mine:
        for b in range(blocks):
            pl.when(lives[slot, b] > 0)(own_copy(slot, b).start)
    brought = bring()
    lane = lax.broadcasted_iota(jnp.int32, (rows, block_len), 1)
    step = lax.broadcasted_iota(jnp.int32, (rows, block_len), 0) // head_group
    for slot in mine:
        fresh = q_ref[slot, rows:, :].astype(jnp.float32)
        rest = jnp.zeros((block_len - FRESH, head), jnp.float32)
        for k in range(2):
            part = jnp.concatenate([fresh[k * FRESH : (k + 1) * FRESH], rest], axis=0)
            kv_ref[slot - first, span:, k * head : (k + 1) * head] = part.astype(jnp.bfloat16)
    def score(slot):
        for b in range(blocks):
            pl.when(lives[slot, b] > 0)(own_copy(slot, b).wait)
        return lax.dot_general(
            q_ref[slot, :rows, :], kv_ref[slot - first, :, :head], nt_dims, preferred_element_type=jnp.float32
        ) * scale

    def attend(slot, scores):
        parts_s = []
        for b in range(blocks):
            part = scores[:, b * block_len : (b + 1) * block_len]
            parts_s.append(jnp.where(lane < lives[slot, b], part, MASKED))
        parts_s.append(jnp.where((lane <= step) & (lane < steps), scores[:, span:], MASKED))
        peak = jnp.max(functools.reduce(jnp.maximum, parts_s), axis=1, keepdims=True)
        weights = [jnp.exp(part - peak) for part in parts_s]
        total = jnp.sum(functools.reduce(jnp.add, weights), axis=1, keepdims=True)
        acc_ref[slot - first] = split_dot(jnp.concatenate(weights, axis=1), kv_ref[slot - first, :, head:])
        same = lane % rows == lax.broadcasted_iota(jnp.int32, (rows, block_len), 0)
        for ref, column in ((peak_ref, peak), (sum_ref, total)):
            across = jnp.sum(jnp.where(same, column, 0.0), axis=0, keepdims=True)
            ref[slot - first] = jnp.broadcast_to(across, ref.shape[1:])

    scores = score(first)
    for slot in mine:
        later = score(slot + 1) if slot + 1 in mine else None
        attend(slot, scores)
        scores = later
    for copy in brought:
        copy.wait()


def bring_kernel(
    scale, head_group, blocks, steps, n_inst,
    q_ref, pool_ref, weight_ref,
    peak_ref, sum_ref, acc_ref, sent_ref, held_ref, place_ref, slot_ref,
    kv_ref, sems, sent_sems, held_sem,
):
    pool_size = pool_ref.shape[0]
    slots, rows, head = q_ref.shape[0], q_ref.shape[1] - 2 * FRESH, q_ref.shape[2]
    entries = sent_ref.shape[0]
    plan = Plan(q_ref, blocks, entries)

    def bring():
        copies = []
        for e in range(entries):
            block_id = jnp.clip(plan.block[e], 0, pool_size - 1)
            copies.append(
                pltpu.make_async_copy(pool_ref.at[block_id], sent_ref.at[e], sent_sems.at[e])
            )
            copies[e].start()
        held_copy = pltpu.make_async_copy(
            weight_ref.at[:, pl.ds(0, held_ref.shape[1])], held_ref, held_sem
        )
        held_copy.start()
        copies.append(held_copy)
        lane = lax.broadcasted_iota(jnp.int32, place_ref.shape, 1)
        places = jnp.zeros(place_ref.shape, jnp.int32)
        for e in range(entries):
            dest = jnp.clip(plan.dest[e], 0, n_inst - 1)
            rank = sum((plan.dest[f] == plan.dest[e]).astype(jnp.int32) for f in range(e))
            place = jnp.minimum(rank, CAP - 1) * n_inst + dest
            places = jnp.where(lane == e, place, places)
        place_ref[...] = places
        line = lax.broadcasted_iota(jnp.int32, slot_ref.shape, 0)
        arrival = line * (head // rows) + lax.broadcasted_iota(jnp.int32, slot_ref.shape, 1) // rows
        slot_of = jnp.full(slot_ref.shape, -1, jnp.int32)
        for slot in range(slots):
            for b in range(blocks):
                slot_of = jnp.where(arrival == plan.table[slot][b] - pool_size, slot, slot_of)
        slot_ref[...] = slot_of
        return copies

    own_kernel(
        scale, head_group, blocks, 0, steps, plan, q_ref, pool_ref,
        peak_ref, sum_ref, acc_ref, kv_ref, sems, bring,
    )


def three_terms(values):
    high = values.astype(jnp.bfloat16).astype(jnp.float32)
    rest = values - high
    middle = rest.astype(jnp.bfloat16).astype(jnp.float32)
    return high, middle, rest - middle


def answer_kernel(
    scale, place_ref, asked_ref, sent_ref, out_ref, peak_ref, sum_ref
):
    entries, block_len, width = sent_ref.shape
    head = width // 2
    n_inst = out_ref.shape[0]
    rows = (out_ref.shape[1] - INFO) // CAP
    out_ref[...] = jnp.zeros_like(out_ref)
    peak_ref[...] = jnp.zeros_like(peak_ref)
    sum_ref[...] = jnp.zeros_like(sum_ref)
    lane = lax.broadcasted_iota(jnp.int32, (rows, block_len), 1)
    row = lax.broadcasted_iota(jnp.int32, (rows, block_len), 0)
    key = lane.astype(jnp.float32)
    places, starts, masks, scores = [], [], [], []
    across = place_ref[...]
    for e in range(entries):
        place = across[0, e]
        dest = lax.rem(place, n_inst)
        rank = lax.div(place, n_inst)
        start = pl.multiple_of(rank * rows, rows)
        query = asked_ref[dest, pl.ds(start, rows), :]
        info = asked_ref[dest, CAP * rows :, :].astype(jnp.float32)
        live = jnp.where(rank == 0, info[0:1], info[INFO // 2 : INFO // 2 + 1])
        places.append((place, dest))
        starts.append(start)
        masks.append(key < live)
        scores.append(
            lax.dot_general(
                query, sent_ref[e, :, :head], nt_dims, preferred_element_type=jnp.float32
            )
        )
    peaks, totals, results = [], [], []
    for e in range(entries):
        masked = jnp.where(masks[e], scores[e] * scale, MASKED)
        peak = jnp.max(masked, axis=1, keepdims=True)
        weights = jnp.where(masks[e], jnp.exp(masked - peak), 0.0)
        total = jnp.sum(weights, axis=1, keepdims=True)
        values = split_dot(weights, sent_ref[e, :, head:])
        peaks.append(peak)
        totals.append(total)
        results.append((values / jnp.where(total > 0.0, total, 1.0)).astype(jnp.bfloat16))
    for e in range(entries):
        place, dest = places[e]
        out_ref[dest, pl.ds(starts[e], rows), :] = results[e]
        here = lane == row + starts[e]
        peak_ref[pl.ds(place, 1), :] = jnp.sum(
            jnp.where(here, peaks[e], 0.0), axis=0, keepdims=True
        )
        sum_ref[pl.ds(place, 1), :] = jnp.sum(
            jnp.where(here, totals[e], 0.0), axis=0, keepdims=True
        )
    row = lax.broadcasted_iota(jnp.int32, (INFO, block_len), 0)
    terms = three_terms(peak_ref[:n_inst] + peak_ref[n_inst:])
    terms += three_terms(sum_ref[:n_inst] + sum_ref[n_inst:])
    for i in range(n_inst):
        info = jnp.zeros((INFO, block_len), jnp.float32)
        for k, term in enumerate(terms):
            info = jnp.where(row == k, term[i : i + 1], info)
        out_ref[i, CAP * rows :, :] = info.astype(jnp.bfloat16)


def over_groups(combine, row, size):
    shift = row.shape[1] // 2
    while shift >= size:
        row = combine(row, pltpu.roll(row, shift, axis=1))
        shift //= 2
    return row


def project_kernel(
    slot_ref, back_ref, peak_ref, sum_ref, acc_ref,
    held_ref, weight_ref, out_ref, att_ref, w_ref, sems,
):
    slots, rows, head = acc_ref.shape
    n_inst = back_ref.shape[0]
    parts, out_rows, part_cols = out_ref.shape
    held = held_ref.shape[1]
    steps = out_rows // slots
    group = rows // steps
    ahead = held // part_cols

    def copy(c):
        return pltpu.make_async_copy(
            weight_ref.at[:, pl.ds(pl.multiple_of(c * part_cols, part_cols), part_cols)],
            w_ref.at[:, pl.ds(pl.multiple_of((c - ahead) * part_cols, part_cols), part_cols)],
            sems.at[c],
        )

    for c in range(ahead, parts):
        copy(c).start()
    across = head // rows
    slot_of = slot_ref[...]
    lines = slot_of.shape[0]
    apart = across // CAP
    peak_rows, sum_rows = [], []
    for s in range(n_inst):
        info = back_ref[s, CAP * rows :, :].astype(jnp.float32)
        peak_rows.append(info[0:1] + info[1:2] + info[2:3])
        sum_rows.append(info[3:4] + info[4:5] + info[5:6])

    def together(per_source):
        total = None
        for k in range(apart):
            part = jnp.concatenate(per_source[k::apart], axis=0)
            if k:
                part = pltpu.roll(part, k * CAP * rows, axis=1)
            total = part if total is None else total + part
        return total

    peaks, sums = together(peak_rows), together(sum_rows)
    best, best_of = [], jnp.zeros((lines, head), jnp.float32)
    for k in range(slots):
        top = jnp.max(jnp.where(slot_of == k, peaks, MASKED), axis=0, keepdims=True)
        best.append(jnp.maximum(over_groups(jnp.maximum, top, rows), peak_ref[k]))
        best_of = jnp.where(slot_of == k, best[k], best_of)
    gains = jnp.where(slot_of >= 0, sums * jnp.exp(peaks - best_of), 0.0)
    keeps, matrix = [], []
    same = lax.broadcasted_iota(jnp.int32, (rows, head), 1) % rows == lax.broadcasted_iota(
        jnp.int32, (rows, head), 0
    )
    first_group = lax.broadcasted_iota(jnp.int32, (rows, head), 1) < rows
    for k in range(slots):
        mine = jnp.where(slot_of == k, gains, 0.0)
        keep = jnp.exp(peak_ref[k] - best[k])
        total = over_groups(jnp.add, jnp.sum(mine, axis=0, keepdims=True), rows)
        inverse = 1.0 / (total + sum_ref[k] * keep)
        keep = (keep * inverse)[0:1]
        keeps.append(
            jnp.sum(jnp.where(same & first_group, keep, 0.0), axis=1, keepdims=True)
        )
        mine = mine * inverse
        matrix.append(
            jnp.concatenate(
                [jnp.where(same, mine[j : j + 1], 0.0) for j in range(lines)], axis=1
            )
        )
    values = back_ref[:, : CAP * rows, :].reshape(n_inst * CAP * rows, head)
    arrived = split_dot(jnp.concatenate(matrix, axis=0), values)
    for slot in range(slots):
        done = keeps[slot] * acc_ref[slot] + arrived[slot * rows : (slot + 1) * rows]
        for step in range(steps):
            for g in range(group):
                at = step * group + g
                to = step * slots + slot
                att_ref[to : to + 1, g * head : (g + 1) * head] = done[at : at + 1]
    attended = att_ref[...].astype(jnp.bfloat16)

    def multiply(c, source, start):
        def tile(k, carry):
            at = pl.multiple_of(k * TILE, TILE)
            weight = source[:, pl.ds(pl.multiple_of(start + at, TILE), TILE)]
            out_ref[c, :, pl.ds(at, TILE)] = jnp.dot(
                attended, weight, preferred_element_type=jnp.float32
            ).astype(jnp.bfloat16)
            return carry

        lax.fori_loop(0, part_cols // TILE, tile, 0, unroll=True)

    for c in range(ahead):
        multiply(c, held_ref, c * part_cols)

    def part(c, carry):
        copy(c).wait()
        multiply(c, w_ref, (c - ahead) * part_cols)
        return carry

    lax.fori_loop(ahead, parts, part, 0)


def params(mib):
    return pltpu.CompilerParams(vmem_limit_bytes=mib * 1024 * 1024)


def shards(queries, new_kv, kv_pool, out_weight, send_block, send_dest, block_table, cache_len):
    n_inst = lax.axis_size("inst")
    n_tp = lax.axis_size("tp")
    steps, slots, head_width = queries.shape
    pool_size, block_len, _, width = kv_pool.shape
    head = width // 2
    group = head_width // head
    rows = steps * group
    blocks = block_table.shape[1]
    entries = send_block.shape[0]
    columns = out_weight.shape[1]
    arrivals = n_inst * CAP
    scale = head ** (-0.5)
    f32, bf16, i32 = jnp.float32, jnp.bfloat16, jnp.int32
    shape = jax.ShapeDtypeStruct
    pool = kv_pool.reshape(pool_size, block_len, width)
    fresh = new_kv.reshape(steps, slots, width)

    packet = shape((n_inst, CAP * rows + INFO, head), bf16)
    ask, slot_query = pl.pallas_call(
        functools.partial(ask_kernel, pool_size, block_len),
        out_shape=(
            packet,
            shape((slots, rows + 2 * FRESH, head), bf16),
        ),
        in_specs=[HBM] * 6,
        out_specs=(VMEM, VMEM),
        scratch_shapes=[
            pltpu.SMEM((slots, blocks), i32),
            pltpu.SMEM((slots,), i32),
            pltpu.SMEM((entries,), i32),
            pltpu.SMEM((entries,), i32),
            pltpu.SMEM((arrivals + 1,), i32),
            pltpu.SMEM((arrivals + 1,), i32),
            pltpu.VMEM(queries.shape, bf16),
            pltpu.VMEM(fresh.shape, bf16),
            pltpu.VMEM((slots, rows + 2 * FRESH, head), f32),
            pltpu.SemaphoreType.DMA((6,)),
        ],
        compiler_params=params(64),
        name="ask",
    )(block_table, cache_len, send_block, send_dest, queries, fresh)
    asked = lax.all_to_all(ask, "inst", 0, 0, tiled=True)

    ahead = columns // n_tp
    own = shape((slots, rows, head), f32)
    stat = shape((slots, 8, head), f32)
    own_peak, own_sum, own_acc, sent, held, place, slot_of = pl.pallas_call(
        functools.partial(bring_kernel, scale, group, blocks, steps, n_inst),
        out_shape=(
            stat, stat, own,
            shape((entries, block_len, width), bf16),
            shape((head_width, ahead), bf16),
            shape((8, head), i32),
            shape((arrivals * rows // head, head), i32),
        ),
        in_specs=[VMEM, HBM, HBM],
        out_specs=(VMEM,) * 7,
        scratch_shapes=[
            pltpu.VMEM((slots, (blocks + 1) * block_len, width), bf16),
            pltpu.SemaphoreType.DMA((slots, blocks)),
            pltpu.SemaphoreType.DMA((entries,)),
            pltpu.SemaphoreType.DMA,
        ],
        compiler_params=params(50),
        cost_estimate=pl.CostEstimate(
            flops=4 * slots * rows * blocks * block_len * width,
            bytes_accessed=8 * slots * blocks * block_len * width,
            transcendentals=slots * rows * blocks * block_len,
        ),
        name="own",
    )(slot_query, pool, out_weight)

    part_cols = columns // n_tp
    answer = pl.pallas_call(
        functools.partial(answer_kernel, scale),
        out_shape=packet,
        in_specs=[VMEM, VMEM, VMEM],
        out_specs=VMEM,
        scratch_shapes=[
            pltpu.VMEM((arrivals, head), f32),
            pltpu.VMEM((arrivals, head), f32),
        ],
        compiler_params=params(16),
        name="answer",
    )(place, asked, sent)
    back = lax.all_to_all(answer, "inst", 0, 0, tiled=True)

    out_rows = steps * slots
    partial_out = pl.pallas_call(
        project_kernel,
        out_shape=shape((n_tp, out_rows, part_cols), bf16),
        in_specs=[VMEM] * 6 + [HBM],
        out_specs=VMEM,
        scratch_shapes=[
            pltpu.VMEM((out_rows, head_width), f32),
            pltpu.VMEM((head_width, columns - ahead), bf16),
            pltpu.SemaphoreType.DMA((n_tp,)),
        ],
        compiler_params=params(44),
        name="project",
    )(slot_of, back, own_peak, own_sum, own_acc, held, out_weight)
    shares = lax.all_to_all(partial_out, "tp", 0, 0, tiled=True)
    total = jnp.sum(shares.astype(f32), axis=0).astype(bf16)
    return total.reshape(steps, slots, columns // n_tp)


def solution(mesh):
    return jax.shard_map(
        shards,
        mesh=mesh,
        in_specs=(
            P(None, "inst", "tp"),
            P(None, "inst", "tp", None),
            P("inst", None, "tp", None),
            P("tp", None),
            P("inst"),
            P("inst"),
            P("inst", None),
            P("inst"),
        ),
        out_specs=P(None, "inst", "tp"),
        check_vma=False,
    )
```

```python
import functools

import jax
import jax.numpy as jnp
from jax import lax
from jax.experimental import pallas as pl
from jax.experimental.pallas import tpu as pltpu
from jax.sharding import PartitionSpec as P

CAP = 2
INFO = 8
MASKED = -1e30
TILE = 256
FRESH = 8
PLAN_ROW = 4
PACK = 4
LENGTH_BASE = 64

VMEM = pl.BlockSpec(memory_space=pltpu.VMEM)
HBM = pl.BlockSpec(memory_space=pltpu.HBM)

nt_dims = (((1,), (1,)), ((), ()))


def split_dot(weights, values):
    rows = weights.shape[0]
    high = weights.astype(jnp.bfloat16)
    low = (weights - high.astype(jnp.float32)).astype(jnp.bfloat16)
    both = jnp.dot(
        jnp.concatenate([high, low], axis=0), values, preferred_element_type=jnp.float32
    )
    return both[:rows] + both[rows:]


def ask_kernel(
    pool_size, block_len, table_hbm, len_hbm, block_hbm, dest_hbm, q_hbm, new_hbm,
    out_ref, query_ref,
    table_ref, len_ref, block_ref, dest_ref, code_ref, live_ref, q_ref, new_ref, rows_ref, sems,
):
    slots, blocks = table_ref.shape
    steps = q_ref.shape[0]
    rows, head = query_ref.shape[1] - 2 * FRESH, query_ref.shape[2]
    group = rows // steps
    arrivals = out_ref.shape[0] * CAP
    copies = [
        pltpu.make_async_copy(source, target, sems.at[k])
        for k, (source, target) in enumerate(
            (
                (q_hbm, q_ref),
                (new_hbm, new_ref),
                (table_hbm, table_ref),
                (len_hbm, len_ref),
                (block_hbm, block_ref),
                (dest_hbm, dest_ref),
            )
        )
    ]
    for copy in copies:
        copy.start()
    rows_ref[:, rows:, :] = jnp.zeros((slots, 2 * FRESH, head), jnp.float32)
    for a in range(arrivals):
        code_ref[a] = 0
        live_ref[a] = 0
    for copy in copies:
        copy.wait()
    for step in range(steps):
        query = q_ref[step].astype(jnp.float32)
        for slot in range(slots):
            for g in range(group):
                at = step * group + g
                rows_ref[slot, at : at + 1, :] = query[slot : slot + 1, g * head : (g + 1) * head]
        fresh = new_ref[step].astype(jnp.float32)
        for slot in range(slots):
            for k in range(2):
                at = rows + k * FRESH + step
                rows_ref[slot, at : at + 1, :] = fresh[slot : slot + 1, k * head : (k + 1) * head]
    plan = []
    for slot in range(slots):
        length = len_ref[slot]
        for b in range(blocks):
            block_id = table_ref[slot, b]
            arrival = jnp.where(block_id >= pool_size, block_id - pool_size, arrivals)
            code_ref[arrival] = slot
            live_ref[arrival] = jnp.clip(length - b * block_len, 0, block_len)
            plan.append(block_id)
    plan += [len_ref[slot] // LENGTH_BASE for slot in range(slots)]
    plan += [len_ref[slot] % LENGTH_BASE for slot in range(slots)]
    plan += [block_ref[e] for e in range(block_ref.shape[0])]
    plan += [dest_ref[e] for e in range(dest_ref.shape[0])]
    lane = lax.broadcasted_iota(jnp.int32, (1, head), 1)
    line = jnp.zeros((1, head), jnp.int32)
    for k, number in enumerate(plan):
        line = jnp.where(lane == k, number, line)
    rows_ref[0, rows + PLAN_ROW : rows + PLAN_ROW + 1, :] = line.astype(jnp.float32)
    for slot in range(slots):
        query_ref[slot] = rows_ref[slot].astype(jnp.bfloat16)
    row = lax.broadcasted_iota(jnp.int32, (INFO, head), 0)
    for a in range(arrivals):
        source, rank = a // CAP, a % CAP
        out_ref[source, rank * rows : (rank + 1) * rows, :] = query_ref[code_ref[a], :rows, :]
    for source in range(arrivals // CAP):
        live = jnp.where(row < INFO // 2, live_ref[source * CAP], live_ref[source * CAP + 1])
        out_ref[source, CAP * rows :, :] = live.astype(jnp.float32).astype(jnp.bfloat16)


class Plan:
    def __init__(self, q_ref, blocks, entries):
        slots, rows = q_ref.shape[0], q_ref.shape[1] - 2 * FRESH
        row = q_ref[0, rows:, :].astype(jnp.float32)[PLAN_ROW : PLAN_ROW + 1].astype(jnp.int32)
        numbers = [row[0, k] for k in range(slots * (blocks + 2) + 2 * entries)]
        at = slots * blocks
        self.table = [numbers[slot * blocks : (slot + 1) * blocks] for slot in range(slots)]
        self.length = [
            numbers[at + slot] * LENGTH_BASE + numbers[at + slots + slot] for slot in range(slots)
        ]
        at += 2 * slots
        self.block, self.dest = numbers[at : at + entries], numbers[at + entries :]


def own_kernel(
    scale, head_group, blocks, first,
    steps, plan, q_ref, pool_ref,
    peak_ref, sum_ref, acc_ref, kv_ref, sems, bring,
):
    pool_size, block_len, _ = pool_ref.shape
    slots, rows, head = q_ref.shape[0], q_ref.shape[1] - 2 * FRESH, q_ref.shape[2]
    span = blocks * block_len
    mine = range(first, first + peak_ref.shape[0])

    def own_copy(slot, b):
        block_id = jnp.clip(plan.table[slot][b], 0, pool_size - 1)
        return pltpu.make_async_copy(
            pool_ref.at[block_id],
            kv_ref.at[slot - first, pl.ds(b * block_len, block_len), :],
            sems.at[slot - first, b],
        )

    def live_tokens(slot, b):
        live = jnp.clip(plan.length[slot] - b * block_len, 0, block_len)
        return jnp.where(plan.table[slot][b] < pool_size, live, 0)

    lives = {(slot, b): live_tokens(slot, b) for slot in mine for b in range(blocks)}
    kv_ref[:, :, head:] = jnp.zeros((kv_ref.shape[0], kv_ref.shape[1], head), kv_ref.dtype)
    for slot in mine:
        for b in range(blocks):
            pl.when(lives[slot, b] > 0)(own_copy(slot, b).start)
    brought = bring()
    lane = lax.broadcasted_iota(jnp.int32, (rows, block_len), 1)
    step = lax.broadcasted_iota(jnp.int32, (rows, block_len), 0) // head_group
    for slot in mine:
        fresh = q_ref[slot, rows:, :].astype(jnp.float32)
        rest = jnp.zeros((block_len - FRESH, head), jnp.float32)
        for k in range(2):
            part = jnp.concatenate([fresh[k * FRESH : (k + 1) * FRESH], rest], axis=0)
            kv_ref[slot - first, span:, k * head : (k + 1) * head] = part.astype(jnp.bfloat16)
    def score(slot):
        for b in range(blocks):
            pl.when(lives[slot, b] > 0)(own_copy(slot, b).wait)
        return lax.dot_general(
            q_ref[slot, :rows, :], kv_ref[slot - first, :, :head], nt_dims, preferred_element_type=jnp.float32
        ) * scale

    def attend(slot, scores):
        parts_s = []
        for b in range(blocks):
            part = scores[:, b * block_len : (b + 1) * block_len]
            parts_s.append(jnp.where(lane < lives[slot, b], part, MASKED))
        parts_s.append(jnp.where((lane <= step) & (lane < steps), scores[:, span:], MASKED))
        peak = jnp.max(functools.reduce(jnp.maximum, parts_s), axis=1, keepdims=True)
        weights = [jnp.exp(part - peak) for part in parts_s]
        total = jnp.sum(functools.reduce(jnp.add, weights), axis=1, keepdims=True)
        acc_ref[slot - first] = split_dot(jnp.concatenate(weights, axis=1), kv_ref[slot - first, :, head:])
        same = lane % rows == lax.broadcasted_iota(jnp.int32, (rows, block_len), 0)
        for ref, column in ((peak_ref, peak), (sum_ref, total)):
            across = jnp.sum(jnp.where(same, column, 0.0), axis=0, keepdims=True)
            ref[slot - first] = jnp.broadcast_to(across, ref.shape[1:])

    scores = score(first)
    for slot in mine:
        later = score(slot + 1) if slot + 1 in mine else None
        attend(slot, scores)
        scores = later
    for copy in brought:
        copy.wait()


def bring_kernel(
    scale, head_group, blocks, steps, n_inst,
    q_ref, pool_ref, weight_ref,
    peak_ref, sum_ref, acc_ref, sent_ref, held_ref, place_ref, slot_ref,
    kv_ref, sems, sent_sems, held_sem,
):
    pool_size = pool_ref.shape[0]
    slots, rows, head = q_ref.shape[0], q_ref.shape[1] - 2 * FRESH, q_ref.shape[2]
    entries = sent_ref.shape[0]
    plan = Plan(q_ref, blocks, entries)

    def bring():
        copies = []
        for e in range(entries):
            block_id = jnp.clip(plan.block[e], 0, pool_size - 1)
            copies.append(
                pltpu.make_async_copy(pool_ref.at[block_id], sent_ref.at[e], sent_sems.at[e])
            )
            copies[e].start()
        held_copy = pltpu.make_async_copy(
            weight_ref.at[:, pl.ds(0, held_ref.shape[1])], held_ref, held_sem
        )
        held_copy.start()
        copies.append(held_copy)
        lane = lax.broadcasted_iota(jnp.int32, place_ref.shape, 1)
        places = [0] * (entries // PACK)
        for e in range(entries):
            dest = jnp.clip(plan.dest[e], 0, n_inst - 1)
            rank = sum((plan.dest[f] == plan.dest[e]).astype(jnp.int32) for f in range(e))
            place = jnp.minimum(rank, CAP - 1) * n_inst + dest
            places[e // PACK] += place << (8 * (e % PACK))
        packed = jnp.zeros(place_ref.shape, jnp.int32)
        for k, number in enumerate(places):
            packed = jnp.where(lane == k, number, packed)
        place_ref[...] = packed
        line = lax.broadcasted_iota(jnp.int32, slot_ref.shape, 0)
        arrival = line * (head // rows) + lax.broadcasted_iota(jnp.int32, slot_ref.shape, 1) // rows
        slot_of = jnp.full(slot_ref.shape, -1, jnp.int32)
        for slot in range(slots):
            for b in range(blocks):
                slot_of = jnp.where(arrival == plan.table[slot][b] - pool_size, slot, slot_of)
        slot_ref[...] = slot_of
        return copies

    own_kernel(
        scale, head_group, blocks, 0, steps, plan, q_ref, pool_ref,
        peak_ref, sum_ref, acc_ref, kv_ref, sems, bring,
    )


def three_terms(values):
    high = values.astype(jnp.bfloat16).astype(jnp.float32)
    rest = values - high
    middle = rest.astype(jnp.bfloat16).astype(jnp.float32)
    return high, middle, rest - middle


def answer_kernel(
    scale, place_ref, asked_ref, sent_ref, out_ref, peak_ref, sum_ref
):
    entries, block_len, width = sent_ref.shape
    head = width // 2
    n_inst = out_ref.shape[0]
    rows = (out_ref.shape[1] - INFO) // CAP
    out_ref[...] = jnp.zeros_like(out_ref)
    peak_ref[...] = jnp.zeros_like(peak_ref)
    sum_ref[...] = jnp.zeros_like(sum_ref)
    lane = lax.broadcasted_iota(jnp.int32, (rows, block_len), 1)
    row = lax.broadcasted_iota(jnp.int32, (rows, block_len), 0)
    key = lane.astype(jnp.float32)
    places, starts, masks, scores = [], [], [], []
    across = place_ref[...]
    packed = [across[0, k] for k in range(entries // PACK)]
    for e in range(entries):
        place = (packed[e // PACK] >> (8 * (e % PACK))) & 127
        dest = lax.rem(place, n_inst)
        rank = lax.div(place, n_inst)
        start = pl.multiple_of(rank * rows, rows)
        query = asked_ref[dest, pl.ds(start, rows), :]
        info = asked_ref[dest, CAP * rows :, :].astype(jnp.float32)
        live = jnp.where(rank == 0, info[0:1], info[INFO // 2 : INFO // 2 + 1])
        places.append((place, dest))
        starts.append(start)
        masks.append(key < live)
        scores.append(
            lax.dot_general(
                query, sent_ref[e, :, :head], nt_dims, preferred_element_type=jnp.float32
            )
        )
    peaks, totals, results = [], [], []
    for e in range(entries):
        masked = jnp.where(masks[e], scores[e] * scale, MASKED)
        peak = jnp.max(masked, axis=1, keepdims=True)
        weights = jnp.where(masks[e], jnp.exp(masked - peak), 0.0)
        total = jnp.sum(weights, axis=1, keepdims=True)
        values = split_dot(weights, sent_ref[e, :, head:])
        peaks.append(peak)
        totals.append(total)
        results.append((values / jnp.where(total > 0.0, total, 1.0)).astype(jnp.bfloat16))
    for e in range(entries):
        place, dest = places[e]
        out_ref[dest, pl.ds(starts[e], rows), :] = results[e]
        here = lane == row + starts[e]
        peak_ref[pl.ds(place, 1), :] = jnp.sum(
            jnp.where(here, peaks[e], 0.0), axis=0, keepdims=True
        )
        sum_ref[pl.ds(place, 1), :] = jnp.sum(
            jnp.where(here, totals[e], 0.0), axis=0, keepdims=True
        )
    row = lax.broadcasted_iota(jnp.int32, (INFO, block_len), 0)
    terms = three_terms(peak_ref[:n_inst] + peak_ref[n_inst:])
    terms += three_terms(sum_ref[:n_inst] + sum_ref[n_inst:])
    for i in range(n_inst):
        info = jnp.zeros((INFO, block_len), jnp.float32)
        for k, term in enumerate(terms):
            info = jnp.where(row == k, term[i : i + 1], info)
        out_ref[i, CAP * rows :, :] = info.astype(jnp.bfloat16)


def over_groups(combine, row, size):
    shift = row.shape[1] // 2
    while shift >= size:
        row = combine(row, pltpu.roll(row, shift, axis=1))
        shift //= 2
    return row


def project_kernel(
    slot_ref, back_ref, peak_ref, sum_ref, acc_ref,
    held_ref, weight_ref, out_ref, att_ref, w_ref, sems,
):
    slots, rows, head = acc_ref.shape
    n_inst = back_ref.shape[0]
    parts, out_rows, part_cols = out_ref.shape
    held = held_ref.shape[1]
    steps = out_rows // slots
    group = rows // steps
    ahead = held // part_cols

    def copy(c):
        return pltpu.make_async_copy(
            weight_ref.at[:, pl.ds(pl.multiple_of(c * part_cols, part_cols), part_cols)],
            w_ref.at[:, pl.ds(pl.multiple_of((c - ahead) * part_cols, part_cols), part_cols)],
            sems.at[c],
        )

    for c in range(ahead, parts):
        copy(c).start()
    across = head // rows
    slot_of = slot_ref[...]
    lines = slot_of.shape[0]
    apart = across // CAP
    peak_rows, sum_rows = [], []
    for s in range(n_inst):
        info = back_ref[s, CAP * rows :, :].astype(jnp.float32)
        peak_rows.append(info[0:1] + info[1:2] + info[2:3])
        sum_rows.append(info[3:4] + info[4:5] + info[5:6])

    def together(per_source):
        total = None
        for k in range(apart):
            part = jnp.concatenate(per_source[k::apart], axis=0)
            if k:
                part = pltpu.roll(part, k * CAP * rows, axis=1)
            total = part if total is None else total + part
        return total

    peaks, sums = together(peak_rows), together(sum_rows)
    best, best_of = [], jnp.zeros((lines, head), jnp.float32)
    for k in range(slots):
        top = jnp.max(jnp.where(slot_of == k, peaks, MASKED), axis=0, keepdims=True)
        best.append(jnp.maximum(over_groups(jnp.maximum, top, rows), peak_ref[k]))
        best_of = jnp.where(slot_of == k, best[k], best_of)
    gains = jnp.where(slot_of >= 0, sums * jnp.exp(peaks - best_of), 0.0)
    keeps, matrix = [], []
    same = lax.broadcasted_iota(jnp.int32, (rows, head), 1) % rows == lax.broadcasted_iota(
        jnp.int32, (rows, head), 0
    )
    first_group = lax.broadcasted_iota(jnp.int32, (rows, head), 1) < rows
    for k in range(slots):
        mine = jnp.where(slot_of == k, gains, 0.0)
        keep = jnp.exp(peak_ref[k] - best[k])
        total = over_groups(jnp.add, jnp.sum(mine, axis=0, keepdims=True), rows)
        inverse = 1.0 / (total + sum_ref[k] * keep)
        keep = (keep * inverse)[0:1]
        keeps.append(
            jnp.sum(jnp.where(same & first_group, keep, 0.0), axis=1, keepdims=True)
        )
        mine = mine * inverse
        matrix.append(
            jnp.concatenate(
                [jnp.where(same, mine[j : j + 1], 0.0) for j in range(lines)], axis=1
            )
        )
    values = back_ref[:, : CAP * rows, :].reshape(n_inst * CAP * rows, head)
    arrived = split_dot(jnp.concatenate(matrix, axis=0), values)
    for slot in range(slots):
        done = keeps[slot] * acc_ref[slot] + arrived[slot * rows : (slot + 1) * rows]
        for step in range(steps):
            for g in range(group):
                at = step * group + g
                to = step * slots + slot
                att_ref[to : to + 1, g * head : (g + 1) * head] = done[at : at + 1]
    attended = att_ref[...].astype(jnp.bfloat16)

    def multiply(c, source, start):
        def tile(k, carry):
            at = pl.multiple_of(k * TILE, TILE)
            weight = source[:, pl.ds(pl.multiple_of(start + at, TILE), TILE)]
            out_ref[c, :, pl.ds(at, TILE)] = jnp.dot(
                attended, weight, preferred_element_type=jnp.float32
            ).astype(jnp.bfloat16)
            return carry

        lax.fori_loop(0, part_cols // TILE, tile, 0, unroll=True)

    for c in range(ahead):
        multiply(c, held_ref, c * part_cols)

    def part(c, carry):
        copy(c).wait()
        multiply(c, w_ref, (c - ahead) * part_cols)
        return carry

    lax.fori_loop(ahead, parts, part, 0)


def params(mib):
    return pltpu.CompilerParams(vmem_limit_bytes=mib * 1024 * 1024)


def shards(queries, new_kv, kv_pool, out_weight, send_block, send_dest, block_table, cache_len):
    n_inst = lax.axis_size("inst")
    n_tp = lax.axis_size("tp")
    steps, slots, head_width = queries.shape
    pool_size, block_len, _, width = kv_pool.shape
    head = width // 2
    group = head_width // head
    rows = steps * group
    blocks = block_table.shape[1]
    entries = send_block.shape[0]
    columns = out_weight.shape[1]
    arrivals = n_inst * CAP
    scale = head ** (-0.5)
    f32, bf16, i32 = jnp.float32, jnp.bfloat16, jnp.int32
    shape = jax.ShapeDtypeStruct
    pool = kv_pool.reshape(pool_size, block_len, width)
    fresh = new_kv.reshape(steps, slots, width)

    packet = shape((n_inst, CAP * rows + INFO, head), bf16)
    ask, slot_query = pl.pallas_call(
        functools.partial(ask_kernel, pool_size, block_len),
        out_shape=(
            packet,
            shape((slots, rows + 2 * FRESH, head), bf16),
        ),
        in_specs=[HBM] * 6,
        out_specs=(VMEM, VMEM),
        scratch_shapes=[
            pltpu.SMEM((slots, blocks), i32),
            pltpu.SMEM((slots,), i32),
            pltpu.SMEM((entries,), i32),
            pltpu.SMEM((entries,), i32),
            pltpu.SMEM((arrivals + 1,), i32),
            pltpu.SMEM((arrivals + 1,), i32),
            pltpu.VMEM(queries.shape, bf16),
            pltpu.VMEM(fresh.shape, bf16),
            pltpu.VMEM((slots, rows + 2 * FRESH, head), f32),
            pltpu.SemaphoreType.DMA((6,)),
        ],
        compiler_params=params(64),
        name="ask",
    )(block_table, cache_len, send_block, send_dest, queries, fresh)
    asked = lax.all_to_all(ask, "inst", 0, 0, tiled=True)

    ahead = columns // n_tp
    own = shape((slots, rows, head), f32)
    stat = shape((slots, 8, head), f32)
    own_peak, own_sum, own_acc, sent, held, place, slot_of = pl.pallas_call(
        functools.partial(bring_kernel, scale, group, blocks, steps, n_inst),
        out_shape=(
            stat, stat, own,
            shape((entries, block_len, width), bf16),
            shape((head_width, ahead), bf16),
            shape((8, head), i32),
            shape((arrivals * rows // head, head), i32),
        ),
        in_specs=[VMEM, HBM, HBM],
        out_specs=(VMEM,) * 7,
        scratch_shapes=[
            pltpu.VMEM((slots, (blocks + 1) * block_len, width), bf16),
            pltpu.SemaphoreType.DMA((slots, blocks)),
            pltpu.SemaphoreType.DMA((entries,)),
            pltpu.SemaphoreType.DMA,
        ],
        compiler_params=params(50),
        cost_estimate=pl.CostEstimate(
            flops=4 * slots * rows * blocks * block_len * width,
            bytes_accessed=8 * slots * blocks * block_len * width,
            transcendentals=slots * rows * blocks * block_len,
        ),
        name="own",
    )(slot_query, pool, out_weight)

    part_cols = columns // n_tp
    answer = pl.pallas_call(
        functools.partial(answer_kernel, scale),
        out_shape=packet,
        in_specs=[VMEM, VMEM, VMEM],
        out_specs=VMEM,
        scratch_shapes=[
            pltpu.VMEM((arrivals, head), f32),
            pltpu.VMEM((arrivals, head), f32),
        ],
        compiler_params=params(16),
        name="answer",
    )(place, asked, sent)
    back = lax.all_to_all(answer, "inst", 0, 0, tiled=True)

    out_rows = steps * slots
    partial_out = pl.pallas_call(
        project_kernel,
        out_shape=shape((n_tp, out_rows, part_cols), bf16),
        in_specs=[VMEM] * 6 + [HBM],
        out_specs=VMEM,
        scratch_shapes=[
            pltpu.VMEM((out_rows, head_width), f32),
            pltpu.VMEM((head_width, columns - ahead), bf16),
            pltpu.SemaphoreType.DMA((n_tp,)),
        ],
        compiler_params=params(44),
        name="project",
    )(slot_of, back, own_peak, own_sum, own_acc, held, out_weight)
    shares = lax.all_to_all(partial_out, "tp", 0, 0, tiled=True)
    total = jnp.sum(shares.astype(f32), axis=0).astype(bf16)
    return total.reshape(steps, slots, columns // n_tp)


def solution(mesh):
    return jax.shard_map(
        shards,
        mesh=mesh,
        in_specs=(
            P(None, "inst", "tp"),
            P(None, "inst", "tp", None),
            P("inst", None, "tp", None),
            P("tp", None),
            P("inst"),
            P("inst"),
            P("inst", None),
            P("inst"),
        ),
        out_specs=P(None, "inst", "tp"),
        check_vma=False,
    )
```

```python
import functools

import jax
import jax.numpy as jnp
from jax import lax
from jax.experimental import pallas as pl
from jax.experimental.pallas import tpu as pltpu
from jax.sharding import PartitionSpec as P

CAP = 2
INFO = 8
MASKED = -1e30
TILE = 256
FRESH = 8
PLAN_ROW = 4
PACK = 4
CHUNKS = 2
LENGTH_BASE = 64

VMEM = pl.BlockSpec(memory_space=pltpu.VMEM)
HBM = pl.BlockSpec(memory_space=pltpu.HBM)

nt_dims = (((1,), (1,)), ((), ()))


def split_dot(weights, values):
    rows = weights.shape[0]
    high = weights.astype(jnp.bfloat16)
    low = (weights - high.astype(jnp.float32)).astype(jnp.bfloat16)
    both = jnp.dot(
        jnp.concatenate([high, low], axis=0), values, preferred_element_type=jnp.float32
    )
    return both[:rows] + both[rows:]


def ask_kernel(
    pool_size, block_len, table_hbm, len_hbm, block_hbm, dest_hbm, q_hbm, new_hbm,
    out_ref, query_ref,
    table_ref, len_ref, block_ref, dest_ref, code_ref, live_ref, q_ref, new_ref, rows_ref, sems,
):
    slots, blocks = table_ref.shape
    steps = q_ref.shape[0]
    rows, head = query_ref.shape[1] - 2 * FRESH, query_ref.shape[2]
    group = rows // steps
    arrivals = out_ref.shape[0] * CAP
    copies = [
        pltpu.make_async_copy(source, target, sems.at[k])
        for k, (source, target) in enumerate(
            (
                (q_hbm, q_ref),
                (new_hbm, new_ref),
                (table_hbm, table_ref),
                (len_hbm, len_ref),
                (block_hbm, block_ref),
                (dest_hbm, dest_ref),
            )
        )
    ]
    for copy in copies:
        copy.start()
    rows_ref[:, rows:, :] = jnp.zeros((slots, 2 * FRESH, head), jnp.float32)
    for a in range(arrivals):
        code_ref[a] = 0
        live_ref[a] = 0
    for copy in copies:
        copy.wait()
    for step in range(steps):
        query = q_ref[step].astype(jnp.float32)
        for slot in range(slots):
            for g in range(group):
                at = step * group + g
                rows_ref[slot, at : at + 1, :] = query[slot : slot + 1, g * head : (g + 1) * head]
        fresh = new_ref[step].astype(jnp.float32)
        for slot in range(slots):
            for k in range(2):
                at = rows + k * FRESH + step
                rows_ref[slot, at : at + 1, :] = fresh[slot : slot + 1, k * head : (k + 1) * head]
    plan = []
    for slot in range(slots):
        length = len_ref[slot]
        for b in range(blocks):
            block_id = table_ref[slot, b]
            arrival = jnp.where(block_id >= pool_size, block_id - pool_size, arrivals)
            code_ref[arrival] = slot
            live_ref[arrival] = jnp.clip(length - b * block_len, 0, block_len)
            plan.append(block_id)
    plan += [len_ref[slot] // LENGTH_BASE for slot in range(slots)]
    plan += [len_ref[slot] % LENGTH_BASE for slot in range(slots)]
    plan += [block_ref[e] for e in range(block_ref.shape[0])]
    plan += [dest_ref[e] for e in range(dest_ref.shape[0])]
    lane = lax.broadcasted_iota(jnp.int32, (1, head), 1)
    line = jnp.zeros((1, head), jnp.int32)
    for k, number in enumerate(plan):
        line = jnp.where(lane == k, number, line)
    rows_ref[0, rows + PLAN_ROW : rows + PLAN_ROW + 1, :] = line.astype(jnp.float32)
    for slot in range(slots):
        query_ref[slot] = rows_ref[slot].astype(jnp.bfloat16)
    row = lax.broadcasted_iota(jnp.int32, (INFO, head), 0)
    for a in range(arrivals):
        source, rank = a // CAP, a % CAP
        out_ref[source, rank * rows : (rank + 1) * rows, :] = query_ref[code_ref[a], :rows, :]
    for source in range(arrivals // CAP):
        live = jnp.where(row < INFO // 2, live_ref[source * CAP], live_ref[source * CAP + 1])
        out_ref[source, CAP * rows :, :] = live.astype(jnp.float32).astype(jnp.bfloat16)


class Plan:
    def __init__(self, q_ref, blocks, entries):
        slots, rows = q_ref.shape[0], q_ref.shape[1] - 2 * FRESH
        row = q_ref[0, rows:, :].astype(jnp.float32)[PLAN_ROW : PLAN_ROW + 1].astype(jnp.int32)
        numbers = [row[0, k] for k in range(slots * (blocks + 2) + 2 * entries)]
        at = slots * blocks
        self.table = [numbers[slot * blocks : (slot + 1) * blocks] for slot in range(slots)]
        self.length = [
            numbers[at + slot] * LENGTH_BASE + numbers[at + slots + slot] for slot in range(slots)
        ]
        at += 2 * slots
        self.block, self.dest = numbers[at : at + entries], numbers[at + entries :]


def own_kernel(
    scale, head_group, blocks, first,
    steps, plan, q_ref, pool_ref,
    peak_ref, sum_ref, acc_ref, kv_ref, sems, bring,
):
    pool_size, block_len, _ = pool_ref.shape
    slots, rows, head = q_ref.shape[0], q_ref.shape[1] - 2 * FRESH, q_ref.shape[2]
    span = blocks * block_len
    mine = range(first, first + peak_ref.shape[0])

    def own_copy(slot, b):
        block_id = jnp.clip(plan.table[slot][b], 0, pool_size - 1)
        return pltpu.make_async_copy(
            pool_ref.at[block_id],
            kv_ref.at[slot - first, pl.ds(b * block_len, block_len), :],
            sems.at[slot - first, b],
        )

    def live_tokens(slot, b):
        live = jnp.clip(plan.length[slot] - b * block_len, 0, block_len)
        return jnp.where(plan.table[slot][b] < pool_size, live, 0)

    lives = {(slot, b): live_tokens(slot, b) for slot in mine for b in range(blocks)}
    kv_ref[:, :, head:] = jnp.zeros((kv_ref.shape[0], kv_ref.shape[1], head), kv_ref.dtype)
    for slot in mine:
        for b in range(blocks):
            pl.when(lives[slot, b] > 0)(own_copy(slot, b).start)
    brought = bring()
    lane = lax.broadcasted_iota(jnp.int32, (rows, block_len), 1)
    step = lax.broadcasted_iota(jnp.int32, (rows, block_len), 0) // head_group
    for slot in mine:
        fresh = q_ref[slot, rows:, :].astype(jnp.float32)
        rest = jnp.zeros((block_len - FRESH, head), jnp.float32)
        for k in range(2):
            part = jnp.concatenate([fresh[k * FRESH : (k + 1) * FRESH], rest], axis=0)
            kv_ref[slot - first, span:, k * head : (k + 1) * head] = part.astype(jnp.bfloat16)
    def score(slot):
        for b in range(blocks):
            pl.when(lives[slot, b] > 0)(own_copy(slot, b).wait)
        return lax.dot_general(
            q_ref[slot, :rows, :], kv_ref[slot - first, :, :head], nt_dims, preferred_element_type=jnp.float32
        ) * scale

    def attend(slot, scores):
        parts_s = []
        for b in range(blocks):
            part = scores[:, b * block_len : (b + 1) * block_len]
            parts_s.append(jnp.where(lane < lives[slot, b], part, MASKED))
        parts_s.append(jnp.where((lane <= step) & (lane < steps), scores[:, span:], MASKED))
        peak = jnp.max(functools.reduce(jnp.maximum, parts_s), axis=1, keepdims=True)
        weights = [jnp.exp(part - peak) for part in parts_s]
        total = jnp.sum(functools.reduce(jnp.add, weights), axis=1, keepdims=True)
        acc_ref[slot - first] = split_dot(jnp.concatenate(weights, axis=1), kv_ref[slot - first, :, head:])
        same = lane % rows == lax.broadcasted_iota(jnp.int32, (rows, block_len), 0)
        for ref, column in ((peak_ref, peak), (sum_ref, total)):
            across = jnp.sum(jnp.where(same, column, 0.0), axis=0, keepdims=True)
            ref[slot - first] = jnp.broadcast_to(across, ref.shape[1:])

    scores = score(first)
    for slot in mine:
        later = score(slot + 1) if slot + 1 in mine else None
        attend(slot, scores)
        scores = later
    for copy in brought:
        copy.wait()


def bring_kernel(
    scale, head_group, blocks, steps, n_inst,
    q_ref, pool_ref, weight_ref,
    peak_ref, sum_ref, acc_ref, sent_ref, held_ref, place_ref, slot_ref,
    kv_ref, sems, sent_sems, held_sem,
):
    pool_size = pool_ref.shape[0]
    slots, rows, head = q_ref.shape[0], q_ref.shape[1] - 2 * FRESH, q_ref.shape[2]
    entries = sent_ref.shape[0]
    plan = Plan(q_ref, blocks, entries)

    def bring():
        copies = []
        for e in range(entries):
            block_id = jnp.clip(plan.block[e], 0, pool_size - 1)
            copies.append(
                pltpu.make_async_copy(pool_ref.at[block_id], sent_ref.at[e], sent_sems.at[e])
            )
            copies[e].start()
        held_copy = pltpu.make_async_copy(
            weight_ref.at[:, pl.ds(0, held_ref.shape[1])], held_ref, held_sem
        )
        held_copy.start()
        copies.append(held_copy)
        lane = lax.broadcasted_iota(jnp.int32, place_ref.shape, 1)
        places = [0] * (entries // PACK)
        for e in range(entries):
            dest = jnp.clip(plan.dest[e], 0, n_inst - 1)
            rank = sum((plan.dest[f] == plan.dest[e]).astype(jnp.int32) for f in range(e))
            place = jnp.minimum(rank, CAP - 1) * n_inst + dest
            places[e // PACK] += place << (8 * (e % PACK))
        packed = jnp.zeros(place_ref.shape, jnp.int32)
        for k, number in enumerate(places):
            packed = jnp.where(lane == k, number, packed)
        place_ref[...] = packed
        line = lax.broadcasted_iota(jnp.int32, slot_ref.shape, 0)
        arrival = line * (head // rows) + lax.broadcasted_iota(jnp.int32, slot_ref.shape, 1) // rows
        slot_of = jnp.full(slot_ref.shape, -1, jnp.int32)
        for slot in range(slots):
            for b in range(blocks):
                slot_of = jnp.where(arrival == plan.table[slot][b] - pool_size, slot, slot_of)
        slot_ref[...] = slot_of
        return copies

    own_kernel(
        scale, head_group, blocks, 0, steps, plan, q_ref, pool_ref,
        peak_ref, sum_ref, acc_ref, kv_ref, sems, bring,
    )


def three_terms(values):
    high = values.astype(jnp.bfloat16).astype(jnp.float32)
    rest = values - high
    middle = rest.astype(jnp.bfloat16).astype(jnp.float32)
    return high, middle, rest - middle


def answer_kernel(
    scale, place_ref, asked_ref, sent_ref, out_ref, peak_ref, sum_ref
):
    entries, block_len, width = sent_ref.shape
    head = width // 2
    n_inst = out_ref.shape[0]
    rows = (out_ref.shape[1] - INFO) // CAP
    out_ref[...] = jnp.zeros_like(out_ref)
    peak_ref[...] = jnp.zeros_like(peak_ref)
    sum_ref[...] = jnp.zeros_like(sum_ref)
    lane = lax.broadcasted_iota(jnp.int32, (rows, block_len), 1)
    row = lax.broadcasted_iota(jnp.int32, (rows, block_len), 0)
    key = lane.astype(jnp.float32)
    places, starts, masks, scores = [], [], [], []
    across = place_ref[...]
    packed = [across[0, k] for k in range(entries // PACK)]
    for e in range(entries):
        place = (packed[e // PACK] >> (8 * (e % PACK))) & 127
        dest = lax.rem(place, n_inst)
        rank = lax.div(place, n_inst)
        start = pl.multiple_of(rank * rows, rows)
        query = asked_ref[dest, pl.ds(start, rows), :]
        info = asked_ref[dest, CAP * rows :, :].astype(jnp.float32)
        live = jnp.where(rank == 0, info[0:1], info[INFO // 2 : INFO // 2 + 1])
        places.append((place, dest))
        starts.append(start)
        masks.append(key < live)
        scores.append(
            lax.dot_general(
                query, sent_ref[e, :, :head], nt_dims, preferred_element_type=jnp.float32
            )
        )
    peaks, totals, results = [], [], []
    for e in range(entries):
        masked = jnp.where(masks[e], scores[e] * scale, MASKED)
        peak = jnp.max(masked, axis=1, keepdims=True)
        weights = jnp.where(masks[e], jnp.exp(masked - peak), 0.0)
        total = jnp.sum(weights, axis=1, keepdims=True)
        values = split_dot(weights, sent_ref[e, :, head:])
        peaks.append(peak)
        totals.append(total)
        results.append((values / jnp.where(total > 0.0, total, 1.0)).astype(jnp.bfloat16))
    for e in range(entries):
        place, dest = places[e]
        out_ref[dest, pl.ds(starts[e], rows), :] = results[e]
        here = lane == row + starts[e]
        peak_ref[pl.ds(place, 1), :] = jnp.sum(
            jnp.where(here, peaks[e], 0.0), axis=0, keepdims=True
        )
        sum_ref[pl.ds(place, 1), :] = jnp.sum(
            jnp.where(here, totals[e], 0.0), axis=0, keepdims=True
        )
    row = lax.broadcasted_iota(jnp.int32, (INFO, block_len), 0)
    terms = three_terms(peak_ref[:n_inst] + peak_ref[n_inst:])
    terms += three_terms(sum_ref[:n_inst] + sum_ref[n_inst:])
    for i in range(n_inst):
        info = jnp.zeros((INFO, block_len), jnp.float32)
        for k, term in enumerate(terms):
            info = jnp.where(row == k, term[i : i + 1], info)
        out_ref[i, CAP * rows :, :] = info.astype(jnp.bfloat16)


def over_groups(combine, row, size):
    shift = row.shape[1] // 2
    while shift >= size:
        row = combine(row, pltpu.roll(row, shift, axis=1))
        shift //= 2
    return row


def project_kernel(
    slot_ref, back_ref, peak_ref, sum_ref, acc_ref,
    held_ref, weight_ref, out_ref, att_ref, w_ref, sems,
):
    slots, rows, head = acc_ref.shape
    n_inst = back_ref.shape[0]
    parts, out_rows, part_cols = out_ref.shape
    held = held_ref.shape[1]
    steps = out_rows // slots
    group = rows // steps
    chunk = part_cols // CHUNKS
    ahead = held // chunk

    def copy(c):
        return pltpu.make_async_copy(
            weight_ref.at[:, pl.ds(pl.multiple_of(c * chunk, chunk), chunk)],
            w_ref.at[:, pl.ds(pl.multiple_of((c - ahead) * chunk, chunk), chunk)],
            sems.at[c],
        )

    for c in range(ahead, parts * CHUNKS):
        copy(c).start()
    across = head // rows
    slot_of = slot_ref[...]
    lines = slot_of.shape[0]
    apart = across // CAP
    peak_rows, sum_rows = [], []
    for s in range(n_inst):
        info = back_ref[s, CAP * rows :, :].astype(jnp.float32)
        peak_rows.append(info[0:1] + info[1:2] + info[2:3])
        sum_rows.append(info[3:4] + info[4:5] + info[5:6])

    def together(per_source):
        total = None
        for k in range(apart):
            part = jnp.concatenate(per_source[k::apart], axis=0)
            if k:
                part = pltpu.roll(part, k * CAP * rows, axis=1)
            total = part if total is None else total + part
        return total

    peaks, sums = together(peak_rows), together(sum_rows)
    best, best_of = [], jnp.zeros((lines, head), jnp.float32)
    for k in range(slots):
        top = jnp.max(jnp.where(slot_of == k, peaks, MASKED), axis=0, keepdims=True)
        best.append(jnp.maximum(over_groups(jnp.maximum, top, rows), peak_ref[k]))
        best_of = jnp.where(slot_of == k, best[k], best_of)
    gains = jnp.where(slot_of >= 0, sums * jnp.exp(peaks - best_of), 0.0)
    keeps, matrix = [], []
    same = lax.broadcasted_iota(jnp.int32, (rows, head), 1) % rows == lax.broadcasted_iota(
        jnp.int32, (rows, head), 0
    )
    first_group = lax.broadcasted_iota(jnp.int32, (rows, head), 1) < rows
    for k in range(slots):
        mine = jnp.where(slot_of == k, gains, 0.0)
        keep = jnp.exp(peak_ref[k] - best[k])
        total = over_groups(jnp.add, jnp.sum(mine, axis=0, keepdims=True), rows)
        inverse = 1.0 / (total + sum_ref[k] * keep)
        keep = (keep * inverse)[0:1]
        keeps.append(
            jnp.sum(jnp.where(same & first_group, keep, 0.0), axis=1, keepdims=True)
        )
        mine = mine * inverse
        matrix.append(
            jnp.concatenate(
                [jnp.where(same, mine[j : j + 1], 0.0) for j in range(lines)], axis=1
            )
        )
    values = back_ref[:, : CAP * rows, :].reshape(n_inst * CAP * rows, head)
    arrived = split_dot(jnp.concatenate(matrix, axis=0), values)
    for slot in range(slots):
        done = keeps[slot] * acc_ref[slot] + arrived[slot * rows : (slot + 1) * rows]
        for step in range(steps):
            for g in range(group):
                at = step * group + g
                to = step * slots + slot
                att_ref[to : to + 1, g * head : (g + 1) * head] = done[at : at + 1]
    attended = att_ref[...].astype(jnp.bfloat16)

    def multiply(part, at, source, start):
        for low in range(0, chunk, TILE):
            weight = source[:, pl.ds(pl.multiple_of(start + low, TILE), TILE)]
            out_ref[part, :, pl.ds(pl.multiple_of(at + low, TILE), TILE)] = jnp.dot(
                attended, weight, preferred_element_type=jnp.float32
            ).astype(jnp.bfloat16)

    for c in range(ahead):
        multiply(c // CHUNKS, c % CHUNKS * chunk, held_ref, c * chunk)

    def part(p, carry):
        for k in range(CHUNKS):
            c = p * CHUNKS + k
            copy(c).wait()
            multiply(p, k * chunk, w_ref, (c - ahead) * chunk)
        return carry

    lax.fori_loop(held // part_cols, parts, part, 0)


def params(mib):
    return pltpu.CompilerParams(vmem_limit_bytes=mib * 1024 * 1024)


def shards(queries, new_kv, kv_pool, out_weight, send_block, send_dest, block_table, cache_len):
    n_inst = lax.axis_size("inst")
    n_tp = lax.axis_size("tp")
    steps, slots, head_width = queries.shape
    pool_size, block_len, _, width = kv_pool.shape
    head = width // 2
    group = head_width // head
    rows = steps * group
    blocks = block_table.shape[1]
    entries = send_block.shape[0]
    columns = out_weight.shape[1]
    arrivals = n_inst * CAP
    scale = head ** (-0.5)
    f32, bf16, i32 = jnp.float32, jnp.bfloat16, jnp.int32
    shape = jax.ShapeDtypeStruct
    pool = kv_pool.reshape(pool_size, block_len, width)
    fresh = new_kv.reshape(steps, slots, width)

    packet = shape((n_inst, CAP * rows + INFO, head), bf16)
    ask, slot_query = pl.pallas_call(
        functools.partial(ask_kernel, pool_size, block_len),
        out_shape=(
            packet,
            shape((slots, rows + 2 * FRESH, head), bf16),
        ),
        in_specs=[HBM] * 6,
        out_specs=(VMEM, VMEM),
        scratch_shapes=[
            pltpu.SMEM((slots, blocks), i32),
            pltpu.SMEM((slots,), i32),
            pltpu.SMEM((entries,), i32),
            pltpu.SMEM((entries,), i32),
            pltpu.SMEM((arrivals + 1,), i32),
            pltpu.SMEM((arrivals + 1,), i32),
            pltpu.VMEM(queries.shape, bf16),
            pltpu.VMEM(fresh.shape, bf16),
            pltpu.VMEM((slots, rows + 2 * FRESH, head), f32),
            pltpu.SemaphoreType.DMA((6,)),
        ],
        compiler_params=params(64),
        name="ask",
    )(block_table, cache_len, send_block, send_dest, queries, fresh)
    asked = lax.all_to_all(ask, "inst", 0, 0, tiled=True)

    ahead = columns // n_tp
    own = shape((slots, rows, head), f32)
    stat = shape((slots, 8, head), f32)
    own_peak, own_sum, own_acc, sent, held, place, slot_of = pl.pallas_call(
        functools.partial(bring_kernel, scale, group, blocks, steps, n_inst),
        out_shape=(
            stat, stat, own,
            shape((entries, block_len, width), bf16),
            shape((head_width, ahead), bf16),
            shape((8, head), i32),
            shape((arrivals * rows // head, head), i32),
        ),
        in_specs=[VMEM, HBM, HBM],
        out_specs=(VMEM,) * 7,
        scratch_shapes=[
            pltpu.VMEM((slots, (blocks + 1) * block_len, width), bf16),
            pltpu.SemaphoreType.DMA((slots, blocks)),
            pltpu.SemaphoreType.DMA((entries,)),
            pltpu.SemaphoreType.DMA,
        ],
        compiler_params=params(50),
        cost_estimate=pl.CostEstimate(
            flops=4 * slots * rows * blocks * block_len * width,
            bytes_accessed=8 * slots * blocks * block_len * width,
            transcendentals=slots * rows * blocks * block_len,
        ),
        name="own",
    )(slot_query, pool, out_weight)

    part_cols = columns // n_tp
    answer = pl.pallas_call(
        functools.partial(answer_kernel, scale),
        out_shape=packet,
        in_specs=[VMEM, VMEM, VMEM],
        out_specs=VMEM,
        scratch_shapes=[
            pltpu.VMEM((arrivals, head), f32),
            pltpu.VMEM((arrivals, head), f32),
        ],
        compiler_params=params(16),
        name="answer",
    )(place, asked, sent)
    back = lax.all_to_all(answer, "inst", 0, 0, tiled=True)

    out_rows = steps * slots
    partial_out = pl.pallas_call(
        project_kernel,
        out_shape=shape((n_tp, out_rows, part_cols), bf16),
        in_specs=[VMEM] * 6 + [HBM],
        out_specs=VMEM,
        scratch_shapes=[
            pltpu.VMEM((out_rows, head_width), f32),
            pltpu.VMEM((head_width, columns - ahead), bf16),
            pltpu.SemaphoreType.DMA((n_tp * CHUNKS,)),
        ],
        compiler_params=params(44),
        name="project",
    )(slot_of, back, own_peak, own_sum, own_acc, held, out_weight)
    shares = lax.all_to_all(partial_out, "tp", 0, 0, tiled=True)
    total = jnp.sum(shares.astype(f32), axis=0).astype(bf16)
    return total.reshape(steps, slots, columns // n_tp)


def solution(mesh):
    return jax.shard_map(
        shards,
        mesh=mesh,
        in_specs=(
            P(None, "inst", "tp"),
            P(None, "inst", "tp", None),
            P("inst", None, "tp", None),
            P("tp", None),
            P("inst"),
            P("inst"),
            P("inst", None),
            P("inst"),
        ),
        out_specs=P(None, "inst", "tp"),
        check_vma=False,
    )
```

```python
import functools

import jax
import jax.numpy as jnp
from jax import lax
from jax.experimental import pallas as pl
from jax.experimental.pallas import tpu as pltpu
from jax.sharding import PartitionSpec as P

CAP = 2
INFO = 8
MASKED = -1e30
TILE = 1024
FRESH = 8
PLAN_ROW = 4
PACK = 4
LENGTH_BASE = 64

VMEM = pl.BlockSpec(memory_space=pltpu.VMEM)
HBM = pl.BlockSpec(memory_space=pltpu.HBM)

nt_dims = (((1,), (1,)), ((), ()))


def split_dot(weights, values):
    rows = weights.shape[0]
    high = weights.astype(jnp.bfloat16)
    low = (weights - high.astype(jnp.float32)).astype(jnp.bfloat16)
    both = jnp.dot(
        jnp.concatenate([high, low], axis=0), values, preferred_element_type=jnp.float32
    )
    return both[:rows] + both[rows:]


def ask_kernel(
    pool_size, block_len, table_hbm, len_hbm, block_hbm, dest_hbm, q_hbm, new_hbm,
    out_ref, query_ref,
    table_ref, len_ref, block_ref, dest_ref, code_ref, live_ref, q_ref, new_ref, rows_ref, sems,
):
    slots, blocks = table_ref.shape
    steps = q_ref.shape[0]
    rows, head = query_ref.shape[1] - 2 * FRESH, query_ref.shape[2]
    group = rows // steps
    arrivals = out_ref.shape[0] * CAP
    copies = [
        pltpu.make_async_copy(source, target, sems.at[k])
        for k, (source, target) in enumerate(
            (
                (q_hbm, q_ref),
                (new_hbm, new_ref),
                (table_hbm, table_ref),
                (len_hbm, len_ref),
                (block_hbm, block_ref),
                (dest_hbm, dest_ref),
            )
        )
    ]
    for copy in copies:
        copy.start()
    rows_ref[:, rows:, :] = jnp.zeros((slots, 2 * FRESH, head), jnp.float32)
    for a in range(arrivals):
        code_ref[a] = 0
        live_ref[a] = 0
    for copy in copies:
        copy.wait()
    for step in range(steps):
        query = q_ref[step].astype(jnp.float32)
        for slot in range(slots):
            for g in range(group):
                at = step * group + g
                rows_ref[slot, at : at + 1, :] = query[slot : slot + 1, g * head : (g + 1) * head]
        fresh = new_ref[step].astype(jnp.float32)
        for slot in range(slots):
            for k in range(2):
                at = rows + k * FRESH + step
                rows_ref[slot, at : at + 1, :] = fresh[slot : slot + 1, k * head : (k + 1) * head]
    plan = []
    for slot in range(slots):
        length = len_ref[slot]
        for b in range(blocks):
            block_id = table_ref[slot, b]
            arrival = jnp.where(block_id >= pool_size, block_id - pool_size, arrivals)
            code_ref[arrival] = slot
            live_ref[arrival] = jnp.clip(length - b * block_len, 0, block_len)
            plan.append(block_id)
    plan += [len_ref[slot] // LENGTH_BASE for slot in range(slots)]
    plan += [len_ref[slot] % LENGTH_BASE for slot in range(slots)]
    plan += [block_ref[e] for e in range(block_ref.shape[0])]
    plan += [dest_ref[e] for e in range(dest_ref.shape[0])]
    lane = lax.broadcasted_iota(jnp.int32, (1, head), 1)
    line = jnp.zeros((1, head), jnp.int32)
    for k, number in enumerate(plan):
        line = jnp.where(lane == k, number, line)
    rows_ref[0, rows + PLAN_ROW : rows + PLAN_ROW + 1, :] = line.astype(jnp.float32)
    for slot in range(slots):
        query_ref[slot] = rows_ref[slot].astype(jnp.bfloat16)
    row = lax.broadcasted_iota(jnp.int32, (INFO, head), 0)
    for a in range(arrivals):
        source, rank = a // CAP, a % CAP
        out_ref[source, rank * rows : (rank + 1) * rows, :] = query_ref[code_ref[a], :rows, :]
    for source in range(arrivals // CAP):
        live = jnp.where(row < INFO // 2, live_ref[source * CAP], live_ref[source * CAP + 1])
        out_ref[source, CAP * rows :, :] = live.astype(jnp.float32).astype(jnp.bfloat16)


class Plan:
    def __init__(self, q_ref, blocks, entries):
        slots, rows = q_ref.shape[0], q_ref.shape[1] - 2 * FRESH
        row = q_ref[0, rows:, :].astype(jnp.float32)[PLAN_ROW : PLAN_ROW + 1].astype(jnp.int32)
        numbers = [row[0, k] for k in range(slots * (blocks + 2) + 2 * entries)]
        at = slots * blocks
        self.table = [numbers[slot * blocks : (slot + 1) * blocks] for slot in range(slots)]
        self.length = [
            numbers[at + slot] * LENGTH_BASE + numbers[at + slots + slot] for slot in range(slots)
        ]
        at += 2 * slots
        self.block, self.dest = numbers[at : at + entries], numbers[at + entries :]


def own_kernel(
    scale, head_group, blocks, first,
    steps, plan, q_ref, pool_ref,
    peak_ref, sum_ref, acc_ref, kv_ref, sems, bring,
):
    pool_size, block_len, _ = pool_ref.shape
    slots, rows, head = q_ref.shape[0], q_ref.shape[1] - 2 * FRESH, q_ref.shape[2]
    span = blocks * block_len
    mine = range(first, first + peak_ref.shape[0])

    def own_copy(slot, b):
        block_id = jnp.clip(plan.table[slot][b], 0, pool_size - 1)
        return pltpu.make_async_copy(
            pool_ref.at[block_id],
            kv_ref.at[slot - first, pl.ds(b * block_len, block_len), :],
            sems.at[slot - first, b],
        )

    def live_tokens(slot, b):
        live = jnp.clip(plan.length[slot] - b * block_len, 0, block_len)
        return jnp.where(plan.table[slot][b] < pool_size, live, 0)

    lives = {(slot, b): live_tokens(slot, b) for slot in mine for b in range(blocks)}
    kv_ref[:, :, head:] = jnp.zeros((kv_ref.shape[0], kv_ref.shape[1], head), kv_ref.dtype)
    for slot in mine:
        for b in range(blocks):
            pl.when(lives[slot, b] > 0)(own_copy(slot, b).start)
    brought = bring()
    lane = lax.broadcasted_iota(jnp.int32, (rows, block_len), 1)
    step = lax.broadcasted_iota(jnp.int32, (rows, block_len), 0) // head_group
    for slot in mine:
        fresh = q_ref[slot, rows:, :].astype(jnp.float32)
        rest = jnp.zeros((block_len - FRESH, head), jnp.float32)
        for k in range(2):
            part = jnp.concatenate([fresh[k * FRESH : (k + 1) * FRESH], rest], axis=0)
            kv_ref[slot - first, span:, k * head : (k + 1) * head] = part.astype(jnp.bfloat16)
    def score(slot):
        for b in range(blocks):
            pl.when(lives[slot, b] > 0)(own_copy(slot, b).wait)
        return lax.dot_general(
            q_ref[slot, :rows, :], kv_ref[slot - first, :, :head], nt_dims, preferred_element_type=jnp.float32
        ) * scale

    def attend(slot, scores):
        parts_s = []
        for b in range(blocks):
            part = scores[:, b * block_len : (b + 1) * block_len]
            parts_s.append(jnp.where(lane < lives[slot, b], part, MASKED))
        parts_s.append(jnp.where((lane <= step) & (lane < steps), scores[:, span:], MASKED))
        peak = jnp.max(functools.reduce(jnp.maximum, parts_s), axis=1, keepdims=True)
        weights = [jnp.exp(part - peak) for part in parts_s]
        total = jnp.sum(functools.reduce(jnp.add, weights), axis=1, keepdims=True)
        acc_ref[slot - first] = split_dot(jnp.concatenate(weights, axis=1), kv_ref[slot - first, :, head:])
        same = lane % rows == lax.broadcasted_iota(jnp.int32, (rows, block_len), 0)
        for ref, column in ((peak_ref, peak), (sum_ref, total)):
            across = jnp.sum(jnp.where(same, column, 0.0), axis=0, keepdims=True)
            ref[slot - first] = jnp.broadcast_to(across, ref.shape[1:])

    scores = score(first)
    for slot in mine:
        later = score(slot + 1) if slot + 1 in mine else None
        attend(slot, scores)
        scores = later
    for copy in brought:
        copy.wait()


def bring_kernel(
    scale, head_group, blocks, steps, n_inst,
    q_ref, pool_ref, weight_ref,
    peak_ref, sum_ref, acc_ref, sent_ref, held_ref, place_ref, slot_ref,
    kv_ref, sems, sent_sems, held_sem,
):
    pool_size = pool_ref.shape[0]
    slots, rows, head = q_ref.shape[0], q_ref.shape[1] - 2 * FRESH, q_ref.shape[2]
    entries = sent_ref.shape[0]
    plan = Plan(q_ref, blocks, entries)

    def bring():
        copies = []
        for e in range(entries):
            block_id = jnp.clip(plan.block[e], 0, pool_size - 1)
            copies.append(
                pltpu.make_async_copy(pool_ref.at[block_id], sent_ref.at[e], sent_sems.at[e])
            )
            copies[e].start()
        held_copy = pltpu.make_async_copy(
            weight_ref.at[:, pl.ds(0, held_ref.shape[1])], held_ref, held_sem
        )
        held_copy.start()
        copies.append(held_copy)
        lane = lax.broadcasted_iota(jnp.int32, place_ref.shape, 1)
        places = [0] * (entries // PACK)
        for e in range(entries):
            dest = jnp.clip(plan.dest[e], 0, n_inst - 1)
            rank = sum((plan.dest[f] == plan.dest[e]).astype(jnp.int32) for f in range(e))
            place = jnp.minimum(rank, CAP - 1) * n_inst + dest
            places[e // PACK] += place << (8 * (e % PACK))
        packed = jnp.zeros(place_ref.shape, jnp.int32)
        for k, number in enumerate(places):
            packed = jnp.where(lane == k, number, packed)
        place_ref[...] = packed
        line = lax.broadcasted_iota(jnp.int32, slot_ref.shape, 0)
        arrival = line * (head // rows) + lax.broadcasted_iota(jnp.int32, slot_ref.shape, 1) // rows
        slot_of = jnp.full(slot_ref.shape, -1, jnp.int32)
        for slot in range(slots):
            for b in range(blocks):
                slot_of = jnp.where(arrival == plan.table[slot][b] - pool_size, slot, slot_of)
        slot_ref[...] = slot_of
        return copies

    own_kernel(
        scale, head_group, blocks, 0, steps, plan, q_ref, pool_ref,
        peak_ref, sum_ref, acc_ref, kv_ref, sems, bring,
    )


def three_terms(values):
    high = values.astype(jnp.bfloat16).astype(jnp.float32)
    rest = values - high
    middle = rest.astype(jnp.bfloat16).astype(jnp.float32)
    return high, middle, rest - middle


def answer_kernel(
    scale, place_ref, asked_ref, sent_ref, out_ref, peak_ref, sum_ref
):
    entries, block_len, width = sent_ref.shape
    head = width // 2
    n_inst = out_ref.shape[0]
    rows = (out_ref.shape[1] - INFO) // CAP
    out_ref[...] = jnp.zeros_like(out_ref)
    peak_ref[...] = jnp.zeros_like(peak_ref)
    sum_ref[...] = jnp.zeros_like(sum_ref)
    lane = lax.broadcasted_iota(jnp.int32, (rows, block_len), 1)
    row = lax.broadcasted_iota(jnp.int32, (rows, block_len), 0)
    key = lane.astype(jnp.float32)
    places, starts, masks, scores = [], [], [], []
    across = place_ref[...]
    packed = [across[0, k] for k in range(entries // PACK)]
    for e in range(entries):
        place = (packed[e // PACK] >> (8 * (e % PACK))) & 127
        dest = lax.rem(place, n_inst)
        rank = lax.div(place, n_inst)
        start = pl.multiple_of(rank * rows, rows)
        query = asked_ref[dest, pl.ds(start, rows), :]
        info = asked_ref[dest, CAP * rows :, :].astype(jnp.float32)
        live = jnp.where(rank == 0, info[0:1], info[INFO // 2 : INFO // 2 + 1])
        places.append((place, dest))
        starts.append(start)
        masks.append(key < live)
        scores.append(
            lax.dot_general(
                query, sent_ref[e, :, :head], nt_dims, preferred_element_type=jnp.float32
            )
        )
    peaks, totals, results = [], [], []
    for e in range(entries):
        masked = jnp.where(masks[e], scores[e] * scale, MASKED)
        peak = jnp.max(masked, axis=1, keepdims=True)
        weights = jnp.where(masks[e], jnp.exp(masked - peak), 0.0)
        total = jnp.sum(weights, axis=1, keepdims=True)
        values = split_dot(weights, sent_ref[e, :, head:])
        peaks.append(peak)
        totals.append(total)
        results.append((values / jnp.where(total > 0.0, total, 1.0)).astype(jnp.bfloat16))
    for e in range(entries):
        place, dest = places[e]
        out_ref[dest, pl.ds(starts[e], rows), :] = results[e]
        here = lane == row + starts[e]
        peak_ref[pl.ds(place, 1), :] = jnp.sum(
            jnp.where(here, peaks[e], 0.0), axis=0, keepdims=True
        )
        sum_ref[pl.ds(place, 1), :] = jnp.sum(
            jnp.where(here, totals[e], 0.0), axis=0, keepdims=True
        )
    row = lax.broadcasted_iota(jnp.int32, (INFO, block_len), 0)
    terms = three_terms(peak_ref[:n_inst] + peak_ref[n_inst:])
    terms += three_terms(sum_ref[:n_inst] + sum_ref[n_inst:])
    for i in range(n_inst):
        info = jnp.zeros((INFO, block_len), jnp.float32)
        for k, term in enumerate(terms):
            info = jnp.where(row == k, term[i : i + 1], info)
        out_ref[i, CAP * rows :, :] = info.astype(jnp.bfloat16)


def over_groups(combine, row, size):
    shift = row.shape[1] // 2
    while shift >= size:
        row = combine(row, pltpu.roll(row, shift, axis=1))
        shift //= 2
    return row


def project_kernel(
    slot_ref, back_ref, peak_ref, sum_ref, acc_ref,
    held_ref, weight_ref, out_ref, att_ref, w_ref, sems,
):
    slots, rows, head = acc_ref.shape
    n_inst = back_ref.shape[0]
    parts, out_rows, part_cols = out_ref.shape
    held = held_ref.shape[1]
    steps = out_rows // slots
    group = rows // steps
    ahead = held // part_cols

    def copy(c):
        return pltpu.make_async_copy(
            weight_ref.at[:, pl.ds(pl.multiple_of(c * part_cols, part_cols), part_cols)],
            w_ref.at[:, pl.ds(pl.multiple_of((c - ahead) * part_cols, part_cols), part_cols)],
            sems.at[c],
        )

    for c in range(ahead, parts):
        copy(c).start()
    across = head // rows
    slot_of = slot_ref[...]
    lines = slot_of.shape[0]
    apart = across // CAP
    peak_rows, sum_rows = [], []
    for s in range(n_inst):
        info = back_ref[s, CAP * rows :, :].astype(jnp.float32)
        peak_rows.append(info[0:1] + info[1:2] + info[2:3])
        sum_rows.append(info[3:4] + info[4:5] + info[5:6])

    def together(per_source):
        total = None
        for k in range(apart):
            part = jnp.concatenate(per_source[k::apart], axis=0)
            if k:
                part = pltpu.roll(part, k * CAP * rows, axis=1)
            total = part if total is None else total + part
        return total

    peaks, sums = together(peak_rows), together(sum_rows)
    best, best_of = [], jnp.zeros((lines, head), jnp.float32)
    for k in range(slots):
        top = jnp.max(jnp.where(slot_of == k, peaks, MASKED), axis=0, keepdims=True)
        best.append(jnp.maximum(over_groups(jnp.maximum, top, rows), peak_ref[k]))
        best_of = jnp.where(slot_of == k, best[k], best_of)
    gains = jnp.where(slot_of >= 0, sums * jnp.exp(peaks - best_of), 0.0)
    keeps, matrix = [], []
    same = lax.broadcasted_iota(jnp.int32, (rows, head), 1) % rows == lax.broadcasted_iota(
        jnp.int32, (rows, head), 0
    )
    first_group = lax.broadcasted_iota(jnp.int32, (rows, head), 1) < rows
    for k in range(slots):
        mine = jnp.where(slot_of == k, gains, 0.0)
        keep = jnp.exp(peak_ref[k] - best[k])
        total = over_groups(jnp.add, jnp.sum(mine, axis=0, keepdims=True), rows)
        inverse = 1.0 / (total + sum_ref[k] * keep)
        keep = (keep * inverse)[0:1]
        keeps.append(
            jnp.sum(jnp.where(same & first_group, keep, 0.0), axis=1, keepdims=True)
        )
        mine = mine * inverse
        matrix.append(
            jnp.concatenate(
                [jnp.where(same, mine[j : j + 1], 0.0) for j in range(lines)], axis=1
            )
        )
    values = back_ref[:, : CAP * rows, :].reshape(n_inst * CAP * rows, head)
    arrived = split_dot(jnp.concatenate(matrix, axis=0), values)
    for slot in range(slots):
        done = keeps[slot] * acc_ref[slot] + arrived[slot * rows : (slot + 1) * rows]
        for step in range(steps):
            for g in range(group):
                at = step * group + g
                to = step * slots + slot
                att_ref[to : to + 1, g * head : (g + 1) * head] = done[at : at + 1]
    attended = att_ref[...].astype(jnp.bfloat16)

    def multiply(c, source, start):
        def tile(k, carry):
            at = pl.multiple_of(k * TILE, TILE)
            weight = source[:, pl.ds(pl.multiple_of(start + at, TILE), TILE)]
            out_ref[c, :, pl.ds(at, TILE)] = jnp.dot(
                attended, weight, preferred_element_type=jnp.float32
            ).astype(jnp.bfloat16)
            return carry

        lax.fori_loop(0, part_cols // TILE, tile, 0, unroll=True)

    for c in range(ahead):
        multiply(c, held_ref, c * part_cols)

    def part(c, carry):
        copy(c).wait()
        multiply(c, w_ref, (c - ahead) * part_cols)
        return carry

    lax.fori_loop(ahead, parts, part, 0)


def params(mib):
    return pltpu.CompilerParams(vmem_limit_bytes=mib * 1024 * 1024)


def shards(queries, new_kv, kv_pool, out_weight, send_block, send_dest, block_table, cache_len):
    n_inst = lax.axis_size("inst")
    n_tp = lax.axis_size("tp")
    steps, slots, head_width = queries.shape
    pool_size, block_len, _, width = kv_pool.shape
    head = width // 2
    group = head_width // head
    rows = steps * group
    blocks = block_table.shape[1]
    entries = send_block.shape[0]
    columns = out_weight.shape[1]
    arrivals = n_inst * CAP
    scale = head ** (-0.5)
    f32, bf16, i32 = jnp.float32, jnp.bfloat16, jnp.int32
    shape = jax.ShapeDtypeStruct
    pool = kv_pool.reshape(pool_size, block_len, width)
    fresh = new_kv.reshape(steps, slots, width)

    packet = shape((n_inst, CAP * rows + INFO, head), bf16)
    ask, slot_query = pl.pallas_call(
        functools.partial(ask_kernel, pool_size, block_len),
        out_shape=(
            packet,
            shape((slots, rows + 2 * FRESH, head), bf16),
        ),
        in_specs=[HBM] * 6,
        out_specs=(VMEM, VMEM),
        scratch_shapes=[
            pltpu.SMEM((slots, blocks), i32),
            pltpu.SMEM((slots,), i32),
            pltpu.SMEM((entries,), i32),
            pltpu.SMEM((entries,), i32),
            pltpu.SMEM((arrivals + 1,), i32),
            pltpu.SMEM((arrivals + 1,), i32),
            pltpu.VMEM(queries.shape, bf16),
            pltpu.VMEM(fresh.shape, bf16),
            pltpu.VMEM((slots, rows + 2 * FRESH, head), f32),
            pltpu.SemaphoreType.DMA((6,)),
        ],
        compiler_params=params(64),
        name="ask",
    )(block_table, cache_len, send_block, send_dest, queries, fresh)
    asked = lax.all_to_all(ask, "inst", 0, 0, tiled=True)

    ahead = columns // n_tp
    own = shape((slots, rows, head), f32)
    stat = shape((slots, 8, head), f32)
    own_peak, own_sum, own_acc, sent, held, place, slot_of = pl.pallas_call(
        functools.partial(bring_kernel, scale, group, blocks, steps, n_inst),
        out_shape=(
            stat, stat, own,
            shape((entries, block_len, width), bf16),
            shape((head_width, ahead), bf16),
            shape((8, head), i32),
            shape((arrivals * rows // head, head), i32),
        ),
        in_specs=[VMEM, HBM, HBM],
        out_specs=(VMEM,) * 7,
        scratch_shapes=[
            pltpu.VMEM((slots, (blocks + 1) * block_len, width), bf16),
            pltpu.SemaphoreType.DMA((slots, blocks)),
            pltpu.SemaphoreType.DMA((entries,)),
            pltpu.SemaphoreType.DMA,
        ],
        compiler_params=params(50),
        cost_estimate=pl.CostEstimate(
            flops=4 * slots * rows * blocks * block_len * width,
            bytes_accessed=8 * slots * blocks * block_len * width,
            transcendentals=slots * rows * blocks * block_len,
        ),
        name="own",
    )(slot_query, pool, out_weight)

    part_cols = columns // n_tp
    answer = pl.pallas_call(
        functools.partial(answer_kernel, scale),
        out_shape=packet,
        in_specs=[VMEM, VMEM, VMEM],
        out_specs=VMEM,
        scratch_shapes=[
            pltpu.VMEM((arrivals, head), f32),
            pltpu.VMEM((arrivals, head), f32),
        ],
        compiler_params=params(16),
        name="answer",
    )(place, asked, sent)
    back = lax.all_to_all(answer, "inst", 0, 0, tiled=True)

    out_rows = steps * slots
    partial_out = pl.pallas_call(
        project_kernel,
        out_shape=shape((n_tp, out_rows, part_cols), bf16),
        in_specs=[VMEM] * 6 + [HBM],
        out_specs=VMEM,
        scratch_shapes=[
            pltpu.VMEM((out_rows, head_width), f32),
            pltpu.VMEM((head_width, columns - ahead), bf16),
            pltpu.SemaphoreType.DMA((n_tp,)),
        ],
        compiler_params=params(44),
        name="project",
    )(slot_of, back, own_peak, own_sum, own_acc, held, out_weight)
    shares = lax.all_to_all(partial_out, "tp", 0, 0, tiled=True)
    total = jnp.sum(shares.astype(f32), axis=0).astype(bf16)
    return total.reshape(steps, slots, columns // n_tp)


def solution(mesh):
    return jax.shard_map(
        shards,
        mesh=mesh,
        in_specs=(
            P(None, "inst", "tp"),
            P(None, "inst", "tp", None),
            P("inst", None, "tp", None),
            P("tp", None),
            P("inst"),
            P("inst"),
            P("inst", None),
            P("inst"),
        ),
        out_specs=P(None, "inst", "tp"),
        check_vma=False,
    )
```
